32 devices in a mesh: img: 8 (over z, x), lvl: 4 (over y, core).
Axes of the slice: x: 2, y: 2, z: 4, core: 2. Of those that a mesh axis runs over, the one named last changes fastest.
Arguments:
- pyramid: bfloat16 [8, 4, 64, 64, 256], P('img', 'lvl'), may hold values from -6 to 6
- image_size: int32 [8, 2], P('img'), may hold values from 128 to 256
- region_boxes: int32 [2, 4, 2048], P(None, None, ('img', 'lvl')), may hold values from 0 to 4096, as said below
- routes: int32 [2, 2048], P(None, ('img', 'lvl')), may hold values from 0 to 3, as said below
- labels: int32 [2, 2048], P(None, ('img', 'lvl')), may hold values from 0 to 80
- targets: float32 [2, 4, 2048], P(None, None, ('img', 'lvl')), may hold values from -6 to 6
- feature_weight: bfloat16 [2, 12544, 1024], P(None, 'lvl'), may hold values from -0.078125 to 0.078125
- feature_bias: float32 [2, 1024], replicated, may hold values from -3 to 3
- hidden_weight: bfloat16 [2, 1024, 1024], replicated, may hold values from -0.25 to 0.25
- hidden_bias: float32 [2, 1024], replicated, may hold values from -3 to 3
- class_weight: bfloat16 [2, 1024, 81], replicated, may hold values from -0.5 to 0.5
- class_bias: float32 [2, 81], replicated, may hold values from -3 to 3
- delta_weight: bfloat16 [2, 1024, 320], replicated, may hold values from -0.5 to 0.5
- delta_bias: float32 [2, 320], replicated, may hold values from -3 to 3
Outputs:
- class_logits: float32 [2, 2048, 81], P(None, ('img', 'lvl'))
- region_deltas: float32 [2, 2048, 320], P(None, ('img', 'lvl'))
- pyramid_grad: bfloat16 [8, 4, 64, 64, 256], P('img', 'lvl')
- feature_weight_grad: float32 [2, 12544, 1024], P(None, 'lvl', 'img')
- feature_bias_grad: float32 [2, 1024], replicated
- hidden_weight_grad: float32 [2, 1024, 1024], P(None, ('img', 'lvl'))
- hidden_bias_grad: float32 [2, 1024], replicated
- class_weight_grad: float32 [2, 1024, 81], P(None, ('img', 'lvl'))
- class_bias_grad: float32 [2, 81], replicated
- delta_weight_grad: float32 [2, 1024, 320], P(None, ('img', 'lvl'))
- delta_bias_grad: float32 [2, 320], replicated
The draws below stay inside these ranges and needn't reach their ends.
Inputs may be any that keep to these rules, and one draw needn't show every extreme that they name: `routes`: in each section and on each device's 64 rows, no level is named by more than 32 rows; for every image and section one level, drawn from the seed, is named by exactly 32 rows of each of the image's 4 devices. `region_boxes`: top < bottom and left < right; each side is 1 to min(12, 64 / 2**l) cells of the region's level l, a cell being 16 * 4 * 2**l units.
All inputs are finite; a program needn't handle non-finite values.
Results may differ from the reference program's by a relative error of at most 0.023.
Values may be sent and summed in bfloat16 or wider, within the bound.
No kernel may reach another device: no remote copies, remote signals or barrier semaphores. Data moves between devices by JAX's collectives and lax.ppermute only.
A program may use at most 256 MiB of HBM per device.

```python
import jax
import jax.numpy as jnp
from jax import lax

CHANNELS = 256
HIDDEN_SIZE = 1024
CLASSES = 81
POOL = 7
SAMPLES = 2
LEVELS = 4
SECTIONS = 2
GRID = 64
SPAN = 12
WINDOW = 16
ROI_DEV = 64
CAP = 32
FEAT = 12544
DELTAS = 320
IMAGES = 8
ROIS = 2048


def level_draw(key, tag):
    key = jax.random.fold_in(key, tag)
    keys = jax.random.split(key, 7)
    blocks = ROIS // ROI_DEV
    full_level = jax.random.randint(keys[0], (SECTIONS, IMAGES), 0, LEVELS)
    full_rows = jnp.repeat(full_level, LEVELS, axis=1)
    others = (full_rows[:, :, None] + 1 + jax.random.randint(keys[1], (SECTIONS, blocks, ROI_DEV - CAP), 0, LEVELS - 1)) % LEVELS
    levels = jnp.concatenate([jnp.broadcast_to(full_rows[:, :, None], (SECTIONS, blocks, CAP)), others], axis=2)
    scores = jax.random.randint(keys[2], (SECTIONS, blocks, ROI_DEV), 0, 1 << 20) * ROI_DEV + jnp.arange(ROI_DEV, dtype=jnp.int32)
    order = jnp.argsort(scores, axis=2, stable=True)
    levels = jnp.take_along_axis(levels, order, axis=2).reshape(SECTIONS, ROIS).astype(jnp.int32)
    cell_units = 16 * jnp.left_shift(jnp.int32(4), levels)
    longest = jnp.minimum(SPAN, jnp.right_shift(jnp.int32(GRID), levels))
    side_y = jax.random.randint(keys[3], (SECTIONS, ROIS), cell_units, longest * cell_units + 1)
    side_x = jax.random.randint(keys[4], (SECTIONS, ROIS), cell_units, longest * cell_units + 1)
    canvas = 64 * GRID
    corner_y = jax.random.randint(keys[5], (SECTIONS, ROIS), 0, canvas - side_y + 1)
    corner_x = jax.random.randint(keys[6], (SECTIONS, ROIS), 0, canvas - side_x + 1)
    boxes = jnp.stack([corner_y, corner_x, corner_y + side_y, corner_x + side_x], axis=1)
    return (levels, boxes.astype(jnp.int32))


def draw_routes(key, part):
    return level_draw(key, 11)[0]


def draw_region_boxes(key, part):
    return level_draw(key, 11)[1]


def set_ends(result, own_key, low, high):
    longest = result.shape.index(max(result.shape))
    spots = []
    for shift in (0, 1):
        where = [jax.random.randint(jax.random.fold_in(own_key, axis), (), 0, length) for axis, length in enumerate(result.shape)]
        where[longest] = (where[longest] + shift) % result.shape[longest]
        spots.append(tuple(where))
    return result.at[spots[0]].set(low).at[spots[1]].set(high)


def block_scale(own_key, dims, cuts, smallest, largest):
    loudness = 1.0
    for dim, shards_of in cuts:
        draws = jax.random.uniform(jax.random.fold_in(jax.random.fold_in(own_key, 6), dim), (shards_of,), jnp.float32, smallest / len(cuts), largest / len(cuts))
        loudness = loudness * jnp.repeat(jnp.exp(draws), dims[dim] // shards_of).reshape((-1,) + (1,) * (len(dims) - 1 - dim))
    return loudness


def normal_values(key, extent, scale, reach, pieces=(), kind=jnp.bfloat16):
    entries = scale * jax.random.normal(key, extent, jnp.float32)
    if pieces:
        entries = entries * block_scale(key, extent, pieces, -0.22, 0.18)
    return jnp.clip(entries, -reach, reach).astype(kind)


def setup_inputs(seed: int = 0) -> dict:
    arg_keys = jax.random.split(jax.random.key(seed), 15)
    pyramid = normal_values(arg_keys[0], (IMAGES, LEVELS, GRID, GRID, CHANNELS), 1.0, 6.0, ((0, 8), (1, 4)))
    image_size = set_ends(jax.random.randint(arg_keys[1], (IMAGES, 2), 2 * GRID, 4 * GRID + 1), jax.random.fold_in(arg_keys[1], 1), 2 * GRID, 4 * GRID).astype(jnp.int32)
    region_boxes = draw_region_boxes(jax.random.fold_in(arg_keys[14], 71), 0)
    routes = draw_routes(jax.random.fold_in(arg_keys[14], 71), 0)
    labels = set_ends(jax.random.randint(arg_keys[4], (SECTIONS, ROIS), 0, CLASSES), jax.random.fold_in(arg_keys[4], 1), 0, CLASSES - 1).astype(jnp.int32)
    targets = normal_values(arg_keys[5], (SECTIONS, 4, ROIS), 1.0, 6.0, ((2, 32),), jnp.float32)
    feature_weight = normal_values(arg_keys[6], (SECTIONS, FEAT, HIDDEN_SIZE), (FEAT // 2) ** -0.5, 0.078125, ((1, 4),))
    feature_bias = normal_values(arg_keys[7], (SECTIONS, HIDDEN_SIZE), 0.5, 3.0, (), jnp.float32)
    hidden_weight = normal_values(arg_keys[8], (SECTIONS, HIDDEN_SIZE, HIDDEN_SIZE), (HIDDEN_SIZE // 2) ** -0.5, 0.25)
    hidden_bias = normal_values(arg_keys[9], (SECTIONS, HIDDEN_SIZE), 0.5, 3.0, (), jnp.float32)
    class_weight = normal_values(arg_keys[10], (SECTIONS, HIDDEN_SIZE, CLASSES), (HIDDEN_SIZE // 8) ** -0.5, 0.5)
    class_bias = normal_values(arg_keys[11], (SECTIONS, CLASSES), 0.5, 3.0, (), jnp.float32)
    delta_weight = normal_values(arg_keys[12], (SECTIONS, HIDDEN_SIZE, DELTAS), (HIDDEN_SIZE // 8) ** -0.5, 0.5)
    delta_bias = normal_values(arg_keys[13], (SECTIONS, DELTAS), 0.5, 3.0, (), jnp.float32)
    return {"pyramid": pyramid, "image_size": image_size, "region_boxes": region_boxes, "routes": routes, "labels": labels, "targets": targets, "feature_weight": feature_weight, "feature_bias": feature_bias, "hidden_weight": hidden_weight, "hidden_bias": hidden_bias, "class_weight": class_weight, "class_bias": class_bias, "delta_weight": delta_weight, "delta_bias": delta_bias}


@jax.custom_vjp
def low(v):
    return lax.optimization_barrier(v.astype(jnp.bfloat16)).astype(jnp.float32)

@jax.custom_vjp
def low_back(v):
    return v

def low_keep(v):
    return (low(v), None)

def low_pass(kept, grad):
    return (grad,)

def back_keep(v):
    return (v, None)

def back_low(kept, grad):
    return (low(grad),)
low.defvjp(low_keep, low_pass)
low_back.defvjp(back_keep, back_low)

def bin_weights(low_edge, high_edge, stride):
    odd_steps = 2 * jnp.arange(POOL * SAMPLES, dtype=jnp.int32) + 1
    span_units = 2 * POOL * SAMPLES
    numerator = span_units * low_edge[..., None] + odd_steps * (high_edge - low_edge)[..., None] - span_units * 8 * stride[..., None]
    denominator = span_units * 16 * stride[..., None]
    floor_cell = jnp.floor_divide(numerator, denominator)
    fraction = (numerator - floor_cell * denominator).astype(jnp.float32) / denominator.astype(jnp.float32)
    start_cell = floor_cell[..., 0]
    offset = floor_cell - start_cell[..., None]
    cell_index = jnp.arange(WINDOW, dtype=jnp.int32)
    lower_hit = (offset[..., None] == cell_index).astype(jnp.float32)
    upper_hit = (offset[..., None] + 1 == cell_index).astype(jnp.float32)
    weights = (1.0 - fraction)[..., None] * lower_hit + fraction[..., None] * upper_hit
    weights = weights.reshape(weights.shape[:-2] + (POOL, SAMPLES, WINDOW))
    return (start_cell, lax.optimization_barrier(jnp.sum(weights, axis=-2)) * (1.0 / SAMPLES))

def level_mask(image_height, image_width, stride):
    rows_valid = (image_height + stride - 1) // stride
    cols_valid = (image_width + stride - 1) // stride
    cell_index = jnp.arange(GRID, dtype=jnp.int32)
    return ((cell_index[:, None] < rows_valid) & (cell_index[None, :] < cols_valid)).astype(jnp.float32)

def regroup(array):
    moved = array.reshape(array.shape[:-1] + (IMAGES, LEVELS * ROI_DEV))
    return jnp.moveaxis(moved, -2, 0)

def reference(pyramid, image_size, region_boxes, routes, labels, targets, feature_weight, feature_bias, hidden_weight, hidden_bias, class_weight, class_bias, delta_weight, delta_bias):
    highest = lax.Precision.HIGHEST
    box_groups = regroup(region_boxes)
    route_groups = regroup(routes)
    label_groups = regroup(labels)
    target_groups = regroup(targets)
    row_total = LEVELS * ROI_DEV

    def forward(pyr, f_weight, f_bias, h_weight, h_bias, c_weight, c_bias, d_weight, d_bias):

        def image_step(inputs):
            level_maps, image_dims, boxes_here, routes_here, labels_here, targets_here = inputs
            image_height = image_dims[0]
            image_width = image_dims[1]
            strides = jnp.left_shift(jnp.int32(4), jnp.arange(LEVELS, dtype=jnp.int32))
            masks = jax.vmap(lambda stride: level_mask(image_height, image_width, stride))(strides)
            masked = level_maps * masks[..., None]
            padded = jnp.pad(masked, ((0, 0), (1, WINDOW), (1, WINDOW), (0, 0)))
            limits = jnp.stack([image_height, image_width, image_height, image_width]) * 16
            clipped = jnp.clip(boxes_here, 0, limits[None, :, None])
            stride_rows = jnp.left_shift(jnp.int32(4), routes_here)
            start_y, weight_y = bin_weights(clipped[:, 0], clipped[:, 2], stride_rows)
            start_x, weight_x = bin_weights(clipped[:, 1], clipped[:, 3], stride_rows)
            weight_y = low(weight_y)
            weight_x = low(weight_x)
            zero_index = jnp.zeros((), jnp.int32)

            def fetch(level_index, corner_y, corner_x):
                begin = (level_index.astype(jnp.int32), (corner_y + 1).astype(jnp.int32), (corner_x + 1).astype(jnp.int32), zero_index)
                return lax.dynamic_slice(padded, begin, (1, WINDOW, WINDOW, CHANNELS))[0]
            windows = jax.vmap(jax.vmap(fetch))(routes_here, start_y, start_x)
            partial_value = jnp.einsum('snbh,snhwc->snbwc', weight_y, windows, precision=highest)
            pooled = jnp.einsum('snbwc,snxw->sncbx', partial_value, weight_x, precision=highest)
            pooled = low(low_back(pooled.reshape(SECTIONS, row_total, FEAT)))
            pre_feature = low_back(jnp.einsum('snf,sfh->snh', pooled, f_weight, precision=highest) + f_bias[:, None, :])
            hidden_one = low(jax.nn.silu(pre_feature))
            pre_hidden = low_back(jnp.einsum('snh,shk->snk', hidden_one, h_weight, precision=highest) + h_bias[:, None, :])
            hidden_two = low(jax.nn.silu(pre_hidden))
            logits = low_back(jnp.einsum('snh,shc->snc', hidden_two, c_weight, precision=highest) + c_bias[:, None, :])
            deltas = low_back(jnp.einsum('snh,shd->snd', hidden_two, d_weight, precision=highest) + d_bias[:, None, :])
            label_hot = (labels_here[..., None] == jnp.arange(CLASSES, dtype=jnp.int32)).astype(jnp.float32)
            cross = jax.nn.logsumexp(logits, axis=-1) - lax.optimization_barrier(jnp.sum(logits * label_hot, axis=-1))
            fore_hot = label_hot[..., :CLASSES - 1]
            grouped = deltas.reshape(SECTIONS, row_total, CLASSES - 1, 4)
            chosen = lax.optimization_barrier(jnp.sum(grouped * fore_hot[..., None], axis=2))
            error = chosen - jnp.swapaxes(targets_here, 1, 2)
            magnitude = jnp.abs(error)
            huber = jnp.where(magnitude < 1.0, 0.5 * error * error, magnitude - 0.5)
            foreground = lax.optimization_barrier(jnp.sum(fore_hot, axis=-1))
            image_loss = jnp.sum(cross) + jnp.sum(huber * foreground[..., None])
            return (image_loss, logits, deltas)
        losses, logits_all, deltas_all = lax.map(jax.checkpoint(image_step), (pyr, image_size, box_groups, route_groups, label_groups, target_groups))
        logits_out = jnp.moveaxis(logits_all, 0, 1).reshape(SECTIONS, ROIS, CLASSES)
        deltas_out = jnp.moveaxis(deltas_all, 0, 1).reshape(SECTIONS, ROIS, DELTAS)
        return (jnp.sum(losses), (logits_out, deltas_out))
    params = (pyramid.astype(jnp.float32), feature_weight.astype(jnp.float32), feature_bias, hidden_weight.astype(jnp.float32), hidden_bias, class_weight.astype(jnp.float32), class_bias, delta_weight.astype(jnp.float32), delta_bias)
    total, pullback, outputs = jax.vjp(forward, *params, has_aux=True)
    grads = pullback(jnp.ones_like(total))
    return (outputs[0], outputs[1], grads[0].astype(jnp.bfloat16), grads[1], grads[2], grads[3], grads[4], grads[5], grads[6], grads[7], grads[8])
```

```python
import jax
import jax.numpy as jnp
from jax import lax
from jax.experimental import pallas as pl
from jax.experimental.pallas import tpu as pltpu
from jax.sharding import PartitionSpec as P

CHANNELS = 256
CLASSES = 81
POOL = 7
GRID = 64
DELTAS = 320

WIDTH = 80
ROWS = 140
BASES = (1, 66, 99, 116)
CELLS = ROWS * WIDTH
LANES = 128
WIDE = 3200
UNROLL = 32


def cost(microseconds):
    return pl.CostEstimate(flops=int(microseconds * SCALE * 1_150_000_000), bytes_accessed=0, transcendentals=0)


def params(mebibytes):
    return pltpu.CompilerParams(vmem_limit_bytes=mebibytes << 20)


SCALE = 1.0


def low_half(rows):
    return lax.broadcasted_iota(jnp.int32, (rows, LANES), 1) < 64


def tent(position, step, cell):
    first = jnp.maximum(1.0 - jnp.abs(position - cell), 0.0)
    second = jnp.maximum(1.0 - jnp.abs(position + step - cell), 0.0)
    return ((first + second) * 0.5).astype(jnp.bfloat16).astype(jnp.float32)


def place_rows(maps, upper, lower, upper_row, lower_row, cells):
    low = low_half(8)
    tiles = cells // 8
    zero = jnp.zeros((8, LANES), jnp.float32)
    values = [upper[8 * t : 8 * t + 8] for t in range(tiles)]
    turned = [pltpu.roll(v, 64, 1) for v in values]
    for t in range(-1, tiles):
        here, here_turned = (values[t], turned[t]) if t >= 0 else (zero, zero)
        after, after_turned = (values[t + 1], turned[t + 1]) if t + 1 < tiles else (zero, zero)
        maps[pl.ds(upper_row * WIDTH + 8 + 8 * t, 8), :] = jnp.where(low, here, after_turned)
        maps[pl.ds(lower_row * WIDTH + 8 + 8 * t, 8), :] = jnp.where(low, here_turned, after)


def fill_maps(maps, fine_ref, coarse_ref):
    def clear(t, carry):
        maps[pl.ds(pl.multiple_of(t * 160, 160), 160), :] = jnp.zeros((160, LANES), jnp.float32)
        return carry

    lax.fori_loop(0, CELLS // 160, clear, 0)

    def fine_row(y, carry):
        row = fine_ref[y].astype(jnp.float32)
        place_rows(maps, row, row, BASES[0] + y, BASES[0] + 32 + y, 64)
        return carry

    lax.fori_loop(0, 32, fine_row, 0)
    for level, cells in ((1, 32), (2, 16), (3, 8)):
        for y in range(cells // 2 if level == 1 else cells):
            row = coarse_ref[level, y].astype(jnp.float32)[:cells]
            if level == 1:
                place_rows(maps, row, row, BASES[1] + y, BASES[1] + 16 + y, 32)
            else:
                place_upper(maps, row, BASES[level] + y, cells)


def place_upper(maps, row, at, cells):
    low = low_half(8)
    tiles = cells // 8
    zero = jnp.zeros((8, LANES), jnp.float32)
    values = [row[8 * t : 8 * t + 8] for t in range(tiles)]
    for t in range(-1, tiles):
        here = values[t] if t >= 0 else zero
        after = pltpu.roll(values[t + 1], 64, 1) if t + 1 < tiles else zero
        maps[pl.ds(at * WIDTH + 8 + 8 * t, 8), :] = jnp.where(low, here, after)


def crop_kernel(table_ref, fine_ref, coarse_ref, out_ref, slab, maps, section):
    rb = out_ref.shape[0]
    base = pl.program_id(0) * rb

    @pl.when(pl.program_id(0) == 0)
    def _():
        fill_maps(maps, fine_ref, coarse_ref)

    low = low_half(8)
    lane = lax.broadcasted_iota(jnp.int32, (8, LANES), 1)
    bins = (2 * lax.broadcasted_iota(jnp.int32, (8, LANES), 0)).astype(jnp.float32)
    lane_y = (lane // 8).astype(jnp.float32)
    lane_x = (lane % 8).astype(jnp.float32)

    def one(r):
        start = table_ref[section, 0, base + r].astype(jnp.int32)
        y_at, y_step, x_at, x_step = [table_ref[section, 1 + j, base + r] for j in range(4)]
        window = jnp.concatenate([maps[pl.ds(start + WIDTH * j, 8), :] for j in range(16)], axis=0)
        wy = tent(y_at + y_step * bins, y_step, lane_y)
        x_position = x_at + x_step * bins
        wx = [tent(x_position, x_step, lane_x + 8.0 * h) for h in range(2)]
        rows = [jnp.broadcast_to(wy[b : b + 1], (8, LANES)) for b in range(POOL)]
        weight = jnp.concatenate([rows[b] * wx[h] for h in range(2) for b in range(POOL)], axis=0)
        both = jnp.dot(weight.astype(jnp.bfloat16), window.astype(jnp.bfloat16), preferred_element_type=jnp.float32)
        near = [both[8 * b : 8 * b + 8] for b in range(POOL)]
        far = [both[56 + 8 * b : 64 + 8 * b] for b in range(POOL)]
        zero = jnp.zeros((8, LANES), jnp.float32)
        for i in range(4):
            near_odd, far_odd = (near[2 * i + 1], far[2 * i + 1]) if i < 3 else (zero, zero)
            pair = jnp.where(low, near[2 * i], far_odd) + pltpu.roll(jnp.where(low, near_odd, far[2 * i]), 64, 1)
            slab[pl.ds(i * 8 * rb + r, 8, stride=rb), :] = pair

    def step(t, carry):
        for u in range(UNROLL):
            one(t * UNROLL + u)
        return carry

    lax.fori_loop(0, rb // UNROLL, step, 0)
    for i in range(3):
        for e in range(POOL):
            out_ref[:, pl.ds((7 * i + e) * LANES, LANES)] = slab[pl.ds((8 * i + e) * rb, rb), :].astype(jnp.bfloat16)
    for j in range(4):
        first = slab[pl.ds((24 + 2 * j) * rb, rb), :]
        if j < 3:
            second = slab[pl.ds((25 + 2 * j) * rb, rb), :]
            joined = jnp.where(low_half(rb), first, pltpu.roll(second, 64, 1))
            out_ref[:, pl.ds((21 + j) * LANES, LANES)] = joined.astype(jnp.bfloat16)
        else:
            out_ref[:, pl.ds(24 * LANES, LANES)] = jnp.where(low_half(rb), first, 0.0).astype(jnp.bfloat16)


def crop(table, section, fine, coarse, micros, block=64):
    count = table.shape[2]
    return pl.pallas_call(
        lambda *refs: crop_kernel(*refs, section),
        grid=(count // block,),
        in_specs=[
            pl.BlockSpec(memory_space=pltpu.SMEM),
            pl.BlockSpec(fine.shape, lambda g: (0, 0, 0)),
            pl.BlockSpec(coarse.shape, lambda g: (0, 0, 0, 0)),
        ],
        out_specs=pl.BlockSpec((block, WIDE), lambda g: (g, 0)),
        scratch_shapes=[pltpu.VMEM((32 * block, LANES), jnp.float32), pltpu.VMEM((CELLS, LANES), jnp.float32)],
        out_shape=jax.ShapeDtypeStruct((count, WIDE), jnp.bfloat16),
        cost_estimate=cost(micros),
        compiler_params=params(14),
    )(table, fine, coarse)


def spread_kernel(table_ref, first_ref, second_ref, fine_ref, coarse_ref, slab, sums):
    rb = first_ref.shape[0]
    steps = pl.num_programs(0) // 2
    section = pl.program_id(0) // steps
    base = (pl.program_id(0) % steps) * rb

    @pl.when(pl.program_id(0) == 0)
    def _():
        def clear(t, carry):
            sums[pl.ds(pl.multiple_of(t * 160, 160), 160), :] = jnp.zeros((160, LANES), jnp.float32)
            return carry

        lax.fori_loop(0, CELLS // 160, clear, 0)
        for i in range(4):
            slab[pl.ds((8 * i + 7) * rb, rb), :] = jnp.zeros((rb, LANES), jnp.float32)

    def lay_out(grads_ref):
        for i in range(3):
            for e in range(POOL):
                slab[pl.ds((8 * i + e) * rb, rb), :] = grads_ref[:, pl.ds((7 * i + e) * LANES, LANES)].astype(jnp.float32)
        for j in range(4):
            pair = grads_ref[:, pl.ds((21 + j) * LANES, LANES)].astype(jnp.float32)
            slab[pl.ds((24 + 2 * j) * rb, rb), :] = pair
            if j < 3:
                slab[pl.ds((25 + 2 * j) * rb, rb), :] = pltpu.roll(pair, 64, 1)

    @pl.when(section == 0)
    def _():
        lay_out(first_ref)

    @pl.when(section == 1)
    def _():
        lay_out(second_ref)

    low = low_half(8)
    lane = lax.broadcasted_iota(jnp.int32, (8, LANES), 1)
    row = lax.broadcasted_iota(jnp.int32, (8, LANES), 0).astype(jnp.float32)
    bins_y = (2 * ((lane // 8) % 8)).astype(jnp.float32)
    bins_x = (2 * (lane % 8)).astype(jnp.float32)
    cell_x = row + 8.0 * (lane // 64).astype(jnp.float32)

    def one(r):
        start = table_ref[section, 0, base + r].astype(jnp.int32)
        y_at, y_step, x_at, x_step = [table_ref[section, 1 + j, base + r] for j in range(4)]
        y_position = y_at + y_step * bins_y
        wy = [tent(y_position, y_step, row + 8.0 * h) for h in range(2)]
        wx = tent(x_at + x_step * bins_x, x_step, cell_x)
        rows = [jnp.broadcast_to(wy[y // 8][y % 8 : y % 8 + 1], (8, LANES)) for y in range(16)]
        weight = jnp.concatenate([rows[y] * wx for y in range(16)], axis=0)
        near, far = [], []
        for i in range(4):
            pair = slab[pl.ds(i * 8 * rb + r, 8, stride=rb), :]
            turned = pltpu.roll(pair, 64, 1)
            zero = jnp.zeros_like(pair)
            near.append(jnp.where(low, pair, zero))
            far.append(jnp.where(low, zero, turned))
            near.append(jnp.where(low, turned, zero) if i < 3 else zero)
            far.append(jnp.where(low, zero, pair) if i < 3 else zero)
        grads = jnp.concatenate(near + far, axis=0)
        out = jnp.dot(weight.astype(jnp.bfloat16), grads.astype(jnp.bfloat16), preferred_element_type=jnp.float32)
        for j in range(16):
            sums[pl.ds(start + WIDTH * j, 8), :] += out[8 * j : 8 * j + 8]

    def step(t, carry):
        for u in range(UNROLL):
            one(t * UNROLL + u)
        return carry

    lax.fori_loop(0, rb // UNROLL, step, 0)

    @pl.when(pl.program_id(0) == pl.num_programs(0) - 1)
    def _():
        def gather(upper_row, lower_row, cells):
            tiles = []
            for t in range(cells // 8):
                up, up_far = [sums[pl.ds(upper_row * WIDTH + 8 * t + s, 8), :] for s in (8, 0)]
                down, down_far = [sums[pl.ds(lower_row * WIDTH + 8 * t + s, 8), :] for s in (8, 0)]
                tiles.append(jnp.where(low, up, down_far) + pltpu.roll(jnp.where(low, down, up_far), 64, 1))
            return jnp.concatenate(tiles, axis=0)

        def fine_row(y, carry):
            fine_ref[y] = gather(BASES[0] + y, BASES[0] + 32 + y, 64).astype(jnp.bfloat16)
            return carry

        lax.fori_loop(0, 32, fine_row, 0)
        coarse_ref[...] = jnp.zeros_like(coarse_ref)
        for y in range(16):
            coarse_ref[1, y] = gather(BASES[1] + y, BASES[1] + 16 + y, 32).astype(jnp.bfloat16)
        for level, cells in ((2, 16), (3, 8)):
            for y in range(cells):
                tile = gather(BASES[level] + y, BASES[level] + y, cells)
                tile = jnp.where(low_half(cells), tile, 0.0).astype(jnp.bfloat16)
                coarse_ref[level, y, pl.ds(0, max(cells, 16)), :] = jnp.concatenate([tile, jnp.zeros_like(tile)], axis=0) if cells < 16 else tile


def spread(table, first, second, micros, block=64):
    steps = first.shape[0] // block
    return pl.pallas_call(
        spread_kernel,
        grid=(2 * steps,),
        in_specs=[
            pl.BlockSpec(memory_space=pltpu.SMEM),
            pl.BlockSpec((block, WIDE), lambda g: (jnp.minimum(g, steps - 1), 0)),
            pl.BlockSpec((block, WIDE), lambda g: (jnp.maximum(g - steps, 0), 0)),
        ],
        out_specs=[
            pl.BlockSpec((32, 64, LANES), lambda g: (0, 0, 0)),
            pl.BlockSpec((4, 16, 32, LANES), lambda g: (0, 0, 0, 0)),
        ],
        scratch_shapes=[pltpu.VMEM((32 * block, LANES), jnp.float32), pltpu.VMEM((CELLS, LANES), jnp.float32)],
        out_shape=[
            jax.ShapeDtypeStruct((32, 64, LANES), jnp.bfloat16),
            jax.ShapeDtypeStruct((4, 16, 32, LANES), jnp.bfloat16),
        ],
        cost_estimate=cost(micros),
        compiler_params=params(16),
    )(table, first, second)


def bin_order():
    pairs = [(2 * i + p) * POOL + e for i in range(3) for e in range(POOL) for p in range(2)]
    return pairs + [6 * POOL + e for e in range(POOL)]


def message_kernel(boxes_ref, routes_ref, labels_ref, targets_ref, out_ref):
    for s in range(2):
        rows = [boxes_ref[s].astype(jnp.float32), routes_ref[s : s + 1].astype(jnp.float32)]
        rows += [labels_ref[s : s + 1].astype(jnp.float32), targets_ref[s], jnp.zeros((6, 64), jnp.float32)]
        out_ref[:, pl.ds(64 * s, 64)] = jnp.concatenate(rows, axis=0)


def message(boxes, routes, labels, targets):
    return pl.pallas_call(
        message_kernel,
        out_shape=jax.ShapeDtypeStruct((16, LANES), jnp.float32),
        cost_estimate=cost(1.4),
    )(boxes, routes, labels, targets)


def prepare_kernel(me_ref, image_ref, own_ref, one_ref, two_ref, three_ref, info_ref, table_ref, gathered_ref):
    me = me_ref[0]
    for k, piece in enumerate((own_ref, one_ref, two_ref, three_ref)):
        gathered_ref[jnp.bitwise_xor(me, k)] = piece[...]
    height, width = image_ref[0, 0], image_ref[0, 1]
    for s in range(2):
        rows = jnp.concatenate([gathered_ref[d, :, pl.ds(64 * s, 64)] for d in range(4)], axis=1)
        info_ref[s] = rows
        boxes = rows[:4].astype(jnp.int32)
        route = rows[4:5].astype(jnp.int32)
        lines = []
        for axis, size in ((0, height), (1, width)):
            low_edge = jnp.clip(boxes[axis : axis + 1], 0, size * 16)
            high_edge = jnp.clip(boxes[axis + 2 : axis + 3], 0, size * 16)
            stride = jnp.left_shift(4, route)
            first = 28 * low_edge + (high_edge - low_edge) - 224 * stride
            cell = jnp.right_shift((jnp.right_shift(first, 8 + route) + 7) * 9363, 16) - 1
            units = 448 * stride
            scale = 1.0 / units.astype(jnp.float32)
            lines.append((cell, (first - cell * units).astype(jnp.float32) * scale, (2 * (high_edge - low_edge)).astype(jnp.float32) * scale))
        row = jnp.where(route == 0, BASES[0], jnp.where(route == 1, BASES[1], jnp.where(route == 2, BASES[2], BASES[3])))
        start = (row + lines[0][0]) * WIDTH + 8 + lines[1][0]
        parts = [start.astype(jnp.float32), lines[0][1], lines[0][2], lines[1][1], lines[1][2]]
        table_ref[s] = jnp.concatenate(parts + [jnp.zeros((3, rows.shape[1]), jnp.float32)], axis=0)


def prepare(me, image_size, pieces):
    rows = 2 * LANES
    smem, vmem = pl.BlockSpec(memory_space=pltpu.SMEM), pl.BlockSpec(memory_space=pltpu.VMEM)
    return pl.pallas_call(
        prepare_kernel,
        in_specs=[smem, smem] + [vmem] * 4,
        out_shape=[jax.ShapeDtypeStruct((2, 16, rows), jnp.float32), jax.ShapeDtypeStruct((2, 8, rows), jnp.float32)],
        scratch_shapes=[pltpu.VMEM((4, 16, LANES), jnp.float32)],
        cost_estimate=cost(1.5),
    )(me, image_size, *pieces)


def valid_edges(owner, image_ref):
    shift = 2 + owner
    round_up = jnp.left_shift(1, shift) - 1
    return [jnp.right_shift(image_ref[0, j] + round_up, shift) for j in range(2)]


def pack_kernel(owner_ref, image_ref, upper_ref, lower_ref, small_ref, own_ref, one_ref, two_ref, three_ref, coarse_ref):
    g = pl.program_id(0)
    owner = owner_ref[0]
    rows_valid, cols_valid = valid_edges(owner, image_ref)
    cell = lax.broadcasted_iota(jnp.int32, (GRID, LANES), 0)
    low = low_half(GRID)
    outs = (own_ref, one_ref, two_ref, three_ref)
    for y in range(upper_ref.shape[2]):
        top = (cell < cols_valid) & (g * upper_ref.shape[2] + y < rows_valid)
        bottom = (cell < cols_valid) & (32 + g * upper_ref.shape[2] + y < rows_valid)
        for c in range(2):
            a = jnp.where(top, upper_ref[0, 0, y, :, pl.ds(LANES * c, LANES)].astype(jnp.float32), 0.0)
            b = jnp.where(bottom, lower_ref[0, 0, y, :, pl.ds(LANES * c, LANES)].astype(jnp.float32), 0.0)
            even = jnp.where(low, a, pltpu.roll(b, 64, 1))
            if c == 0:
                even = jnp.where(owner == 0, even, 0.0)
            outs[2 * c][y] = even.astype(jnp.bfloat16)
            outs[2 * c + 1][y] = jnp.where(low, pltpu.roll(a, 64, 1), b).astype(jnp.bfloat16)

    @pl.when(g == 0)
    def _():
        low = low_half(32)
        cell = lax.broadcasted_iota(jnp.int32, (32, LANES), 0)
        for y in range(16):
            top = (cell < cols_valid) & (y < rows_valid)
            bottom = (cell < cols_valid) & (16 + y < rows_valid) & (owner < 2)
            for c in range(2):
                a = jnp.where(top, small_ref[0, 0, y, pl.ds(0, 32), pl.ds(LANES * c, LANES)].astype(jnp.float32), 0.0)
                b = jnp.where(bottom, small_ref[0, 0, 16 + y, pl.ds(0, 32), pl.ds(LANES * c, LANES)].astype(jnp.float32), 0.0)
                coarse_ref[2 * c, y] = jnp.where(low, a, pltpu.roll(b, 64, 1)).astype(jnp.bfloat16)
                coarse_ref[2 * c + 1, y] = jnp.where(low, pltpu.roll(a, 64, 1), b).astype(jnp.bfloat16)


def pack(owner, image_size, pyramid):
    return pl.pallas_call(
        pack_kernel,
        grid=(4,),
        in_specs=[
            pl.BlockSpec(memory_space=pltpu.SMEM),
            pl.BlockSpec(memory_space=pltpu.SMEM),
            pl.BlockSpec((1, 1, 8, GRID, CHANNELS), lambda g: (0, 0, g, 0, 0)),
            pl.BlockSpec((1, 1, 8, GRID, CHANNELS), lambda g: (0, 0, g + 4, 0, 0)),
            pl.BlockSpec((1, 1, 32, GRID, CHANNELS), lambda g: (0, 0, 0, 0, 0)),
        ],
        out_specs=[pl.BlockSpec((8, GRID, LANES), lambda g: (g, 0, 0))] * 4
        + [pl.BlockSpec((4, 16, 32, LANES), lambda g: (0, 0, 0, 0))],
        out_shape=[jax.ShapeDtypeStruct((32, GRID, LANES), jnp.bfloat16)] * 4
        + [jax.ShapeDtypeStruct((4, 16, 32, LANES), jnp.bfloat16)],
        cost_estimate=cost(2.7),
        compiler_params=params(16),
    )(owner, image_size, pyramid, pyramid, pyramid)


def unpack_kernel(owner_ref, image_ref, own_ref, one_ref, two_ref, three_ref, coarse_ref, out_ref):
    g = pl.program_id(0)
    owner = owner_ref[0]
    rows_valid, cols_valid = valid_edges(owner, image_ref)
    count = own_ref.shape[0]

    @pl.when(owner == 0)
    def _():
        cell = lax.broadcasted_iota(jnp.int32, (GRID, LANES), 0)
        low = low_half(GRID)
        quarters = (own_ref, one_ref, two_ref, three_ref)
        for y in range(count):
            top = (cell < cols_valid) & (g * count + y < rows_valid)
            bottom = (cell < cols_valid) & (32 + g * count + y < rows_valid)
            for c in range(2):
                a = quarters[2 * c][y].astype(jnp.float32)
                b = quarters[2 * c + 1][y].astype(jnp.float32)
                upper = jnp.where(low, a, pltpu.roll(b, 64, 1))
                lower = jnp.where(low, pltpu.roll(a, 64, 1), b)
                out_ref[0, y, :, pl.ds(LANES * c, LANES)] = jnp.where(top, upper, 0.0).astype(jnp.bfloat16)
                out_ref[1, y, :, pl.ds(LANES * c, LANES)] = jnp.where(bottom, lower, 0.0).astype(jnp.bfloat16)

    @pl.when(owner != 0)
    def _():
        out_ref[...] = jnp.zeros_like(out_ref)
        cell = lax.broadcasted_iota(jnp.int32, (32, LANES), 0)
        low = low_half(32)
        for y in range(count):
            top = (cell < cols_valid) & (g * count + y < rows_valid)
            line = (g % 2) * count + y
            for c in range(2):
                a = coarse_ref[2 * c, line].astype(jnp.float32)
                b = coarse_ref[2 * c + 1, line].astype(jnp.float32)
                upper = jnp.where(low, a, pltpu.roll(b, 64, 1))
                lower = jnp.where(low, pltpu.roll(a, 64, 1), b)
                row = jnp.where(g < 2, upper, lower)
                out_ref[0, y, pl.ds(0, 32), pl.ds(LANES * c, LANES)] = jnp.where(top, row, 0.0).astype(jnp.bfloat16)


def unpack(owner, image_size, fine, coarse, micros):
    return pl.pallas_call(
        unpack_kernel,
        grid=(4,),
        in_specs=[pl.BlockSpec(memory_space=pltpu.SMEM)] * 2
        + [pl.BlockSpec((8, GRID, LANES), lambda g: (g, 0, 0))] * 4
        + [pl.BlockSpec((4, 16, 32, LANES), lambda g: (0, 0, 0, 0))],
        out_specs=pl.BlockSpec((2, 8, GRID, CHANNELS), lambda g: (0, g, 0, 0)),
        out_shape=jax.ShapeDtypeStruct((2, 32, GRID, CHANNELS), jnp.bfloat16),
        cost_estimate=cost(micros),
        compiler_params=params(16),
    )(owner, image_size, *fine, coarse)


def to_bins_kernel(order_ref, in_ref, out_ref, rows):
    del order_ref
    width = in_ref.shape[2] // LANES
    for t in range(width):
        rows[t] = in_ref[0, :, pl.ds(t * LANES, LANES)].astype(jnp.float32)
    for place, source in enumerate(bin_order()):
        for t in range(width):
            out_ref[place, :, pl.ds(t * LANES, LANES)] = rows[t, pl.ds(source, 16, stride=49), :].astype(jnp.bfloat16)
    out_ref[49] = jnp.zeros(out_ref.shape[1:], jnp.bfloat16)


def to_bins(order, weight, section, micros):
    rows, width = weight.shape[1:]
    channels = rows // 49
    return pl.pallas_call(
        to_bins_kernel,
        grid=(channels // 16,),
        in_specs=[pl.BlockSpec(memory_space=pltpu.SMEM), pl.BlockSpec((1, 784, width), lambda c: (section, c, 0))],
        out_specs=pl.BlockSpec((50, 16, width), lambda c: (0, c, 0)),
        out_shape=jax.ShapeDtypeStruct((50, channels, width), jnp.bfloat16),
        scratch_shapes=[pltpu.VMEM((width // LANES, 784, LANES), jnp.float32)],
        cost_estimate=cost(micros),
        compiler_params=params(16),
    )(order, weight).reshape(WIDE, width)


def first_kernel(pooled_ref, weight_ref, out_ref):
    for n in range(0, out_ref.shape[1], 256):
        here = pl.ds(n, 256)
        out_ref[:, here] = jnp.dot(pooled_ref[...], weight_ref[:, here], preferred_element_type=jnp.float32).astype(jnp.bfloat16)


def first_product(pooled, weight, micros):
    vmem = pl.BlockSpec(memory_space=pltpu.VMEM)
    return pl.pallas_call(
        first_kernel,
        in_specs=[vmem, vmem],
        out_specs=vmem,
        out_shape=jax.ShapeDtypeStruct((pooled.shape[0], weight.shape[1]), jnp.bfloat16),
        cost_estimate=cost(micros),
        compiler_params=params(16),
    )(pooled, weight)


def back_kernel(order_ref, grads_ref, weight_ref, out_ref):
    del order_ref
    for n in range(0, WIDE, 640):
        here = pl.ds(n, 640)
        value = lax.dot_general(grads_ref[...], weight_ref[here, :], NT, preferred_element_type=jnp.float32)
        out_ref[:, here] = value.astype(jnp.bfloat16)


def back_product(order, grads, weight, micros):
    vmem = pl.BlockSpec(memory_space=pltpu.VMEM)
    return pl.pallas_call(
        back_kernel,
        in_specs=[pl.BlockSpec(memory_space=pltpu.SMEM), vmem, vmem],
        out_specs=vmem,
        out_shape=jax.ShapeDtypeStruct((grads.shape[0], WIDE), jnp.bfloat16),
        cost_estimate=cost(micros),
        compiler_params=params(16),
    )(order, grads, weight)


SPLIT = 1536
TAIL = WIDE - SPLIT


def outer_kernel(bits_ref, own, cross, own_pooled, cross_pooled, sent_one, kept_one, sent_two, kept_two):
    rows = own.shape[2]

    def product(pick, at, width, out):
        mine, theirs = [pick(ref).reshape(2 * rows, -1) for ref in (own, cross)]
        for n in range(0, width, 256):
            wide = min(256, width - n)
            here = pl.ds(at + n, wide)
            value = jnp.dot(mine, own_pooled[:, here], preferred_element_type=jnp.float32)
            value = value + jnp.dot(theirs, cross_pooled[:, here], preferred_element_type=jnp.float32)
            out[:, :, pl.ds(n, wide)] = value.astype(out.dtype).reshape(2, rows, wide)

    product(lambda ref: ref[:, bits_ref[1]], 0, SPLIT, sent_one)
    product(lambda ref: ref[bits_ref[3]], SPLIT, TAIL, sent_two)
    product(lambda ref: ref[:, bits_ref[0]], 0, SPLIT, kept_one)
    product(lambda ref: ref[bits_ref[2]], SPLIT, TAIL, kept_two)


def outer_sums(bits, own, cross, own_pooled, cross_pooled, micros):
    rows = own.shape[2]
    vmem = pl.BlockSpec(memory_space=pltpu.VMEM)
    kinds = [(width, dtype) for width in (SPLIT, TAIL) for dtype in (jnp.bfloat16, jnp.float32)]
    return pl.pallas_call(
        outer_kernel,
        in_specs=[pl.BlockSpec(memory_space=pltpu.SMEM)] + [vmem] * 4,
        out_specs=[vmem] * 4,
        out_shape=[jax.ShapeDtypeStruct((2, rows, width), dtype) for width, dtype in kinds],
        cost_estimate=cost(micros),
        compiler_params=params(16),
    )(bits, own, cross, own_pooled, cross_pooled)


def fold_kernel(bits_ref, kept_one, arrived_one, kept_two, arrived_two, one_ref, two_ref):
    up, low = bits_ref[3], bits_ref[1]
    one_ref[...] = (kept_one[up] + arrived_one[up].astype(jnp.float32)).astype(jnp.bfloat16)
    two_ref[...] = (kept_two[low] + arrived_two[low].astype(jnp.float32)).astype(jnp.bfloat16)


def fold(bits, kept_one, arrived_one, kept_two, arrived_two):
    rows = kept_one.shape[1]
    vmem = pl.BlockSpec(memory_space=pltpu.VMEM)
    return pl.pallas_call(
        fold_kernel,
        in_specs=[pl.BlockSpec(memory_space=pltpu.SMEM)] + [vmem] * 4,
        out_specs=[vmem] * 2,
        out_shape=[jax.ShapeDtypeStruct((rows, SPLIT), jnp.bfloat16), jax.ShapeDtypeStruct((rows, TAIL), jnp.bfloat16)],
        cost_estimate=cost(1.5),
        compiler_params=params(16),
    )(bits, kept_one, arrived_one, kept_two, arrived_two)


def from_bins_kernel(bits_ref, *refs):
    del bits_ref
    kept_one, arrived_one, last_one, kept_two, arrived_two, last_two = refs[:6]
    out_ref, turned = refs[-2:]
    for kept, arrived, last, at in ((kept_one, arrived_one, last_one, 0), (kept_two, arrived_two, last_two, SPLIT)):
        for t in range(kept.shape[2] // LANES):
            here = pl.ds(t * LANES, LANES)
            value = kept[0, :, here] + arrived[0, :, here].astype(jnp.float32) + last[:, here].astype(jnp.float32)
            turned[pl.ds(at + t * LANES, LANES), :] = jnp.transpose(value, (1, 0))
    for place, source in enumerate(bin_order()):
        out_ref[0, pl.ds(source, 64, stride=49), :] = turned[pl.ds(place * 64, 64), :]


def from_bins(bits, section, kept, arrived, last, before, rows):
    columns = kept[0].shape[1]
    specs = []
    for at, width in ((2, SPLIT), (0, TAIL)):
        both = pl.BlockSpec((1, columns, width), lambda i, b, at=at: (b[at], 0, 0))
        specs += [both, both, pl.BlockSpec((columns, width), lambda i, b: (0, 0))]
    operands = [kept[0], arrived[0], last[0], kept[1], arrived[1], last[1]]
    aliases = {}
    if before is not None:
        specs.append(pl.BlockSpec(memory_space=pl.ANY))
        operands.append(before)
        aliases = {7: 0}
    return pl.pallas_call(
        from_bins_kernel,
        grid_spec=pltpu.PrefetchScalarGridSpec(
            num_scalar_prefetch=1,
            grid=(1,),
            in_specs=specs,
            out_specs=pl.BlockSpec((1, rows, columns), lambda i, b: (section, 0, 0)),
            scratch_shapes=[pltpu.VMEM((WIDE, LANES), jnp.float32)],
        ),
        out_shape=jax.ShapeDtypeStruct((2, rows, columns), jnp.float32),
        input_output_aliases=aliases,
        cost_estimate=cost(3.4),
        compiler_params=params(16),
    )(bits, *operands)


def silu_slope(values):
    sigma = jax.nn.sigmoid(values)
    return sigma * (1.0 + values * (1.0 - sigma))


NT = (((1,), (1,)), ((), ()))
TN = (((0,), (0,)), ((), ()))
OUTER = 128


def head_kernel(
    me_ref, mine_ref, theirs_ref, info_ref, feature_bias_ref, hidden_ref, hidden_bias_ref, class_ref, class_bias_ref,
    delta_ref, delta_bias_ref,
    *refs, images,
):
    logits_ref, deltas_ref, small_ref, bias_ref, grad_feature_ref, stay_ref, away_ref, outer_scr, turned_scr, weight_scr, row_scr = refs[-11:]
    me, half = me_ref[0], me_ref[1]
    weight_scr[...] = jnp.zeros_like(weight_scr)
    weight_scr[pl.ds(0, CLASSES), :] = class_ref[0]
    weight_scr[pl.ds(OUTER, DELTAS), :] = delta_ref[0]
    row_scr[...] = jnp.zeros_like(row_scr)
    row_scr[:, pl.ds(0, CLASSES)] = class_bias_ref[0]
    row_scr[:, pl.ds(OUTER, DELTAS)] = delta_bias_ref[0]
    f32 = jnp.float32
    rows, hidden = mine_ref.shape
    pre_feature = mine_ref[...].astype(f32) + theirs_ref[...].astype(f32) + feature_bias_ref[0]
    gate_one = jax.nn.sigmoid(pre_feature)
    hidden_one = (pre_feature * gate_one).astype(jnp.bfloat16)
    pre_hidden = jnp.dot(hidden_one, hidden_ref[0], preferred_element_type=f32) + hidden_bias_ref[0]
    gate_two = jax.nn.sigmoid(pre_hidden)
    hidden_two = (pre_hidden * gate_two).astype(jnp.bfloat16)
    outer = lax.dot_general(hidden_two, weight_scr[...], NT, preferred_element_type=f32) + row_scr[...]
    outer_scr[...] = outer
    own = pl.ds(pl.multiple_of(me * (rows // 4), rows // 4), rows // 4)
    logits_ref[0] = outer_scr[own, pl.ds(0, CLASSES)]
    deltas_ref[0] = outer_scr[own, pl.ds(OUTER, DELTAS)]

    columns = jnp.transpose(info_ref[0], (1, 0))
    label = columns[:, 5:6].astype(jnp.int32)
    lane = lax.broadcasted_iota(jnp.int32, (rows, OUTER), 1)
    logits = jnp.where(lane < CLASSES, outer[:, :OUTER], -jnp.inf)
    shifted = jnp.exp(logits - jnp.max(logits, axis=1, keepdims=True))
    grad_logits = shifted / jnp.sum(shifted, axis=1, keepdims=True) - (lane == label).astype(f32)
    wide = lax.broadcasted_iota(jnp.int32, (rows, outer.shape[1] - OUTER), 1)
    hot = (wide // 4 == label) & (label < CLASSES - 1)
    picked = jnp.where(hot, outer[:, OUTER:], 0.0)
    grad_deltas = jnp.zeros_like(picked)
    for j in range(4):
        mine = wide % 4 == j
        chosen = jnp.sum(jnp.where(mine, picked, 0.0), axis=1, keepdims=True)
        error = jnp.clip(chosen - columns[:, 6 + j : 7 + j], -1.0, 1.0)
        grad_deltas = jnp.where(mine & hot, error, grad_deltas)
    grad_outer = jnp.concatenate([grad_logits, grad_deltas], axis=1).astype(jnp.bfloat16)

    grad_two = jnp.dot(grad_outer, weight_scr[...], preferred_element_type=f32)
    slope_two = gate_two * (1.0 + pre_hidden * (1.0 - gate_two))
    grad_pre_hidden = (grad_two * slope_two).astype(jnp.bfloat16)
    grad_one = lax.dot_general(grad_pre_hidden, hidden_ref[0], NT, preferred_element_type=f32)
    slope_one = gate_one * (1.0 + pre_feature * (1.0 - gate_one))
    grad_feature = grad_one * slope_one
    grad_pre_feature = grad_feature.astype(jnp.bfloat16)
    grad_feature_ref[...] = grad_pre_feature
    turned_scr[...] = jnp.transpose(grad_feature, (1, 0)).astype(jnp.bfloat16)
    stay_ref[...] = turned_scr[pl.ds(pl.multiple_of(half * (hidden // 2), hidden // 2), hidden // 2), :]
    away_ref[...] = turned_scr[pl.ds(pl.multiple_of((1 - half) * (hidden // 2), hidden // 2), hidden // 2), :]

    run = hidden // (4 * images)
    row = lax.broadcasted_iota(jnp.int32, (hidden, hidden // 4), 0)
    col = lax.broadcasted_iota(jnp.int32, (hidden, hidden // 4), 1)
    pick = (row == (col // run) * (4 * run) + me * run + col % run).astype(jnp.bfloat16)
    one_rows = jnp.dot(hidden_one, pick, preferred_element_type=f32).astype(jnp.bfloat16)
    two_rows = jnp.dot(hidden_two, pick, preferred_element_type=f32).astype(jnp.bfloat16)
    small_ref[0, :, pl.ds(0, hidden)] = lax.dot_general(one_rows, grad_pre_hidden, TN, preferred_element_type=f32).astype(jnp.bfloat16)
    small_ref[0, :, pl.ds(hidden, outer.shape[1])] = lax.dot_general(two_rows, grad_outer, TN, preferred_element_type=f32).astype(jnp.bfloat16)
    bias_ref[0, :, pl.ds(0, hidden)] = jnp.sum(grad_pre_feature.astype(f32), axis=0, keepdims=True)
    bias_ref[0, :, pl.ds(hidden, hidden)] = jnp.sum(grad_pre_hidden.astype(f32), axis=0, keepdims=True)
    bias_ref[0, :, pl.ds(2 * hidden, outer.shape[1])] = jnp.sum(grad_outer.astype(f32), axis=0, keepdims=True)


def head(me, mine, theirs, section, stacked, images, before, micros):
    rows, hidden = mine.shape
    width = 512
    sections = stacked[0].shape[0]

    def whole(shape):
        return pl.BlockSpec(shape, lambda g, m: (0,) * len(shape))

    def of_section(array):
        return pl.BlockSpec((1,) + array.shape[1:], lambda g, m: (section, 0, 0))

    def kernel(*refs):
        head_kernel(*refs, images=images)

    shared = [
        jax.ShapeDtypeStruct((sections, rows // 4, CLASSES), jnp.float32),
        jax.ShapeDtypeStruct((sections, rows // 4, DELTAS), jnp.float32),
        jax.ShapeDtypeStruct((sections, hidden // 4, hidden + width), jnp.bfloat16),
        jax.ShapeDtypeStruct((sections, 1, 2 * hidden + width), jnp.float32),
    ]
    single = [
        jax.ShapeDtypeStruct((rows, hidden), jnp.bfloat16),
        jax.ShapeDtypeStruct((hidden // 2, rows), jnp.bfloat16),
        jax.ShapeDtypeStruct((hidden // 2, rows), jnp.bfloat16),
    ]
    return pl.pallas_call(
        kernel,
        grid_spec=pltpu.PrefetchScalarGridSpec(
            num_scalar_prefetch=1,
            grid=(1,),
            in_specs=[whole(mine.shape), whole(theirs.shape)]
            + [of_section(a) for a in stacked]
            + [pl.BlockSpec(memory_space=pl.ANY)] * len(before),
            out_specs=[of_section(o) for o in shared] + [whole(o.shape) for o in single],
            scratch_shapes=[
                pltpu.VMEM((rows, width), jnp.float32),
                pltpu.VMEM((hidden, rows), jnp.bfloat16),
                pltpu.VMEM((width, hidden), jnp.bfloat16),
                pltpu.VMEM((1, width), jnp.float32),
            ],
        ),
        out_shape=shared + single,
        input_output_aliases={3 + len(stacked) + j: j for j in range(len(before))},
        cost_estimate=cost(micros),
        compiler_params=params(28),
    )(me, mine, theirs, *stacked, *before)


def swap(value, axis, bit):
    size = lax.axis_size(axis)
    return lax.ppermute(value, axis, [(i, i ^ bit) for i in range(size)])


def after(value, *others):
    return lax.optimization_barrier((value,) + others)[0]


def choose(array, axis, bit):
    return lax.dynamic_index_in_dim(array, bit, axis, keepdims=False)


def split_bits(array, bits):
    return array.reshape((2,) * bits + (array.shape[0] >> bits,) + array.shape[1:])


def body(
    pyramid,
    image_size,
    region_boxes,
    routes,
    labels,
    targets,
    feature_weight,
    feature_bias,
    hidden_weight,
    hidden_bias,
    class_weight,
    class_bias,
    delta_weight,
    delta_bias,
):
    images = lax.axis_size("img")
    me = lax.axis_index("lvl").astype(jnp.int32)
    image = lax.axis_index("img").astype(jnp.int32)
    sections = routes.shape[0]
    features = feature_weight.shape[1]
    hidden = hidden_weight.shape[2]
    top = images // 2
    steps = images.bit_length() - 2
    half = jnp.minimum(image & top, 1)
    own_bits = [jnp.minimum(image & (1 << b), 1) for b in range(steps)]
    me_list = jnp.stack([me, half])

    own, *quarters, small = pack(me_list, image_size, pyramid)
    arrived = [lax.ppermute(q, "lvl", [(0, d + 1)]) for d, q in enumerate(quarters)]
    coarse = lax.all_to_all(small, "lvl", split_axis=0, concat_axis=0, tiled=True)
    sent = message(region_boxes, routes, labels, targets)
    info, table = prepare(me_list, image_size, [sent] + [swap(sent, "lvl", k) for k in (1, 2, 3)])
    cross_table = swap(table, "img", top)
    weight_a = to_bins(me_list, feature_weight, 0, 10)
    fine = own + arrived[0] + arrived[1] + arrived[2]
    cross_fine = swap(fine, "img", top)
    cross_coarse = swap(coarse, "img", top)

    stacked = (
        info, feature_bias[:, None], hidden_weight, hidden_bias[:, None], jnp.swapaxes(class_weight, 1, 2),
        class_bias[:, None], jnp.swapaxes(delta_weight, 1, 2), delta_bias[:, None],
    )

    def run_head(s, parts, before, ready, micros):
        results = head(after(me_list, *ready), *parts, s, stacked, images, before, micros)
        shared, (grads, stay, away) = results[:4], results[4:]
        return shared, grads, stay, swap(away, "img", top)

    def add(first, second):
        return (first.astype(jnp.float32) + second.astype(jnp.float32)).astype(jnp.bfloat16)

    pooled_a = crop(after(table, weight_a), 0, fine, coarse, 12)
    part_a = first_product(pooled_a, weight_a, 1)
    weight_b = to_bins(after(me_list, part_a), feature_weight, 1, 8)
    chip_a = add(part_a, swap(part_a, "lvl", 1))
    pooled_b = crop(after(table, weight_b, chip_a), 1, fine, coarse, 8)
    part_b = first_product(pooled_b, weight_b, 0)
    shared, grads_a, stay_a, cross_a = run_head(0, (chip_a, swap(chip_a, "lvl", 2)), (), [part_b], 8)
    chip_b = add(after(part_b, grads_a), swap(part_b, "lvl", 1))
    slots_a = back_product(after(me_list, chip_b), grads_a, weight_a, 0)
    far_a = crop(after(cross_table, chip_b), 0, cross_fine, cross_coarse, 8)
    slots_a = after(slots_a, far_a)
    cross_a = after(cross_a, far_a)
    shared, grads_b, stay_b, cross_b = run_head(1, (chip_b, swap(chip_b, "lvl", 2)), shared, [slots_a, cross_a], 0)
    logits, deltas, small, biases = shared
    if images == 8:
        bits = jnp.stack([own_bits[0], 1 - own_bits[0], own_bits[1], 1 - own_bits[1]])

        def weight_sums(stay, cross, pooled, far, ready):
            pieces = [v.reshape(2, 2, hidden // images, -1) for v in (stay, cross)]
            sent_one, kept_one, sent_two, kept_two = outer_sums(after(bits, *ready), *pieces, pooled, far, 0)
            return (kept_one, kept_two), (swap(sent_one, "img", 1), swap(sent_two, "img", 2))

        def second_step(kept, arrived, ready):
            one, two = fold(after(bits, *ready), kept[0], arrived[0], kept[1], arrived[1])
            return one, (swap(one, "img", 2), swap(two, "img", 1))

        kept_a, arrived_a = weight_sums(stay_a, cross_a, pooled_a, far_a, [grads_b])
        slots_b = back_product(after(me_list, kept_a[0]), grads_b, weight_b, 12)
        fine_grad, coarse_grad = spread(table, slots_a, slots_b, 0)
        folded, last_a = second_step(kept_a, arrived_a, [fine_grad])
        far_b = crop(after(cross_table, folded, cross_b), 1, cross_fine, cross_coarse, 50)
        kept_b, arrived_b = weight_sums(stay_b, cross_b, pooled_b, far_b, [])
        biases = after(biases, kept_a[0])
        late = [kept_b[0]]
    else:
        slots_b = back_product(me_list, grads_b, weight_b, 5)
        fine_grad, coarse_grad = spread(table, slots_a, slots_b, 20)
        far_b = crop(cross_table, 1, cross_fine, cross_coarse, 10)
        late = []
        totals = []
        for stay, cross, pooled, far in ((stay_a, cross_a, pooled_a, far_a), (stay_b, cross_b, pooled_b, far_b)):
            total = jnp.dot(stay, pooled, preferred_element_type=jnp.float32)
            total = total + jnp.dot(cross, far, preferred_element_type=jnp.float32)
            for b in range(steps)[::-1]:
                halves = split_bits(total, 1)
                away = choose(halves, 0, 1 - own_bits[b]).astype(jnp.bfloat16)
                total = choose(halves, 0, own_bits[b]) + swap(away, "img", 1 << b).astype(jnp.float32)
            totals.append(total[:, :features])
        order = bin_order()
        back = jnp.array([order.index(j) for j in range(49)])
        total = jnp.stack(totals)
        total = total.reshape(sections, total.shape[1], 49, features // 49)[:, :, back]
        feature_weight_grad = total.transpose(0, 3, 2, 1).reshape(sections, features, -1)

    pieces = [fine_grad] + [lax.ppermute(fine_grad, "lvl", [(d, 0)]) for d in (1, 2, 3)]
    coarse_all = lax.all_to_all(coarse_grad, "lvl", split_axis=0, concat_axis=0, tiled=True)
    pyramid_grad = unpack(after(me_list, *late), image_size, pieces, coarse_all, 12)
    if images == 8:
        feature_weight_grad = from_bins(after(bits, pyramid_grad), 0, kept_a, arrived_a, last_a, None, features)
        last_b = second_step(kept_b, arrived_b, [feature_weight_grad])[1]
        feature_weight_grad = from_bins(bits, 1, kept_b, arrived_b, last_b, feature_weight_grad, features)
    pyramid_grad = pyramid_grad.reshape(1, 1, GRID, GRID, CHANNELS)

    small = lax.psum_scatter(after(small, fine_grad), "img", scatter_dimension=1, tiled=True).astype(jnp.float32)
    biases = biases.reshape(sections, -1)
    bit = top
    while bit:
        biases = biases + swap(biases, "img", bit)
        bit //= 2
    outer_at = 2 * hidden
    delta_at = outer_at + OUTER
    return (
        logits,
        deltas,
        pyramid_grad,
        feature_weight_grad,
        biases[:, :hidden],
        small[:, :, :hidden],
        biases[:, hidden:outer_at],
        small[:, :, hidden : hidden + CLASSES],
        biases[:, outer_at : outer_at + CLASSES],
        small[:, :, hidden + OUTER : hidden + OUTER + DELTAS],
        biases[:, delta_at : delta_at + DELTAS],
    )


def solution(mesh):
    return jax.shard_map(
        body,
        mesh=mesh,
        in_specs=(
            P("img", "lvl", None, None, None),
            P("img", None),
            P(None, None, ("img", "lvl")),
            P(None, ("img", "lvl")),
            P(None, ("img", "lvl")),
            P(None, None, ("img", "lvl")),
            P(None, "lvl", None),
            P(),
            P(),
            P(),
            P(),
            P(),
            P(),
            P(),
        ),
        out_specs=(
            P(None, ("img", "lvl"), None),
            P(None, ("img", "lvl"), None),
            P("img", "lvl", None, None, None),
            P(None, "lvl", "img"),
            P(),
            P(None, ("img", "lvl"), None),
            P(),
            P(None, ("img", "lvl"), None),
            P(),
            P(None, ("img", "lvl"), None),
            P(),
        ),
        check_vma=False,
    )
```

```python
import jax
import jax.numpy as jnp
from jax import lax
from jax.experimental import pallas as pl
from jax.experimental.pallas import tpu as pltpu
from jax.sharding import PartitionSpec as P

CHANNELS = 256
CLASSES = 81
POOL = 7
GRID = 64
DELTAS = 320

WIDTH = 80
ROWS = 140
BASES = (1, 66, 99, 116)
CELLS = ROWS * WIDTH
LANES = 128
WIDE = 3200
EXTRA = 16
FINE = 2048
NOTES = FINE + 3 * 512
BUFFER = NOTES + 4 * 32
UNROLL = 64


def cost(microseconds):
    return pl.CostEstimate(flops=int(microseconds * SCALE * 1_150_000_000), bytes_accessed=0, transcendentals=0)


def in_hbm(array):
    return pltpu.with_memory_space_constraint(array, pltpu.HBM)


def params(mebibytes):
    return pltpu.CompilerParams(vmem_limit_bytes=mebibytes << 20)


SCALE = 1.0
CROSS = "permute"


def low_half(rows):
    return lax.broadcasted_iota(jnp.int32, (rows, LANES), 1) < 64


def tent(position, step, cell):
    first = jnp.maximum(1.0 - jnp.abs(position - cell), 0.0)
    second = jnp.maximum(1.0 - jnp.abs(position + step - cell), 0.0)
    return ((first + second) * 0.5).astype(jnp.bfloat16).astype(jnp.float32)


def place_rows(maps, upper, lower, upper_row, lower_row, cells):
    low = low_half(8)
    tiles = cells // 8
    zero = jnp.zeros((8, LANES), jnp.float32)
    values = [upper[8 * t : 8 * t + 8] for t in range(tiles)]
    turned = [pltpu.roll(v, 64, 1) for v in values]
    for t in range(-1, tiles):
        here, here_turned = (values[t], turned[t]) if t >= 0 else (zero, zero)
        after, after_turned = (values[t + 1], turned[t + 1]) if t + 1 < tiles else (zero, zero)
        maps[pl.ds(upper_row * WIDTH + 8 + 8 * t, 8), :] = jnp.where(low, here, after_turned)
        maps[pl.ds(lower_row * WIDTH + 8 + 8 * t, 8), :] = jnp.where(low, here_turned, after)


def fill_maps(maps, levels_ref):
    zero = jnp.zeros((8, LANES), jnp.float32)
    for row in (0, BASES[1] - 1):
        for t in range(WIDTH // 8):
            maps[pl.ds(row * WIDTH + 8 * t, 8), :] = zero

    def clear_edge(y, carry):
        maps[pl.ds(pl.multiple_of((BASES[0] + y) * WIDTH + WIDTH - 8, 8), 8), :] = zero
        return carry

    lax.fori_loop(0, GRID, clear_edge, 0, unroll=8)

    def clear(t, carry):
        maps[pl.ds(pl.multiple_of(BASES[1] * WIDTH + t * 160, 160), 160), :] = jnp.zeros((160, LANES), jnp.float32)
        return carry

    lax.fori_loop(0, (ROWS - BASES[1]) * WIDTH // 160, clear, 0, unroll=2)

    def fine_row(y, carry):
        row = levels_ref[0, pl.ds(pl.multiple_of(y * 64, 64), 64), :].astype(jnp.float32)
        place_rows(maps, row, row, BASES[0] + y, BASES[0] + 32 + y, 64)
        return carry

    lax.fori_loop(0, 32, fine_row, 0, unroll=4)
    for level, cells in ((1, 32), (2, 16), (3, 8)):
        for y in range(cells // 2 if level == 1 else cells):
            row = levels_ref[0, pl.ds(FINE + (level - 1) * 512 + y * 32, 32), :].astype(jnp.float32)[:cells]
            if level == 1:
                place_rows(maps, row, row, BASES[1] + y, BASES[1] + 16 + y, 32)
            else:
                place_upper(maps, row, BASES[level] + y, cells)


def place_upper(maps, row, at, cells):
    low = low_half(8)
    tiles = cells // 8
    zero = jnp.zeros((8, LANES), jnp.float32)
    values = [row[8 * t : 8 * t + 8] for t in range(tiles)]
    for t in range(-1, tiles):
        here = values[t] if t >= 0 else zero
        after = pltpu.roll(values[t + 1], 64, 1) if t + 1 < tiles else zero
        maps[pl.ds(at * WIDTH + 8 + 8 * t, 8), :] = jnp.where(low, here, after)


def crop_kernel(slot_ref, table_ref, levels_ref, out_ref, slab, maps, section):
    del slot_ref
    rb = out_ref.shape[0]
    base = pl.program_id(0) * rb

    @pl.when(pl.program_id(0) == 0)
    def _():
        fill_maps(maps, levels_ref)

    low = low_half(8)
    lane = lax.broadcasted_iota(jnp.int32, (8, LANES), 1)
    bins = (2 * lax.broadcasted_iota(jnp.int32, (8, LANES), 0)).astype(jnp.float32)
    lane_y = (lane // 8).astype(jnp.float32)
    lane_x = (lane % 8).astype(jnp.float32)

    def one(r):
        start = table_ref[section, 0, base + r].astype(jnp.int32)
        y_at, y_step, x_at, x_step = [table_ref[section, 1 + j, base + r] for j in range(4)]
        window = jnp.concatenate([maps[pl.ds(start + WIDTH * j, 8), :] for j in range(16)], axis=0)
        wy = tent(y_at + y_step * bins, y_step, lane_y)
        x_position = x_at + x_step * bins
        wx = [tent(x_position, x_step, lane_x + 8.0 * h) for h in range(2)]
        rows = [jnp.broadcast_to(wy[b : b + 1], (8, LANES)) for b in range(POOL)]
        weight = jnp.concatenate([rows[b] * wx[h] for h in range(2) for b in range(POOL)], axis=0)
        both = jnp.dot(weight.astype(jnp.bfloat16), window.astype(jnp.bfloat16), preferred_element_type=jnp.float32)
        near = [both[8 * b : 8 * b + 8] for b in range(POOL)]
        far = [both[56 + 8 * b : 64 + 8 * b] for b in range(POOL)]
        zero = jnp.zeros((8, LANES), jnp.float32)
        for i in range(4):
            near_odd, far_odd = (near[2 * i + 1], far[2 * i + 1]) if i < 3 else (zero, zero)
            pair = jnp.where(low, near[2 * i], far_odd) + pltpu.roll(jnp.where(low, near_odd, far[2 * i]), 64, 1)
            slab[pl.ds(i * 8 * rb + r, 8, stride=rb), :] = pair

    def step(t, carry):
        for u in range(UNROLL):
            one(t * UNROLL + u)
        return carry

    lax.fori_loop(0, rb // UNROLL, step, 0)
    for i in range(3):
        for e in range(POOL):
            out_ref[:, pl.ds((7 * i + e) * LANES, LANES)] = slab[pl.ds((8 * i + e) * rb, rb), :].astype(jnp.bfloat16)
    for j in range(4):
        first = slab[pl.ds((24 + 2 * j) * rb, rb), :]
        if j < 3:
            second = slab[pl.ds((25 + 2 * j) * rb, rb), :]
            joined = jnp.where(low_half(rb), first, pltpu.roll(second, 64, 1))
            out_ref[:, pl.ds((21 + j) * LANES, LANES)] = joined.astype(jnp.bfloat16)
        else:
            out_ref[:, pl.ds(24 * LANES, LANES)] = jnp.where(low_half(rb), first, 0.0).astype(jnp.bfloat16)


def crop(slot, table, section, levels, micros, block=64):
    count = table.shape[2]
    return pl.pallas_call(
        lambda *refs: crop_kernel(*refs, section),
        grid_spec=pltpu.PrefetchScalarGridSpec(
            num_scalar_prefetch=1,
            grid=(count // block,),
            in_specs=[
                pl.BlockSpec(memory_space=pltpu.SMEM),
                pl.BlockSpec((1, BUFFER, LANES), lambda g, s: (s[0], 0, 0)),
            ],
            out_specs=pl.BlockSpec((block, WIDE), lambda g, s: (g, 0)),
            scratch_shapes=[pltpu.VMEM((32 * block, LANES), jnp.float32), pltpu.VMEM((CELLS, LANES), jnp.float32)],
        ),
        out_shape=jax.ShapeDtypeStruct((count, WIDE), jnp.bfloat16),
        cost_estimate=cost(micros),
        compiler_params=params(11),
    )(slot, table, levels)


def spread_kernel(table_ref, first_ref, second_ref, out_ref, slab, sums):
    rb = first_ref.shape[0]
    steps = pl.num_programs(0) // 2
    section = pl.program_id(0) // steps
    base = (pl.program_id(0) % steps) * rb

    @pl.when(pl.program_id(0) == 0)
    def _():
        def clear(t, carry):
            sums[pl.ds(pl.multiple_of(t * 160, 160), 160), :] = jnp.zeros((160, LANES), jnp.float32)
            return carry

        lax.fori_loop(0, CELLS // 160, clear, 0, unroll=2)
        for i in range(4):
            slab[pl.ds((8 * i + 7) * rb, rb), :] = jnp.zeros((rb, LANES), jnp.float32)

    def lay_out(grads_ref):
        for i in range(3):
            for e in range(POOL):
                slab[pl.ds((8 * i + e) * rb, rb), :] = grads_ref[:, pl.ds((7 * i + e) * LANES, LANES)].astype(jnp.float32)
        for j in range(4):
            pair = grads_ref[:, pl.ds((21 + j) * LANES, LANES)].astype(jnp.float32)
            slab[pl.ds((24 + 2 * j) * rb, rb), :] = pair
            if j < 3:
                slab[pl.ds((25 + 2 * j) * rb, rb), :] = pltpu.roll(pair, 64, 1)

    @pl.when(section == 0)
    def _():
        lay_out(first_ref)

    @pl.when(section == 1)
    def _():
        lay_out(second_ref)

    low = low_half(8)
    lane = lax.broadcasted_iota(jnp.int32, (8, LANES), 1)
    row = lax.broadcasted_iota(jnp.int32, (8, LANES), 0).astype(jnp.float32)
    bins_y = (2 * ((lane // 8) % 8)).astype(jnp.float32)
    bins_x = (2 * (lane % 8)).astype(jnp.float32)
    cell_x = row + 8.0 * (lane // 64).astype(jnp.float32)

    def one(r):
        start = table_ref[section, 0, base + r].astype(jnp.int32)
        y_at, y_step, x_at, x_step = [table_ref[section, 1 + j, base + r] for j in range(4)]
        y_position = y_at + y_step * bins_y
        wy = [tent(y_position, y_step, row + 8.0 * h) for h in range(2)]
        wx = tent(x_at + x_step * bins_x, x_step, cell_x)
        rows = [jnp.broadcast_to(wy[y // 8][y % 8 : y % 8 + 1], (8, LANES)) for y in range(16)]
        weight = jnp.concatenate([rows[y] * wx for y in range(16)], axis=0)
        near, far = [], []
        for i in range(4):
            pair = slab[pl.ds(i * 8 * rb + r, 8, stride=rb), :]
            turned = pltpu.roll(pair, 64, 1)
            zero = jnp.zeros_like(pair)
            near.append(jnp.where(low, pair, zero))
            far.append(jnp.where(low, zero, turned))
            near.append(jnp.where(low, turned, zero) if i < 3 else zero)
            far.append(jnp.where(low, zero, pair) if i < 3 else zero)
        grads = jnp.concatenate(near + far, axis=0)
        out = jnp.dot(weight.astype(jnp.bfloat16), grads.astype(jnp.bfloat16), preferred_element_type=jnp.float32)
        for j in range(16):
            sums[pl.ds(start + WIDTH * j, 8), :] += out[8 * j : 8 * j + 8]

    def step(t, carry):
        for u in range(UNROLL):
            one(t * UNROLL + u)
        return carry

    lax.fori_loop(0, rb // UNROLL, step, 0)

    @pl.when(pl.program_id(0) == pl.num_programs(0) - 1)
    def _():
        def gather(upper_row, lower_row, cells):
            tiles = []
            for t in range(cells // 8):
                up, up_far = [sums[pl.ds(upper_row * WIDTH + 8 * t + s, 8), :] for s in (8, 0)]
                down, down_far = [sums[pl.ds(lower_row * WIDTH + 8 * t + s, 8), :] for s in (8, 0)]
                tiles.append(jnp.where(low, up, down_far) + pltpu.roll(jnp.where(low, down, up_far), 64, 1))
            return jnp.concatenate(tiles, axis=0)

        def fine_row(y, carry):
            here = pl.ds(pl.multiple_of(y * 64, 64), 64)
            out_ref[0, here, :] = gather(BASES[0] + y, BASES[0] + 32 + y, 64).astype(jnp.bfloat16)
            return carry

        lax.fori_loop(0, 32, fine_row, 0, unroll=4)
        out_ref[1:4, pl.ds(0, 512), :] = jnp.zeros((3, 512, LANES), jnp.bfloat16)
        for y in range(16):
            out_ref[1, pl.ds(32 * y, 32), :] = gather(BASES[1] + y, BASES[1] + 16 + y, 32).astype(jnp.bfloat16)
        for level, cells in ((2, 16), (3, 8)):
            for y in range(cells):
                tile = gather(BASES[level] + y, BASES[level] + y, cells)
                tile = jnp.where(low_half(cells), tile, 0.0)
                if cells < 16:
                    tile = jnp.concatenate([tile, jnp.zeros_like(tile)], axis=0)
                out_ref[level, pl.ds(32 * y, 16), :] = tile.astype(jnp.bfloat16)


def spread(table, first, second, micros, block=64):
    steps = first.shape[0] // block
    return pl.pallas_call(
        spread_kernel,
        grid=(2 * steps,),
        in_specs=[
            pl.BlockSpec(memory_space=pltpu.SMEM),
            pl.BlockSpec((block, WIDE), lambda g: (jnp.minimum(g, steps - 1), 0)),
            pl.BlockSpec((block, WIDE), lambda g: (jnp.maximum(g - steps, 0), 0)),
        ],
        out_specs=pl.BlockSpec((4, FINE, LANES), lambda g: (0, 0, 0)),
        scratch_shapes=[pltpu.VMEM((32 * block, LANES), jnp.float32), pltpu.VMEM((CELLS, LANES), jnp.float32)],
        out_shape=jax.ShapeDtypeStruct((4, FINE, LANES), jnp.bfloat16),
        cost_estimate=cost(micros),
        compiler_params=params(15),
    )(table, first, second)


def bin_order():
    pairs = [(2 * i + p) * POOL + e for i in range(3) for e in range(POOL) for p in range(2)]
    return pairs + [6 * POOL + e for e in range(POOL)]


def write_note(boxes_ref, routes_ref, labels_ref, targets_ref, image_ref):
    halves = []
    for s in range(2):
        boxes = boxes_ref[s]
        high = jnp.right_shift(boxes, 6)
        rest = targets_ref[s]
        parts = [high.astype(jnp.float32), (boxes - 64 * high).astype(jnp.float32)]
        parts += [routes_ref[s : s + 1].astype(jnp.float32), labels_ref[s : s + 1].astype(jnp.float32)]
        for _ in range(3):
            part = rest.astype(jnp.bfloat16).astype(jnp.float32)
            parts.append(part)
            rest = rest - part
        parts += [jnp.full((1, 64), image_ref[0, j], jnp.int32).astype(jnp.float32) for j in range(2)]
        halves.append(jnp.concatenate(parts + [jnp.zeros((8, 64), jnp.float32)], axis=0))
    return jnp.concatenate(halves, axis=1).astype(jnp.bfloat16)


def decode(notes, info_ref, table_ref):
    notes = [n.astype(jnp.float32) for n in notes]
    for s in range(2):
        rows = jnp.concatenate([n[:, 64 * s : 64 * s + 64] for n in notes], axis=1)
        boxes_float = rows[:4] * 64.0 + rows[4:8]
        targets = (rows[10:14] + rows[14:18]) + rows[18:22]
        pad = jnp.zeros((6, rows.shape[1]), jnp.float32)
        info_ref[s] = jnp.concatenate([boxes_float, rows[8:10], targets, pad], axis=0)
        boxes = boxes_float.astype(jnp.int32)
        route = rows[8:9].astype(jnp.int32)
        sizes = rows[22:24].astype(jnp.int32) * 16
        lines = []
        for axis in range(2):
            limit = sizes[axis : axis + 1]
            low_edge = jnp.minimum(jnp.maximum(boxes[axis : axis + 1], 0), limit)
            high_edge = jnp.minimum(jnp.maximum(boxes[axis + 2 : axis + 3], 0), limit)
            stride = jnp.left_shift(4, route)
            first = 28 * low_edge + (high_edge - low_edge) - 224 * stride
            cell = jnp.right_shift((jnp.right_shift(first, 8 + route) + 7) * 9363, 16) - 1
            units = 448 * stride
            scale = 1.0 / units.astype(jnp.float32)
            lines.append((cell, (first - cell * units).astype(jnp.float32) * scale, (2 * (high_edge - low_edge)).astype(jnp.float32) * scale))
        row = jnp.where(route == 0, BASES[0], jnp.where(route == 1, BASES[1], jnp.where(route == 2, BASES[2], BASES[3])))
        start = (row + lines[0][0]) * WIDTH + 8 + lines[1][0]
        parts = [start.astype(jnp.float32), lines[0][1], lines[0][2], lines[1][1], lines[1][2]]
        table_ref[s] = jnp.concatenate(parts + [jnp.zeros((3, rows.shape[1]), jnp.float32)], axis=0)


TABLES = [jax.ShapeDtypeStruct((2, 16, 256), jnp.float32), jax.ShapeDtypeStruct((2, 8, 256), jnp.float32)]


def arrange_kernel(slot_ref, own_ref, one_ref, two_ref, three_ref, coarse_ref, levels_ref, info_ref, table_ref):
    slot = slot_ref[0]
    fine = own_ref[...] + one_ref[...] + two_ref[...] + three_ref[...]
    levels_ref[slot, pl.ds(0, FINE), :] = fine.reshape(FINE, LANES)
    for level in range(1, 4):
        levels_ref[slot, pl.ds(FINE + (level - 1) * 512, 512), :] = coarse_ref[level, pl.ds(0, 512), :]
    for d in range(4):
        levels_ref[slot, pl.ds(NOTES + 32 * d, 32), :] = coarse_ref[d, pl.ds(512, 32), :]
    decode([coarse_ref[d, pl.ds(512, 32), :] for d in range(4)], info_ref, table_ref)


def arrange(slot, slots, own, arrived, coarse):
    vmem = pl.BlockSpec(memory_space=pltpu.VMEM)
    return pl.pallas_call(
        arrange_kernel,
        in_specs=[pl.BlockSpec(memory_space=pltpu.SMEM)] + [vmem] * 5,
        out_shape=[jax.ShapeDtypeStruct((slots, BUFFER, LANES), jnp.bfloat16)] + TABLES,
        cost_estimate=cost(2),
        compiler_params=params(7),
    )(slot, own, *arrived, coarse)


def prepare_kernel(slot_ref, levels_ref, info_ref, table_ref):
    slot = slot_ref[0]
    decode([levels_ref[slot, pl.ds(NOTES + 32 * d, 32), :] for d in range(4)], info_ref, table_ref)


def prepare(slot, levels):
    vmem = pl.BlockSpec(memory_space=pltpu.VMEM)
    return pl.pallas_call(
        prepare_kernel,
        in_specs=[pl.BlockSpec(memory_space=pltpu.SMEM), vmem],
        out_shape=TABLES,
        cost_estimate=cost(1),
    )(slot, levels)[1]


def valid_edges(owner, image_ref):
    shift = 2 + owner
    round_up = jnp.left_shift(1, shift) - 1
    return [jnp.right_shift(image_ref[0, j] + round_up, shift) for j in range(2)]


def pack_kernel(
    owner_ref, image_ref, upper_ref, lower_ref, small_ref, boxes_hbm, routes_hbm, labels_hbm, targets_hbm,
    own_ref, one_ref, two_ref, three_ref, coarse_ref, boxes_ref, routes_ref, labels_ref, targets_ref, sems,
):
    g = pl.program_id(0)
    owner = owner_ref[0]
    rows_valid, cols_valid = valid_edges(owner, image_ref)
    pairs = ((boxes_hbm, boxes_ref), (routes_hbm, routes_ref), (labels_hbm, labels_ref), (targets_hbm, targets_ref))
    copies = [pltpu.make_async_copy(a, b, sems.at[j]) for j, (a, b) in enumerate(pairs)]

    @pl.when(g == 0)
    def _():
        for copy in copies:
            copy.start()

    cell = lax.broadcasted_iota(jnp.int32, (GRID, LANES), 0)
    low = low_half(GRID)
    outs = (own_ref, one_ref, two_ref, three_ref)
    for y in range(upper_ref.shape[2]):
        top = (cell < cols_valid) & (g * upper_ref.shape[2] + y < rows_valid)
        bottom = (cell < cols_valid) & (32 + g * upper_ref.shape[2] + y < rows_valid)
        for c in range(2):
            a = jnp.where(top, upper_ref[0, 0, y, :, pl.ds(LANES * c, LANES)].astype(jnp.float32), 0.0)
            b = jnp.where(bottom, lower_ref[0, 0, y, :, pl.ds(LANES * c, LANES)].astype(jnp.float32), 0.0)
            even = jnp.where(low, a, pltpu.roll(b, 64, 1))
            if c == 0:
                even = jnp.where(owner == 0, even, 0.0)
            outs[2 * c][y] = even.astype(jnp.bfloat16)
            outs[2 * c + 1][y] = jnp.where(low, pltpu.roll(a, 64, 1), b).astype(jnp.bfloat16)

    @pl.when(g == 0)
    def _():
        low = low_half(32)
        cell = lax.broadcasted_iota(jnp.int32, (32, LANES), 0)
        for y in range(16):
            top = (cell < cols_valid) & (y < rows_valid)
            bottom = (cell < cols_valid) & (16 + y < rows_valid) & (owner < 2)
            for c in range(2):
                a = jnp.where(top, small_ref[0, 0, y, pl.ds(0, 32), pl.ds(LANES * c, LANES)].astype(jnp.float32), 0.0)
                b = jnp.where(bottom, small_ref[0, 0, 16 + y, pl.ds(0, 32), pl.ds(LANES * c, LANES)].astype(jnp.float32), 0.0)
                here = pl.ds(32 * y, 32)
                coarse_ref[2 * c, here, :] = jnp.where(low, a, pltpu.roll(b, 64, 1)).astype(jnp.bfloat16)
                coarse_ref[2 * c + 1, here, :] = jnp.where(low, pltpu.roll(a, 64, 1), b).astype(jnp.bfloat16)
        for copy in copies:
            copy.wait()
        note = write_note(boxes_ref, routes_ref, labels_ref, targets_ref, image_ref)
        for d in range(4):
            coarse_ref[d, pl.ds(512, 32), :] = note


def pack(owner, image_size, pyramid, boxes, routes, labels, targets):
    regions = (boxes, routes, labels, targets)
    return pl.pallas_call(
        pack_kernel,
        grid=(4,),
        in_specs=[
            pl.BlockSpec(memory_space=pltpu.SMEM),
            pl.BlockSpec(memory_space=pltpu.SMEM),
            pl.BlockSpec((1, 1, 8, GRID, CHANNELS), lambda g: (0, 0, g, 0, 0)),
            pl.BlockSpec((1, 1, 8, GRID, CHANNELS), lambda g: (0, 0, g + 4, 0, 0)),
            pl.BlockSpec((1, 1, 32, GRID, CHANNELS), lambda g: (0, 0, 0, 0, 0)),
        ]
        + [pl.BlockSpec(memory_space=pltpu.HBM)] * 4,
        out_specs=[pl.BlockSpec((8, GRID, LANES), lambda g: (g, 0, 0))] * 4
        + [pl.BlockSpec((4, 544, LANES), lambda g: (0, 0, 0))],
        scratch_shapes=[pltpu.VMEM(v.shape, v.dtype) for v in regions] + [pltpu.SemaphoreType.DMA((4,))],
        out_shape=[jax.ShapeDtypeStruct((32, GRID, LANES), jnp.bfloat16)] * 4
        + [jax.ShapeDtypeStruct((4, 544, LANES), jnp.bfloat16)],
        cost_estimate=cost(2.7),
        compiler_params=params(8),
    )(owner, in_hbm(image_size), *[in_hbm(pyramid)] * 3, *[in_hbm(v) for v in regions])


def unpack_kernel(owner_ref, image_ref, fine_ref, coarse_ref, out_ref):
    g = pl.program_id(0)
    owner = owner_ref[0]
    rows_valid, cols_valid = valid_edges(owner, image_ref)
    count = out_ref.shape[1]

    @pl.when(owner == 0)
    def _():
        cell = lax.broadcasted_iota(jnp.int32, (GRID, LANES), 0)
        low = low_half(GRID)
        for y in range(count):
            top = (cell < cols_valid) & (g * count + y < rows_valid)
            bottom = (cell < cols_valid) & (32 + g * count + y < rows_valid)
            for c in range(2):
                a = fine_ref[2 * c, pl.ds(y * GRID, GRID), :].astype(jnp.float32)
                b = fine_ref[2 * c + 1, pl.ds(y * GRID, GRID), :].astype(jnp.float32)
                upper = jnp.where(low, a, pltpu.roll(b, 64, 1))
                lower = jnp.where(low, pltpu.roll(a, 64, 1), b)
                out_ref[0, y, :, pl.ds(LANES * c, LANES)] = jnp.where(top, upper, 0.0).astype(jnp.bfloat16)
                out_ref[1, y, :, pl.ds(LANES * c, LANES)] = jnp.where(bottom, lower, 0.0).astype(jnp.bfloat16)

    @pl.when(owner != 0)
    def _():
        out_ref[...] = jnp.zeros_like(out_ref)
        cell = lax.broadcasted_iota(jnp.int32, (32, LANES), 0)
        low = low_half(32)
        for y in range(count):
            top = (cell < cols_valid) & (g * count + y < rows_valid)
            line = pl.ds(pl.multiple_of(((g % 2) * count + y) * 32, 32), 32)
            for c in range(2):
                a = coarse_ref[2 * c, line, :].astype(jnp.float32)
                b = coarse_ref[2 * c + 1, line, :].astype(jnp.float32)
                upper = jnp.where(low, a, pltpu.roll(b, 64, 1))
                lower = jnp.where(low, pltpu.roll(a, 64, 1), b)
                row = jnp.where(g < 2, upper, lower)
                out_ref[0, y, pl.ds(0, 32), pl.ds(LANES * c, LANES)] = jnp.where(top, row, 0.0).astype(jnp.bfloat16)


def unpack(owner, image_size, parts, micros):
    return pl.pallas_call(
        unpack_kernel,
        grid=(4,),
        in_specs=[pl.BlockSpec(memory_space=pltpu.SMEM)] * 2
        + [pl.BlockSpec((4, 512, LANES), lambda g: (0, g, 0)), pl.BlockSpec((4, 512, LANES), lambda g: (0, 0, 0))],
        out_specs=pl.BlockSpec((2, 8, GRID, CHANNELS), lambda g: (0, g, 0, 0)),
        out_shape=jax.ShapeDtypeStruct((2, 32, GRID, CHANNELS), jnp.bfloat16),
        cost_estimate=cost(micros),
        compiler_params=params(7),
    )(owner, image_size, parts, parts)


def to_bins_kernel(order_ref, weight_ref, out_ref, arrived, rows, sems, section):
    del order_ref
    taken = arrived.shape[1]
    blocks = weight_ref.shape[1] // taken

    def fetch(c):
        slot = c % 2
        return pltpu.make_async_copy(weight_ref.at[section, pl.ds(c * taken, taken), :], arrived.at[slot], sems.at[slot])

    fetch(0).start()
    fetch(1).start()

    def step(c, carry):
        fetch(c).wait()
        for t in range(rows.shape[0]):
            rows[t] = arrived[c % 2, :, pl.ds(t * LANES, LANES)].astype(jnp.float32)

        @pl.when(c + 2 < blocks)
        def _():
            fetch(c + 2).start()

        here = pl.ds(pl.multiple_of(c * 16, 16), 16)
        for place, source in enumerate(bin_order()):
            for t in range(rows.shape[0]):
                out_ref[place, here, pl.ds(t * LANES, LANES)] = rows[t, pl.ds(source, 16, stride=49), :].astype(jnp.bfloat16)
        return carry

    lax.fori_loop(0, blocks, step, 0)
    out_ref[49] = jnp.zeros(out_ref.shape[1:], jnp.bfloat16)


def to_bins(order, weight, section, micros):
    rows, width = weight.shape[1:]
    channels = rows // 49
    return pl.pallas_call(
        lambda *refs: to_bins_kernel(*refs, section),
        in_specs=[pl.BlockSpec(memory_space=pltpu.SMEM), pl.BlockSpec(memory_space=pltpu.HBM)],
        out_specs=pl.BlockSpec(memory_space=pltpu.VMEM),
        out_shape=jax.ShapeDtypeStruct((50, channels, width), jnp.bfloat16),
        scratch_shapes=[
            pltpu.VMEM((2, 784, width), jnp.bfloat16),
            pltpu.VMEM((width // LANES, 784, LANES), jnp.float32),
            pltpu.SemaphoreType.DMA((2,)),
        ],
        cost_estimate=cost(micros),
        compiler_params=params(8),
    )(order, in_hbm(weight)).reshape(WIDE, width)


def first_kernel(pooled_ref, weight_ref, out_ref):
    for n in range(0, out_ref.shape[1], 256):
        here = pl.ds(n, 256)
        out_ref[:, here] = jnp.dot(pooled_ref[...], weight_ref[:, here], preferred_element_type=jnp.float32).astype(jnp.bfloat16)


def first_product(pooled, weight, micros):
    vmem = pl.BlockSpec(memory_space=pltpu.VMEM)
    return pl.pallas_call(
        first_kernel,
        in_specs=[vmem, vmem],
        out_specs=vmem,
        out_shape=jax.ShapeDtypeStruct((pooled.shape[0], weight.shape[1]), jnp.bfloat16),
        cost_estimate=cost(micros),
        compiler_params=params(6),
    )(pooled, weight)


def back_kernel(order_ref, grads_ref, weight_ref, out_ref):
    del order_ref
    for n in range(0, WIDE, 640):
        here = pl.ds(n, 640)
        value = lax.dot_general(grads_ref[...], weight_ref[here, :], NT, preferred_element_type=jnp.float32)
        out_ref[:, here] = value.astype(jnp.bfloat16)


def back_product(order, grads, weight, micros):
    vmem = pl.BlockSpec(memory_space=pltpu.VMEM)
    return pl.pallas_call(
        back_kernel,
        in_specs=[pl.BlockSpec(memory_space=pltpu.SMEM), vmem, vmem],
        out_specs=vmem,
        out_shape=jax.ShapeDtypeStruct((grads.shape[0], WIDE), jnp.bfloat16),
        cost_estimate=cost(micros),
        compiler_params=params(6),
    )(order, grads, weight)


SPLIT = 2176
TAIL = WIDE - SPLIT


def outer_kernel(bits_ref, own, cross, own_pooled, cross_pooled, sent_one, kept_one, sent_two, kept_two):
    rows = own.shape[2]

    def product(pick, at, width, out):
        mine, theirs = [pick(ref).reshape(2 * rows, -1) for ref in (own, cross)]
        for n in range(0, width, 256):
            wide = min(256, width - n)
            here = pl.ds(at + n, wide)
            value = jnp.dot(mine, own_pooled[:, here], preferred_element_type=jnp.float32)
            value = value + jnp.dot(theirs, cross_pooled[:, here], preferred_element_type=jnp.float32)
            out[:, :, pl.ds(n, wide)] = value.astype(out.dtype).reshape(2, rows, wide)

    product(lambda ref: ref[:, bits_ref[1]], 0, SPLIT, sent_one)
    product(lambda ref: ref[bits_ref[3]], SPLIT, TAIL, sent_two)
    product(lambda ref: ref[:, bits_ref[0]], 0, SPLIT, kept_one)
    product(lambda ref: ref[bits_ref[2]], SPLIT, TAIL, kept_two)


def outer_sums(bits, own, cross, own_pooled, cross_pooled, micros):
    rows = own.shape[2]
    vmem = pl.BlockSpec(memory_space=pltpu.VMEM)
    kinds = [(width, jnp.bfloat16) for width in (SPLIT, TAIL) for _ in range(2)]
    return pl.pallas_call(
        outer_kernel,
        in_specs=[pl.BlockSpec(memory_space=pltpu.SMEM)] + [vmem] * 4,
        out_specs=[vmem] * 4,
        out_shape=[jax.ShapeDtypeStruct((2, rows, width), dtype) for width, dtype in kinds],
        cost_estimate=cost(micros),
        compiler_params=params(6),
    )(bits, own, cross, own_pooled, cross_pooled)


def fold_kernel(bits_ref, kept_one, arrived_one, kept_two, arrived_two, one_ref, two_ref):
    up, low = bits_ref[3], bits_ref[1]
    one_ref[...] = (kept_one[up].astype(jnp.float32) + arrived_one[up].astype(jnp.float32)).astype(jnp.bfloat16)
    two_ref[...] = (kept_two[low].astype(jnp.float32) + arrived_two[low].astype(jnp.float32)).astype(jnp.bfloat16)


def fold(bits, kept_one, arrived_one, kept_two, arrived_two):
    rows = kept_one.shape[1]
    vmem = pl.BlockSpec(memory_space=pltpu.VMEM)
    return pl.pallas_call(
        fold_kernel,
        in_specs=[pl.BlockSpec(memory_space=pltpu.SMEM)] + [vmem] * 4,
        out_specs=[vmem] * 2,
        out_shape=[jax.ShapeDtypeStruct((rows, SPLIT), jnp.bfloat16), jax.ShapeDtypeStruct((rows, TAIL), jnp.bfloat16)],
        cost_estimate=cost(8),
        compiler_params=params(5),
    )(bits, kept_one, arrived_one, kept_two, arrived_two)


def from_bins_kernel(bits_ref, *refs):
    del bits_ref
    kept_one, arrived_one, last_one, kept_two, arrived_two, last_two = refs[:6]
    out_ref, turned = refs[-2:]
    for kept, arrived, last, at in ((kept_one, arrived_one, last_one, 0), (kept_two, arrived_two, last_two, SPLIT)):
        for t in range(kept.shape[2] // LANES):
            here = pl.ds(t * LANES, LANES)
            value = kept[0, :, here].astype(jnp.float32) + arrived[0, :, here].astype(jnp.float32)
            value = value + last[:, here].astype(jnp.float32)
            turned[pl.ds(at + t * LANES, LANES), :] = jnp.transpose(value, (1, 0))
    for place, source in enumerate(bin_order()):
        out_ref[0, pl.ds(source, 64, stride=49), :] = turned[pl.ds(place * 64, 64), :]


def from_bins(bits, section, kept, arrived, last, before, rows, micros):
    columns = kept[0].shape[1]
    specs = []
    for at, width in ((2, SPLIT), (0, TAIL)):
        both = pl.BlockSpec((1, columns, width), lambda i, b, at=at: (b[at], 0, 0))
        specs += [both, both, pl.BlockSpec((columns, width), lambda i, b: (0, 0))]
    operands = [kept[0], arrived[0], last[0], kept[1], arrived[1], last[1]]
    aliases = {}
    if before is not None:
        specs.append(pl.BlockSpec(memory_space=pl.ANY))
        operands.append(before)
        aliases = {7: 0}
    return pl.pallas_call(
        from_bins_kernel,
        grid_spec=pltpu.PrefetchScalarGridSpec(
            num_scalar_prefetch=1,
            grid=(1,),
            in_specs=specs,
            out_specs=pl.BlockSpec((1, rows, columns), lambda i, b: (section, 0, 0)),
            scratch_shapes=[pltpu.VMEM((WIDE, LANES), jnp.float32)],
        ),
        out_shape=jax.ShapeDtypeStruct((2, rows, columns), jnp.float32),
        input_output_aliases=aliases,
        cost_estimate=cost(micros),
        compiler_params=params(6),
    )(bits, *operands)


def silu_slope(values):
    sigma = jax.nn.sigmoid(values)
    return sigma * (1.0 + values * (1.0 - sigma))


NT = (((1,), (1,)), ((), ()))
TN = (((0,), (0,)), ((), ()))
OUTER = 128


def write_sums(sums, width):
    high = sums.astype(jnp.bfloat16).astype(jnp.float32)
    rows = []
    for part in (high, sums - high):
        rest = part[:, width:]
        if rest.shape[1] < width:
            rest = jnp.concatenate([rest, jnp.zeros((1, width - rest.shape[1]), jnp.float32)], axis=1)
        rows += [part[:, :width], rest]
    return jnp.concatenate(rows + [jnp.zeros((EXTRA - 4, width), jnp.float32)], axis=0).astype(jnp.bfloat16)


def read_sums(note, count):
    note = note.astype(jnp.float32)
    rows = note[0:2] + note[2:4]
    return jnp.concatenate([rows[0:1], rows[1:2]], axis=1)[:, :count]


def head_kernel(
    me_ref, mine_ref, theirs_ref, info_ref, feature_bias_ref, hidden_ref, hidden_bias_ref, class_ref, class_bias_ref,
    delta_ref, delta_bias_ref,
    *refs, images,
):
    logits_ref, deltas_ref, small_ref, small_away_ref, grad_feature_ref, stay_ref, away_ref = refs[-12:-5]
    outer_scr, turned_scr, weight_scr, row_scr, small_scr = refs[-5:]
    me, half = me_ref[0], me_ref[1]
    weight_scr[...] = jnp.zeros_like(weight_scr)
    weight_scr[pl.ds(0, CLASSES), :] = class_ref[0]
    weight_scr[pl.ds(OUTER, DELTAS), :] = delta_ref[0]
    row_scr[...] = jnp.zeros_like(row_scr)
    row_scr[:, pl.ds(0, CLASSES)] = class_bias_ref[0]
    row_scr[:, pl.ds(OUTER, DELTAS)] = delta_bias_ref[0]
    f32 = jnp.float32
    rows, hidden = mine_ref.shape
    pre_feature = mine_ref[...].astype(f32) + theirs_ref[...].astype(f32) + feature_bias_ref[0]
    gate_one = jax.nn.sigmoid(pre_feature)
    hidden_one = (pre_feature * gate_one).astype(jnp.bfloat16)
    pre_hidden = jnp.dot(hidden_one, hidden_ref[0], preferred_element_type=f32) + hidden_bias_ref[0]
    gate_two = jax.nn.sigmoid(pre_hidden)
    hidden_two = (pre_hidden * gate_two).astype(jnp.bfloat16)
    outer = lax.dot_general(hidden_two, weight_scr[...], NT, preferred_element_type=f32) + row_scr[...]
    outer_scr[...] = outer
    own = pl.ds(pl.multiple_of(me * (rows // 4), rows // 4), rows // 4)
    logits_ref[0] = outer_scr[own, pl.ds(0, CLASSES)]
    deltas_ref[0] = outer_scr[own, pl.ds(OUTER, DELTAS)]

    columns = jnp.transpose(info_ref[0], (1, 0))
    label = columns[:, 5:6].astype(jnp.int32)
    lane = lax.broadcasted_iota(jnp.int32, (rows, OUTER), 1)
    logits = jnp.where(lane < CLASSES, outer[:, :OUTER], -jnp.inf)
    shifted = jnp.exp(logits - jnp.max(logits, axis=1, keepdims=True))
    grad_logits = shifted / jnp.sum(shifted, axis=1, keepdims=True) - (lane == label).astype(f32)
    wide = lax.broadcasted_iota(jnp.int32, (rows, outer.shape[1] - OUTER), 1)
    hot = (wide // 4 == label) & (label < CLASSES - 1)
    picked = jnp.where(hot, outer[:, OUTER:], 0.0)
    grad_deltas = jnp.zeros_like(picked)
    for j in range(4):
        mine = wide % 4 == j
        chosen = jnp.sum(jnp.where(mine, picked, 0.0), axis=1, keepdims=True)
        error = jnp.clip(chosen - columns[:, 6 + j : 7 + j], -1.0, 1.0)
        grad_deltas = jnp.where(mine & hot, error, grad_deltas)
    grad_outer = jnp.concatenate([grad_logits, grad_deltas], axis=1).astype(jnp.bfloat16)

    grad_two = jnp.dot(grad_outer, weight_scr[...], preferred_element_type=f32)
    slope_two = gate_two * (1.0 + pre_hidden * (1.0 - gate_two))
    grad_pre_hidden = (grad_two * slope_two).astype(jnp.bfloat16)
    grad_one = lax.dot_general(grad_pre_hidden, hidden_ref[0], NT, preferred_element_type=f32)
    slope_one = gate_one * (1.0 + pre_feature * (1.0 - gate_one))
    grad_feature = grad_one * slope_one
    grad_pre_feature = grad_feature.astype(jnp.bfloat16)
    grad_feature_ref[...] = grad_pre_feature
    turned_scr[...] = jnp.transpose(grad_feature, (1, 0)).astype(jnp.bfloat16)
    stay_ref[...] = turned_scr[pl.ds(pl.multiple_of(half * (hidden // 2), hidden // 2), hidden // 2), :]
    away_ref[...] = turned_scr[pl.ds(pl.multiple_of((1 - half) * (hidden // 2), hidden // 2), hidden // 2), :]

    run = hidden // (4 * images)
    row = lax.broadcasted_iota(jnp.int32, (hidden, hidden // 4), 0)
    col = lax.broadcasted_iota(jnp.int32, (hidden, hidden // 4), 1)
    pick = (row == (col // run) * (4 * run) + me * run + col % run).astype(jnp.bfloat16)
    one_rows = jnp.dot(hidden_one, pick, preferred_element_type=f32).astype(jnp.bfloat16)
    two_rows = jnp.dot(hidden_two, pick, preferred_element_type=f32).astype(jnp.bfloat16)
    small_scr[:, pl.ds(0, hidden)] = lax.dot_general(one_rows, grad_pre_hidden, TN, preferred_element_type=f32).astype(jnp.bfloat16)
    small_scr[:, pl.ds(hidden, outer.shape[1])] = lax.dot_general(two_rows, grad_outer, TN, preferred_element_type=f32).astype(jnp.bfloat16)
    middle = me_ref[2]
    part = small_scr.shape[0] // 2
    if images == 8:
        for j in range(images // 2):
            here = pl.ds(j * run, run)
            for bit, ref in ((middle, small_ref), (1 - middle, small_away_ref)):
                source = (j // 2) * 4 * run + bit * 2 * run + (j % 2) * run
                ref[0, here, :] = small_scr[pl.ds(pl.multiple_of(source, run), run), :]
    else:
        small_ref[0, pl.ds(0, part), :] = small_scr[pl.ds(0, part), :]
        small_away_ref[0, pl.ds(0, part), :] = small_scr[pl.ds(part, part), :]
    sums = [jnp.sum(v.astype(f32), axis=0, keepdims=True) for v in (grad_pre_feature, grad_pre_hidden, grad_outer)]
    sums = jnp.concatenate(sums, axis=1)
    note = write_sums(sums, small_scr.shape[1])
    for ref in (small_ref, small_away_ref):
        ref[0, pl.ds(ref.shape[1] - EXTRA, EXTRA), :] = note


def head(me, mine, theirs, section, stacked, images, before, micros):
    rows, hidden = mine.shape
    width = 512
    sections = stacked[0].shape[0]

    def whole(shape):
        return pl.BlockSpec(shape, lambda g, m: (0,) * len(shape))

    def of_section(array):
        return pl.BlockSpec((1,) + array.shape[1:], lambda g, m: (section, 0, 0))

    def kernel(*refs):
        head_kernel(*refs, images=images)

    shared = [
        jax.ShapeDtypeStruct((sections, rows // 4, CLASSES), jnp.float32),
        jax.ShapeDtypeStruct((sections, rows // 4, DELTAS), jnp.float32),
    ]
    single = [
        jax.ShapeDtypeStruct((1, hidden // 8 + EXTRA, hidden + width), jnp.bfloat16),
        jax.ShapeDtypeStruct((1, hidden // 8 + EXTRA, hidden + width), jnp.bfloat16),
        jax.ShapeDtypeStruct((rows, hidden), jnp.bfloat16),
        jax.ShapeDtypeStruct((hidden // 2, rows), jnp.bfloat16),
        jax.ShapeDtypeStruct((hidden // 2, rows), jnp.bfloat16),
    ]
    return pl.pallas_call(
        kernel,
        grid_spec=pltpu.PrefetchScalarGridSpec(
            num_scalar_prefetch=1,
            grid=(1,),
            in_specs=[whole(mine.shape), whole(theirs.shape)]
            + [of_section(a) for a in stacked]
            + [pl.BlockSpec(memory_space=pl.ANY)] * len(before),
            out_specs=[of_section(o) for o in shared] + [whole(o.shape) for o in single],
            scratch_shapes=[
                pltpu.VMEM((rows, width), jnp.float32),
                pltpu.VMEM((hidden, rows), jnp.bfloat16),
                pltpu.VMEM((width, hidden), jnp.bfloat16),
                pltpu.VMEM((1, width), jnp.float32),
                pltpu.VMEM((hidden // 4, hidden + width), jnp.bfloat16),
            ],
        ),
        out_shape=shared + single,
        input_output_aliases={3 + len(stacked) + j: j for j in range(len(before))},
        cost_estimate=cost(micros),
        compiler_params=params(13),
    )(me, mine, theirs, *stacked, *before)


def pass_sums(s, kept_ref, arrived_ref, refs):
    rows, width = kept_ref.shape[1:]
    notes = [ref[s, pl.ds(rows - EXTRA, EXTRA), :] for ref in (kept_ref, arrived_ref)]
    total = write_sums(read_sums(notes[0], 2 * width) + read_sums(notes[1], 2 * width), width)
    for ref in refs:
        ref[s, pl.ds(ref.shape[1] - EXTRA, EXTRA), :] = total


def small_step_kernel(bits_ref, kept_ref, arrived_ref, stay_ref, away_ref, at):
    sections, rows, width = kept_ref.shape
    run = 32
    for s in range(sections):
        for j in range((rows - EXTRA) // (2 * run)):
            for place, ref in ((bits_ref[at], stay_ref), (bits_ref[at + 1], away_ref)):
                here = pl.ds(pl.multiple_of(j * 2 * run + place * run, run), run)
                value = kept_ref[s, here, :].astype(jnp.float32) + arrived_ref[s, here, :].astype(jnp.float32)
                ref[s, pl.ds(j * run, run), :] = value.astype(jnp.bfloat16)
        pass_sums(s, kept_ref, arrived_ref, (stay_ref, away_ref))


def small_last_kernel(order_ref, kept_ref, arrived_ref, hidden_ref, class_ref, delta_ref, one_ref, two_ref, class_sum_ref, delta_sum_ref):
    del order_ref
    run, hidden = hidden_ref.shape[1:]
    width = kept_ref.shape[2]
    for s in range(kept_ref.shape[0]):
        value = kept_ref[s, pl.ds(0, run), :].astype(jnp.float32) + arrived_ref[s, pl.ds(0, run), :].astype(jnp.float32)
        hidden_ref[s] = value[:, :hidden]
        class_ref[s] = value[:, hidden : hidden + CLASSES]
        delta_ref[s] = value[:, hidden + OUTER : hidden + OUTER + DELTAS]
        sums = read_sums(kept_ref[s, pl.ds(run, EXTRA), :], 2 * width) + read_sums(arrived_ref[s, pl.ds(run, EXTRA), :], 2 * width)
        at = 0
        for ref, step in ((one_ref, hidden), (two_ref, hidden), (class_sum_ref, OUTER), (delta_sum_ref, DELTAS)):
            ref[s : s + 1, :] = sums[:, at : at + ref.shape[1]]
            at += step


def small_join_kernel(bits_ref, *refs):
    outs = refs[4:]
    rows = refs[0].shape[1]
    run = 32
    for s in range(2):
        kept_ref, arrived_ref = refs[s], refs[2 + s]
        count = (rows - EXTRA) // (2 * run)
        for j in range(count):
            for place, ref in ((bits_ref[4], outs[0]), (bits_ref[5], outs[1])):
                here = pl.ds(pl.multiple_of(place * count * run + j * run, run), run)
                value = kept_ref[0, here, :].astype(jnp.float32) + arrived_ref[0, here, :].astype(jnp.float32)
                ref[s, pl.ds(j * run, run), :] = value.astype(jnp.bfloat16)
        notes = [ref[0, pl.ds(rows - EXTRA, EXTRA), :] for ref in (kept_ref, arrived_ref)]
        width = kept_ref.shape[2]
        total = write_sums(read_sums(notes[0], 2 * width) + read_sums(notes[1], 2 * width), width)
        for ref in outs:
            ref[s, pl.ds(ref.shape[1] - EXTRA, EXTRA), :] = total


def small_join(bits, kept, arrived):
    vmem = pl.BlockSpec(memory_space=pltpu.VMEM)
    _, rows, width = kept[0].shape
    return pl.pallas_call(
        small_join_kernel,
        in_specs=[pl.BlockSpec(memory_space=pltpu.SMEM)] + [vmem] * 4,
        out_specs=[vmem] * 2,
        out_shape=[jax.ShapeDtypeStruct((2, (rows - EXTRA) // 2 + EXTRA, width), jnp.bfloat16)] * 2,
        cost_estimate=cost(1),
        compiler_params=params(8),
    )(bits, *kept, *arrived)


def small_step(bits, at, kept, arrived):
    vmem = pl.BlockSpec(memory_space=pltpu.VMEM)
    sections, rows, width = kept.shape
    return pl.pallas_call(
        lambda *refs: small_step_kernel(*refs, at),
        in_specs=[pl.BlockSpec(memory_space=pltpu.SMEM), vmem, vmem],
        out_specs=[vmem] * 2,
        out_shape=[jax.ShapeDtypeStruct((sections, (rows - EXTRA) // 2 + EXTRA, width), jnp.bfloat16)] * 2,
        cost_estimate=cost(1),
        compiler_params=params(8),
    )(bits, kept, arrived)


def small_last(order, kept, arrived, hidden):
    sections, rows, width = kept.shape
    shapes = [(sections, rows - EXTRA, n) for n in (hidden, CLASSES, DELTAS)]
    shapes += [(sections, n) for n in (hidden, hidden, CLASSES, DELTAS)]
    vmem = pl.BlockSpec(memory_space=pltpu.VMEM)
    return pl.pallas_call(
        small_last_kernel,
        in_specs=[pl.BlockSpec(memory_space=pltpu.SMEM), vmem, vmem],
        out_shape=[jax.ShapeDtypeStruct(shape, jnp.float32) for shape in shapes],
        cost_estimate=cost(1),
        compiler_params=params(8),
    )(order, kept, arrived)


def swap(value, axis, bit):
    size = lax.axis_size(axis)
    return lax.ppermute(value, axis, [(i, i ^ bit) for i in range(size)])


def after(value, *others):
    return lax.optimization_barrier((value,) + others)[0]


def choose(array, axis, bit):
    return lax.dynamic_index_in_dim(array, bit, axis, keepdims=False)


def split_bits(array, bits):
    return array.reshape((2,) * bits + (array.shape[0] >> bits,) + array.shape[1:])


def body(
    pyramid,
    image_size,
    region_boxes,
    routes,
    labels,
    targets,
    feature_weight,
    feature_bias,
    hidden_weight,
    hidden_bias,
    class_weight,
    class_bias,
    delta_weight,
    delta_bias,
):
    images = lax.axis_size("img")
    me = lax.axis_index("lvl").astype(jnp.int32)
    image = lax.axis_index("img").astype(jnp.int32)
    sections = routes.shape[0]
    features = feature_weight.shape[1]
    hidden = hidden_weight.shape[2]
    top = images // 2
    steps = images.bit_length() - 2
    half = jnp.minimum(image & top, 1)
    own_bits = [jnp.minimum(image & (1 << b), 1) for b in range(steps)]
    me_list = jnp.stack([me, half, jnp.minimum(image & 2, 1)])

    own, *quarters, small = pack(me_list, image_size, pyramid, region_boxes, routes, labels, targets)
    arrived = [lax.ppermute(quarters[d], "lvl", [(0, d + 1)]) for d in (1, 2, 0)]
    coarse = lax.all_to_all(small, "lvl", split_axis=0, concat_axis=0, tiled=True)
    weight_a = to_bins(me_list, feature_weight, 0, 10)
    if CROSS == "permute":
        slot = jnp.zeros((1,), jnp.int32)
        levels, info, table = arrange(after(slot, weight_a), 1, own, arrived, coarse)
        cross_levels = swap(levels, "img", top)
    else:
        slot = jnp.reshape(1 - half, (1,))
        pairs = [[i, i + top] for i in range(top)]
        levels, info, table = arrange(after(slot, weight_a), 2, own, arrived, coarse)
        cross_levels = lax.all_to_all(levels, "img", split_axis=0, concat_axis=0, tiled=True, axis_index_groups=pairs)

    stacked = (
        info, feature_bias[:, None], hidden_weight, hidden_bias[:, None], jnp.swapaxes(class_weight, 1, 2),
        class_bias[:, None], jnp.swapaxes(delta_weight, 1, 2), delta_bias[:, None],
    )

    def run_head(s, parts, before, ready, micros):
        results = head(after(me_list, *ready), *parts, s, stacked, images, before, micros)
        shared, small, (grads, stay, away) = results[:2], results[2:4], results[4:]
        return shared, small, grads, stay, swap(away, "img", top)

    def add(first, second):
        return (first.astype(jnp.float32) + second.astype(jnp.float32)).astype(jnp.bfloat16)

    pooled_a = crop(slot, table, 0, levels, 12)
    part_a = first_product(pooled_a, weight_a, 1)
    weight_b = to_bins(after(me_list, part_a), feature_weight, 1, 8)
    chip_a = add(part_a, swap(part_a, "lvl", 1))
    pooled_b = crop(slot, after(table, weight_b, chip_a), 1, levels, 8)
    part_b = first_product(pooled_b, weight_b, 0)
    shared, small_a, grads_a, stay_a, cross_a = run_head(0, (chip_a, swap(chip_a, "lvl", 2)), (), [part_b], 0)
    part_b = after(part_b, grads_a)
    theirs_b = swap(part_b, "lvl", 1)
    cross_table = prepare(after(slot, grads_a), cross_levels)
    chip_b = add(after(part_b, cross_table), theirs_b)
    far_a = crop(slot, after(cross_table, chip_b), 0, cross_levels, 8)
    parts_b = (chip_b, swap(chip_b, "lvl", 2))
    if images == 8:
        bits = jnp.stack([own_bits[0], 1 - own_bits[0], own_bits[1], 1 - own_bits[1], half, 1 - half])

        def weight_sums(stay, cross, pooled, far, ready):
            pieces = [v.reshape(2, 2, hidden // images, -1) for v in (stay, cross)]
            sent_one, kept_one, sent_two, kept_two = outer_sums(after(bits, *ready), *pieces, pooled, far, 0)
            return (kept_one, kept_two), (swap(sent_one, "img", 1), swap(sent_two, "img", 2))

        def second_step(kept, arrived, ready):
            one, two = fold(after(bits, *ready), kept[0], arrived[0], kept[1], arrived[1])
            return one, (swap(one, "img", 2), swap(two, "img", 1))

        small_near_a = swap(small_a[1], "img", 2)
        kept_a, arrived_a = weight_sums(stay_a, cross_a, pooled_a, far_a, [])
        shared, small_b, grads_b, stay_b, cross_b = run_head(1, parts_b, shared, [kept_a[0]], 0)
        small_near_b = swap(small_b[1], "img", 2)
        far_b = crop(slot, after(cross_table, grads_b, small_near_a), 1, cross_levels, 10)
        folded, last_a = second_step(kept_a, arrived_a, [far_b])
        kept_b, arrived_b = weight_sums(stay_b, cross_b, pooled_b, far_b, [folded])
        slots_a = back_product(after(me_list, kept_b[0]), grads_a, weight_a, 10)
        small, away = small_join(after(bits, slots_a), (small_a[0], small_b[0]), (small_near_a, small_near_b))
        arrived_small = swap(away, "img", 4)
        slots_b = back_product(after(me_list, away), grads_b, weight_b, 0)
        spread_out = spread(table, slots_a, slots_b, 0)
        small, away = small_step(after(bits, spread_out), 0, small, arrived_small)
        arrived_small = swap(away, "img", 1)
        folded, last_b = second_step(kept_b, arrived_b, [away, *last_a])
    else:
        shared, small_b, grads_b, stay_b, cross_b = run_head(1, parts_b, shared, [far_a], 0)
        slots_a = back_product(me_list, grads_a, weight_a, 8)
        slots_b = back_product(me_list, grads_b, weight_b, 5)
        spread_out = spread(table, slots_a, slots_b, 20)
        far_b = crop(slot, cross_table, 1, cross_levels, 10)
        totals = []
        for stay, cross, pooled, far in ((stay_a, cross_a, pooled_a, far_a), (stay_b, cross_b, pooled_b, far_b)):
            total = jnp.dot(stay, pooled, preferred_element_type=jnp.float32)
            total = total + jnp.dot(cross, far, preferred_element_type=jnp.float32)
            for b in range(steps)[::-1]:
                halves = split_bits(total, 1)
                away = choose(halves, 0, 1 - own_bits[b]).astype(jnp.bfloat16)
                total = choose(halves, 0, own_bits[b]) + swap(away, "img", 1 << b).astype(jnp.float32)
            totals.append(total[:, :features])
        order = bin_order()
        back = jnp.array([order.index(j) for j in range(49)])
        total = jnp.stack(totals)
        total = total.reshape(sections, total.shape[1], 49, features // 49)[:, :, back]
        feature_weight_grad = total.transpose(0, 3, 2, 1).reshape(sections, features, -1)

    parts = lax.all_to_all(spread_out, "lvl", split_axis=0, concat_axis=0, tiled=True)
    logits, deltas = shared
    if images == 8:
        feature_weight_grad = from_bins(after(bits, folded), 0, kept_a, arrived_a, last_a, None, features, 8)
        small = small_last(after(me_list, feature_weight_grad), small, arrived_small, hidden)
        sums = small[3:]
        feature_weight_grad = from_bins(after(bits, small[0]), 1, kept_b, arrived_b, last_b, feature_weight_grad, features, 8)
        me_list = after(me_list, feature_weight_grad)
    pyramid_grad = unpack(me_list, image_size, parts, 0)
    pyramid_grad = pyramid_grad.reshape(1, 1, GRID, GRID, CHANNELS)

    if images != 8:
        small, small_away = [jnp.concatenate([a, b], axis=0) for a, b in zip(small_a, small_b)]
        notes = small[:, hidden // 8 :].astype(jnp.float32)
        sums = (notes[:, 0:2] + notes[:, 2:4]).reshape(sections, -1)
        sums = lax.psum(sums, "img")
        small = jnp.concatenate([small[:, : hidden // 8], small_away[:, : hidden // 8]], axis=1)
        small = lax.psum_scatter(small, "img", scatter_dimension=1, tiled=True).astype(jnp.float32)
        small = (small[:, :, :hidden], small[:, :, hidden : hidden + CLASSES], small[:, :, hidden + OUTER : hidden + OUTER + DELTAS])
        at = 2 * hidden
        sums = (sums[:, :hidden], sums[:, hidden:at], sums[:, at : at + CLASSES], sums[:, at + OUTER : at + OUTER + DELTAS])
    return (
        logits,
        deltas,
        pyramid_grad,
        feature_weight_grad,
        sums[0],
        small[0],
        sums[1],
        small[1],
        sums[2],
        small[2],
        sums[3],
    )


def solution(mesh):
    return jax.shard_map(
        body,
        mesh=mesh,
        in_specs=(
            P("img", "lvl", None, None, None),
            P("img", None),
            P(None, None, ("img", "lvl")),
            P(None, ("img", "lvl")),
            P(None, ("img", "lvl")),
            P(None, None, ("img", "lvl")),
            P(None, "lvl", None),
            P(),
            P(),
            P(),
            P(),
            P(),
            P(),
            P(),
        ),
        out_specs=(
            P(None, ("img", "lvl"), None),
            P(None, ("img", "lvl"), None),
            P("img", "lvl", None, None, None),
            P(None, "lvl", "img"),
            P(),
            P(None, ("img", "lvl"), None),
            P(),
            P(None, ("img", "lvl"), None),
            P(),
            P(None, ("img", "lvl"), None),
            P(),
        ),
        check_vma=False,
    )
```

```python
import jax
import jax.numpy as jnp
from jax import lax
from jax.experimental import pallas as pl
from jax.experimental.pallas import tpu as pltpu
from jax.sharding import PartitionSpec as P

CHANNELS = 256
CLASSES = 81
POOL = 7
GRID = 64
DELTAS = 320

WIDTH = 80
ROWS = 140
BASES = (1, 66, 99, 116)
CELLS = ROWS * WIDTH
LANES = 128
WIDE = 3200
EXTRA = 16
FINE = 2048
NOTES = FINE + 3 * 512
BUFFER = NOTES + 4 * 32
UNROLL = 64


def cost(microseconds):
    return pl.CostEstimate(flops=int(microseconds * SCALE * 1_150_000_000), bytes_accessed=0, transcendentals=0)


def in_hbm(array):
    return pltpu.with_memory_space_constraint(array, pltpu.HBM)


def params(mebibytes):
    return pltpu.CompilerParams(vmem_limit_bytes=mebibytes << 20)


SCALE = 1.0


def low_half(rows):
    return lax.broadcasted_iota(jnp.int32, (rows, LANES), 1) < 64


def tent(position, step, cell):
    first = jnp.maximum(1.0 - jnp.abs(position - cell), 0.0)
    second = jnp.maximum(1.0 - jnp.abs(position + step - cell), 0.0)
    return ((first + second) * 0.5).astype(jnp.bfloat16).astype(jnp.float32)


def place_rows(maps, upper, lower, upper_row, lower_row, cells):
    low = low_half(8)
    tiles = cells // 8
    zero = jnp.zeros((8, LANES), jnp.float32)
    values = [upper[8 * t : 8 * t + 8] for t in range(tiles)]
    turned = [pltpu.roll(v, 64, 1) for v in values]
    for t in range(-1, tiles):
        here, here_turned = (values[t], turned[t]) if t >= 0 else (zero, zero)
        after, after_turned = (values[t + 1], turned[t + 1]) if t + 1 < tiles else (zero, zero)
        maps[pl.ds(upper_row * WIDTH + 8 + 8 * t, 8), :] = jnp.where(low, here, after_turned)
        maps[pl.ds(lower_row * WIDTH + 8 + 8 * t, 8), :] = jnp.where(low, here_turned, after)


def fill_maps(maps, levels_ref):
    zero = jnp.zeros((8, LANES), jnp.float32)
    for row in (0, BASES[1] - 1):
        for t in range(WIDTH // 8):
            maps[pl.ds(row * WIDTH + 8 * t, 8), :] = zero

    def clear_edge(y, carry):
        maps[pl.ds(pl.multiple_of((BASES[0] + y) * WIDTH + WIDTH - 8, 8), 8), :] = zero
        return carry

    lax.fori_loop(0, GRID, clear_edge, 0, unroll=8)

    def clear(t, carry):
        maps[pl.ds(pl.multiple_of(BASES[1] * WIDTH + t * 160, 160), 160), :] = jnp.zeros((160, LANES), jnp.float32)
        return carry

    lax.fori_loop(0, (ROWS - BASES[1]) * WIDTH // 160, clear, 0, unroll=2)

    def fine_row(y, carry):
        row = levels_ref[0, pl.ds(pl.multiple_of(y * 64, 64), 64), :].astype(jnp.float32)
        place_rows(maps, row, row, BASES[0] + y, BASES[0] + 32 + y, 64)
        return carry

    lax.fori_loop(0, 32, fine_row, 0, unroll=4)
    for level, cells in ((1, 32), (2, 16), (3, 8)):
        for y in range(cells // 2 if level == 1 else cells):
            row = levels_ref[0, pl.ds(FINE + (level - 1) * 512 + y * 32, 32), :].astype(jnp.float32)[:cells]
            if level == 1:
                place_rows(maps, row, row, BASES[1] + y, BASES[1] + 16 + y, 32)
            else:
                place_upper(maps, row, BASES[level] + y, cells)


def place_upper(maps, row, at, cells):
    low = low_half(8)
    tiles = cells // 8
    zero = jnp.zeros((8, LANES), jnp.float32)
    values = [row[8 * t : 8 * t + 8] for t in range(tiles)]
    for t in range(-1, tiles):
        here = values[t] if t >= 0 else zero
        after = pltpu.roll(values[t + 1], 64, 1) if t + 1 < tiles else zero
        maps[pl.ds(at * WIDTH + 8 + 8 * t, 8), :] = jnp.where(low, here, after)


def crop_kernel(table_ref, levels_ref, out_ref, slab, maps, section):
    rb = out_ref.shape[0]
    base = pl.program_id(0) * rb

    @pl.when(pl.program_id(0) == 0)
    def _():
        fill_maps(maps, levels_ref)

    low = low_half(8)
    lane = lax.broadcasted_iota(jnp.int32, (8, LANES), 1)
    bins = (2 * lax.broadcasted_iota(jnp.int32, (8, LANES), 0)).astype(jnp.float32)
    lane_y = (lane // 8).astype(jnp.float32)
    lane_x = (lane % 8).astype(jnp.float32)

    def one(r):
        start = table_ref[section, 0, base + r].astype(jnp.int32)
        y_at, y_step, x_at, x_step = [table_ref[section, 1 + j, base + r] for j in range(4)]
        window = jnp.concatenate([maps[pl.ds(start + WIDTH * j, 8), :] for j in range(16)], axis=0)
        wy = tent(y_at + y_step * bins, y_step, lane_y)
        x_position = x_at + x_step * bins
        wx = [tent(x_position, x_step, lane_x + 8.0 * h) for h in range(2)]
        rows = [jnp.broadcast_to(wy[b : b + 1], (8, LANES)) for b in range(POOL)]
        weight = jnp.concatenate([rows[b] * wx[h] for h in range(2) for b in range(POOL)], axis=0)
        both = jnp.dot(weight.astype(jnp.bfloat16), window.astype(jnp.bfloat16), preferred_element_type=jnp.float32)
        near = [both[8 * b : 8 * b + 8] for b in range(POOL)]
        far = [both[56 + 8 * b : 64 + 8 * b] for b in range(POOL)]
        zero = jnp.zeros((8, LANES), jnp.float32)
        for i in range(4):
            near_odd, far_odd = (near[2 * i + 1], far[2 * i + 1]) if i < 3 else (zero, zero)
            pair = jnp.where(low, near[2 * i], far_odd) + pltpu.roll(jnp.where(low, near_odd, far[2 * i]), 64, 1)
            slab[pl.ds(i * 8 * rb + r, 8, stride=rb), :] = pair

    def step(t, carry):
        for u in range(UNROLL):
            one(t * UNROLL + u)
        return carry

    lax.fori_loop(0, rb // UNROLL, step, 0)
    for i in range(3):
        for e in range(POOL):
            out_ref[:, pl.ds((7 * i + e) * LANES, LANES)] = slab[pl.ds((8 * i + e) * rb, rb), :].astype(jnp.bfloat16)
    for j in range(4):
        first = slab[pl.ds((24 + 2 * j) * rb, rb), :]
        if j < 3:
            second = slab[pl.ds((25 + 2 * j) * rb, rb), :]
            joined = jnp.where(low_half(rb), first, pltpu.roll(second, 64, 1))
            out_ref[:, pl.ds((21 + j) * LANES, LANES)] = joined.astype(jnp.bfloat16)
        else:
            out_ref[:, pl.ds(24 * LANES, LANES)] = jnp.where(low_half(rb), first, 0.0).astype(jnp.bfloat16)


def crop(table, section, levels, micros, block=64):
    count = table.shape[2]
    return pl.pallas_call(
        lambda *refs: crop_kernel(*refs, section),
        grid=(count // block,),
        in_specs=[pl.BlockSpec(memory_space=pltpu.SMEM), pl.BlockSpec(memory_space=pltpu.VMEM)],
        out_specs=pl.BlockSpec((block, WIDE), lambda g: (g, 0)),
        scratch_shapes=[pltpu.VMEM((32 * block, LANES), jnp.float32), pltpu.VMEM((CELLS, LANES), jnp.float32)],
        out_shape=jax.ShapeDtypeStruct((count, WIDE), jnp.bfloat16),
        cost_estimate=cost(micros),
        compiler_params=params(11),
    )(table, levels)


def spread_kernel(table_ref, first_ref, second_ref, out_ref, slab, sums, fine, coarse, sems):
    rb = slab.shape[0] // 32
    steps = pl.num_programs(0) // 2
    section = pl.program_id(0) // steps
    base = (pl.program_id(0) % steps) * rb

    @pl.when(pl.program_id(0) == 0)
    def _():
        def clear(t, carry):
            sums[pl.ds(pl.multiple_of(t * 160, 160), 160), :] = jnp.zeros((160, LANES), jnp.float32)
            return carry

        lax.fori_loop(0, CELLS // 160, clear, 0, unroll=2)
        for i in range(4):
            slab[pl.ds((8 * i + 7) * rb, rb), :] = jnp.zeros((rb, LANES), jnp.float32)

    def lay_out(grads):
        grads_ref = grads.at[pl.ds(pl.multiple_of(base, rb), rb), :]
        for i in range(3):
            for e in range(POOL):
                slab[pl.ds((8 * i + e) * rb, rb), :] = grads_ref[:, pl.ds((7 * i + e) * LANES, LANES)].astype(jnp.float32)
        for j in range(4):
            pair = grads_ref[:, pl.ds((21 + j) * LANES, LANES)].astype(jnp.float32)
            slab[pl.ds((24 + 2 * j) * rb, rb), :] = pair
            if j < 3:
                slab[pl.ds((25 + 2 * j) * rb, rb), :] = pltpu.roll(pair, 64, 1)

    @pl.when(section == 0)
    def _():
        lay_out(first_ref)

    @pl.when(section == 1)
    def _():
        lay_out(second_ref)

    low = low_half(8)
    lane = lax.broadcasted_iota(jnp.int32, (8, LANES), 1)
    row = lax.broadcasted_iota(jnp.int32, (8, LANES), 0).astype(jnp.float32)
    bins_y = (2 * ((lane // 8) % 8)).astype(jnp.float32)
    bins_x = (2 * (lane % 8)).astype(jnp.float32)
    cell_x = row + 8.0 * (lane // 64).astype(jnp.float32)

    def one(r):
        start = table_ref[section, 0, base + r].astype(jnp.int32)
        y_at, y_step, x_at, x_step = [table_ref[section, 1 + j, base + r] for j in range(4)]
        y_position = y_at + y_step * bins_y
        wy = [tent(y_position, y_step, row + 8.0 * h) for h in range(2)]
        wx = tent(x_at + x_step * bins_x, x_step, cell_x)
        rows = [jnp.broadcast_to(wy[y // 8][y % 8 : y % 8 + 1], (8, LANES)) for y in range(16)]
        weight = jnp.concatenate([rows[y] * wx for y in range(16)], axis=0)
        near, far = [], []
        for i in range(4):
            pair = slab[pl.ds(i * 8 * rb + r, 8, stride=rb), :]
            turned = pltpu.roll(pair, 64, 1)
            zero = jnp.zeros_like(pair)
            near.append(jnp.where(low, pair, zero))
            far.append(jnp.where(low, zero, turned))
            near.append(jnp.where(low, turned, zero) if i < 3 else zero)
            far.append(jnp.where(low, zero, pair) if i < 3 else zero)
        grads = jnp.concatenate(near + far, axis=0)
        out = jnp.dot(weight.astype(jnp.bfloat16), grads.astype(jnp.bfloat16), preferred_element_type=jnp.float32)
        for j in range(16):
            sums[pl.ds(start + WIDTH * j, 8), :] += out[8 * j : 8 * j + 8]

    def step(t, carry):
        for u in range(UNROLL):
            one(t * UNROLL + u)
        return carry

    lax.fori_loop(0, rb // UNROLL, step, 0)

    @pl.when(pl.program_id(0) == pl.num_programs(0) - 1)
    def _():
        def gather(upper_row, lower_row, cells):
            tiles = []
            for t in range(cells // 8):
                up, up_far = [sums[pl.ds(upper_row * WIDTH + 8 * t + s, 8), :] for s in (8, 0)]
                down, down_far = [sums[pl.ds(lower_row * WIDTH + 8 * t + s, 8), :] for s in (8, 0)]
                tiles.append(jnp.where(low, up, down_far) + pltpu.roll(jnp.where(low, down, up_far), 64, 1))
            return jnp.concatenate(tiles, axis=0)

        def fine_row(y, carry):
            here = pl.ds(pl.multiple_of(y * 64, 64), 64)
            fine[here, :] = gather(BASES[0] + y, BASES[0] + 32 + y, 64).astype(jnp.bfloat16)
            return carry

        lax.fori_loop(0, 32, fine_row, 0, unroll=4)
        fine_copy = pltpu.make_async_copy(fine, out_ref.at[0], sems.at[0])
        fine_copy.start()
        coarse[...] = jnp.zeros_like(coarse)
        for y in range(16):
            coarse[0, pl.ds(32 * y, 32), :] = gather(BASES[1] + y, BASES[1] + 16 + y, 32).astype(jnp.bfloat16)
        for level, cells in ((2, 16), (3, 8)):
            for y in range(cells):
                tile = gather(BASES[level] + y, BASES[level] + y, cells)
                tile = jnp.where(low_half(cells), tile, 0.0)
                if cells < 16:
                    tile = jnp.concatenate([tile, jnp.zeros_like(tile)], axis=0)
                coarse[level - 1, pl.ds(32 * y, 16), :] = tile.astype(jnp.bfloat16)
        coarse_copy = pltpu.make_async_copy(coarse, out_ref.at[pl.ds(1, 3), pl.ds(0, 512), :], sems.at[1])
        coarse_copy.start()
        fine_copy.wait()
        coarse_copy.wait()


def spread(table, first, second, micros, block=64):
    steps = first.shape[0] // block
    return pl.pallas_call(
        spread_kernel,
        grid=(2 * steps,),
        in_specs=[pl.BlockSpec(memory_space=pltpu.SMEM)] + [pl.BlockSpec(memory_space=pltpu.VMEM)] * 2,
        out_specs=pl.BlockSpec(memory_space=pltpu.HBM),
        scratch_shapes=[
            pltpu.VMEM((32 * block, LANES), jnp.float32),
            pltpu.VMEM((CELLS, LANES), jnp.float32),
            pltpu.VMEM((FINE, LANES), jnp.bfloat16),
            pltpu.VMEM((3, 512, LANES), jnp.bfloat16),
            pltpu.SemaphoreType.DMA((2,)),
        ],
        out_shape=pltpu.HBM((4, FINE, LANES), jnp.bfloat16),
        cost_estimate=cost(micros),
        compiler_params=params(15),
    )(table, first, second)


def bin_order():
    pairs = [(2 * i + p) * POOL + e for i in range(3) for e in range(POOL) for p in range(2)]
    return pairs + [6 * POOL + e for e in range(POOL)]


def write_note(boxes_ref, routes_ref, labels_ref, targets_ref, image_ref):
    halves = []
    for s in range(2):
        boxes = boxes_ref[s]
        high = jnp.right_shift(boxes, 6)
        rest = targets_ref[s]
        parts = [high.astype(jnp.float32), (boxes - 64 * high).astype(jnp.float32)]
        parts += [routes_ref[s : s + 1].astype(jnp.float32), labels_ref[s : s + 1].astype(jnp.float32)]
        for _ in range(3):
            part = rest.astype(jnp.bfloat16).astype(jnp.float32)
            parts.append(part)
            rest = rest - part
        parts += [jnp.full((1, 64), image_ref[0, j], jnp.int32).astype(jnp.float32) for j in range(2)]
        halves.append(jnp.concatenate(parts + [jnp.zeros((8, 64), jnp.float32)], axis=0))
    return jnp.concatenate(halves, axis=1).astype(jnp.bfloat16)


def decode(notes, info_ref, table_ref):
    notes = [n.astype(jnp.float32) for n in notes]
    for s in range(2):
        rows = jnp.concatenate([n[:, 64 * s : 64 * s + 64] for n in notes], axis=1)
        boxes_float = rows[:4] * 64.0 + rows[4:8]
        targets = (rows[10:14] + rows[14:18]) + rows[18:22]
        pad = jnp.zeros((6, rows.shape[1]), jnp.float32)
        info_ref[s] = jnp.concatenate([boxes_float, rows[8:10], targets, pad], axis=0)
        boxes = boxes_float.astype(jnp.int32)
        route = rows[8:9].astype(jnp.int32)
        sizes = rows[22:24].astype(jnp.int32) * 16
        lines = []
        for axis in range(2):
            limit = sizes[axis : axis + 1]
            low_edge = jnp.minimum(jnp.maximum(boxes[axis : axis + 1], 0), limit)
            high_edge = jnp.minimum(jnp.maximum(boxes[axis + 2 : axis + 3], 0), limit)
            stride = jnp.left_shift(4, route)
            first = 28 * low_edge + (high_edge - low_edge) - 224 * stride
            cell = jnp.right_shift((jnp.right_shift(first, 8 + route) + 7) * 9363, 16) - 1
            units = 448 * stride
            scale = 1.0 / units.astype(jnp.float32)
            lines.append((cell, (first - cell * units).astype(jnp.float32) * scale, (2 * (high_edge - low_edge)).astype(jnp.float32) * scale))
        row = jnp.where(route == 0, BASES[0], jnp.where(route == 1, BASES[1], jnp.where(route == 2, BASES[2], BASES[3])))
        start = (row + lines[0][0]) * WIDTH + 8 + lines[1][0]
        parts = [start.astype(jnp.float32), lines[0][1], lines[0][2], lines[1][1], lines[1][2]]
        table_ref[s] = jnp.concatenate(parts + [jnp.zeros((3, rows.shape[1]), jnp.float32)], axis=0)


TABLES = [jax.ShapeDtypeStruct((2, 16, 256), jnp.float32), jax.ShapeDtypeStruct((2, 8, 256), jnp.float32)]


def arrange_kernel(
    slot_ref, own_ref, one_ref, two_ref, three_ref, near_ref, core_ref, chip_ref, far_ref,
    levels_ref, info_ref, table_ref, coarse_ref,
):
    slot, me = slot_ref[0], slot_ref[1]
    for k, ref in enumerate((near_ref, core_ref, chip_ref, far_ref)):
        coarse_ref[jnp.bitwise_xor(me, k)] = ref[...]
    fine = own_ref[...] + one_ref[...] + two_ref[...] + three_ref[...]
    levels_ref[slot, pl.ds(0, FINE), :] = fine.reshape(FINE, LANES)
    for level in range(1, 4):
        levels_ref[slot, pl.ds(FINE + (level - 1) * 512, 512), :] = coarse_ref[level, pl.ds(0, 512), :]
    for d in range(4):
        levels_ref[slot, pl.ds(NOTES + 32 * d, 32), :] = coarse_ref[d, pl.ds(512, 32), :]
    decode([coarse_ref[d, pl.ds(512, 32), :] for d in range(4)], info_ref, table_ref)


def arrange(slot, slots, own, arrived, coarse):
    vmem = pl.BlockSpec(memory_space=pltpu.VMEM)
    return pl.pallas_call(
        arrange_kernel,
        in_specs=[pl.BlockSpec(memory_space=pltpu.SMEM)] + [vmem] * 8,
        out_shape=[jax.ShapeDtypeStruct((slots, BUFFER, LANES), jnp.bfloat16)] + TABLES,
        scratch_shapes=[pltpu.VMEM((4, 544, LANES), jnp.bfloat16)],
        cost_estimate=cost(2),
        compiler_params=params(7),
    )(slot, own, *arrived, *coarse)


def prepare_kernel(slot_ref, levels_ref, info_ref, table_ref):
    slot = slot_ref[0]
    decode([levels_ref[slot, pl.ds(NOTES + 32 * d, 32), :] for d in range(4)], info_ref, table_ref)


def prepare(slot, levels):
    vmem = pl.BlockSpec(memory_space=pltpu.VMEM)
    return pl.pallas_call(
        prepare_kernel,
        in_specs=[pl.BlockSpec(memory_space=pltpu.SMEM), vmem],
        out_shape=TABLES,
        cost_estimate=cost(1),
    )(slot, levels)[1]


def valid_edges(owner, image_ref):
    shift = 2 + owner
    round_up = jnp.left_shift(1, shift) - 1
    return [jnp.right_shift(image_ref[0, j] + round_up, shift) for j in range(2)]


def pack_kernel(
    owner_ref, image_ref, upper_ref, lower_ref, small_ref, boxes_hbm, routes_hbm, labels_hbm, targets_hbm,
    own_ref, one_ref, two_ref, three_ref, near_ref, core_ref, chip_ref, far_ref,
    boxes_ref, routes_ref, labels_ref, targets_ref, sems, coarse_ref,
):
    g = pl.program_id(0)
    owner = owner_ref[0]
    rows_valid, cols_valid = valid_edges(owner, image_ref)
    pairs = ((boxes_hbm, boxes_ref), (routes_hbm, routes_ref), (labels_hbm, labels_ref), (targets_hbm, targets_ref))
    copies = [pltpu.make_async_copy(a, b, sems.at[j]) for j, (a, b) in enumerate(pairs)]

    @pl.when(g == 0)
    def _():
        for copy in copies:
            copy.start()

    cell = lax.broadcasted_iota(jnp.int32, (GRID, LANES), 0)
    low = low_half(GRID)
    outs = (own_ref, one_ref, two_ref, three_ref)
    for y in range(upper_ref.shape[2]):
        top = (cell < cols_valid) & (g * upper_ref.shape[2] + y < rows_valid)
        bottom = (cell < cols_valid) & (32 + g * upper_ref.shape[2] + y < rows_valid)
        for c in range(2):
            a = jnp.where(top, upper_ref[0, 0, y, :, pl.ds(LANES * c, LANES)].astype(jnp.float32), 0.0)
            b = jnp.where(bottom, lower_ref[0, 0, y, :, pl.ds(LANES * c, LANES)].astype(jnp.float32), 0.0)
            even = jnp.where(low, a, pltpu.roll(b, 64, 1))
            if c == 0:
                even = jnp.where(owner == 0, even, 0.0)
            outs[2 * c][y] = even.astype(jnp.bfloat16)
            outs[2 * c + 1][y] = jnp.where(low, pltpu.roll(a, 64, 1), b).astype(jnp.bfloat16)

    @pl.when(g == 0)
    def _():
        low = low_half(32)
        cell = lax.broadcasted_iota(jnp.int32, (32, LANES), 0)
        for y in range(16):
            top = (cell < cols_valid) & (y < rows_valid)
            bottom = (cell < cols_valid) & (16 + y < rows_valid) & (owner < 2)
            for c in range(2):
                a = jnp.where(top, small_ref[0, 0, y, pl.ds(0, 32), pl.ds(LANES * c, LANES)].astype(jnp.float32), 0.0)
                b = jnp.where(bottom, small_ref[0, 0, 16 + y, pl.ds(0, 32), pl.ds(LANES * c, LANES)].astype(jnp.float32), 0.0)
                here = pl.ds(32 * y, 32)
                coarse_ref[2 * c, here, :] = jnp.where(low, a, pltpu.roll(b, 64, 1)).astype(jnp.bfloat16)
                coarse_ref[2 * c + 1, here, :] = jnp.where(low, pltpu.roll(a, 64, 1), b).astype(jnp.bfloat16)
        for copy in copies:
            copy.wait()
        note = write_note(boxes_ref, routes_ref, labels_ref, targets_ref, image_ref)
        for d in range(4):
            coarse_ref[d, pl.ds(512, 32), :] = note
        for k, ref in enumerate((near_ref, core_ref, chip_ref, far_ref)):
            ref[...] = coarse_ref[jnp.bitwise_xor(owner, k)]


def pack(owner, image_size, pyramid, boxes, routes, labels, targets):
    regions = (boxes, routes, labels, targets)
    return pl.pallas_call(
        pack_kernel,
        grid=(4,),
        in_specs=[
            pl.BlockSpec(memory_space=pltpu.SMEM),
            pl.BlockSpec(memory_space=pltpu.SMEM),
            pl.BlockSpec((1, 1, 8, GRID, CHANNELS), lambda g: (0, 0, g, 0, 0)),
            pl.BlockSpec((1, 1, 8, GRID, CHANNELS), lambda g: (0, 0, g + 4, 0, 0)),
            pl.BlockSpec((1, 1, 32, GRID, CHANNELS), lambda g: (0, 0, 0, 0, 0)),
        ]
        + [pl.BlockSpec(memory_space=pltpu.HBM)] * 4,
        out_specs=[pl.BlockSpec((8, GRID, LANES), lambda g: (g, 0, 0))] * 4
        + [pl.BlockSpec((544, LANES), lambda g: (0, 0))] * 4,
        scratch_shapes=[pltpu.VMEM(v.shape, v.dtype) for v in regions]
        + [pltpu.SemaphoreType.DMA((4,)), pltpu.VMEM((4, 544, LANES), jnp.bfloat16)],
        out_shape=[jax.ShapeDtypeStruct((32, GRID, LANES), jnp.bfloat16)] * 4
        + [jax.ShapeDtypeStruct((544, LANES), jnp.bfloat16)] * 4,
        cost_estimate=cost(2.7),
        compiler_params=params(8),
    )(owner, in_hbm(image_size), *[in_hbm(pyramid)] * 3, *[in_hbm(v) for v in regions])


def unpack_kernel(owner_ref, image_ref, fine_ref, coarse_ref, out_ref):
    g = pl.program_id(0)
    owner = owner_ref[0]
    rows_valid, cols_valid = valid_edges(owner, image_ref)
    count = out_ref.shape[1]

    @pl.when(owner == 0)
    def _():
        cell = lax.broadcasted_iota(jnp.int32, (GRID, LANES), 0)
        low = low_half(GRID)
        for y in range(count):
            top = (cell < cols_valid) & (g * count + y < rows_valid)
            bottom = (cell < cols_valid) & (32 + g * count + y < rows_valid)
            for c in range(2):
                a = fine_ref[2 * c, pl.ds(y * GRID, GRID), :].astype(jnp.float32)
                b = fine_ref[2 * c + 1, pl.ds(y * GRID, GRID), :].astype(jnp.float32)
                upper = jnp.where(low, a, pltpu.roll(b, 64, 1))
                lower = jnp.where(low, pltpu.roll(a, 64, 1), b)
                out_ref[0, y, :, pl.ds(LANES * c, LANES)] = jnp.where(top, upper, 0.0).astype(jnp.bfloat16)
                out_ref[1, y, :, pl.ds(LANES * c, LANES)] = jnp.where(bottom, lower, 0.0).astype(jnp.bfloat16)

    @pl.when(owner != 0)
    def _():
        out_ref[...] = jnp.zeros_like(out_ref)
        cell = lax.broadcasted_iota(jnp.int32, (32, LANES), 0)
        low = low_half(32)
        for y in range(count):
            top = (cell < cols_valid) & (g * count + y < rows_valid)
            line = pl.ds(pl.multiple_of(((g % 2) * count + y) * 32, 32), 32)
            for c in range(2):
                a = coarse_ref[2 * c, line, :].astype(jnp.float32)
                b = coarse_ref[2 * c + 1, line, :].astype(jnp.float32)
                upper = jnp.where(low, a, pltpu.roll(b, 64, 1))
                lower = jnp.where(low, pltpu.roll(a, 64, 1), b)
                row = jnp.where(g < 2, upper, lower)
                out_ref[0, y, pl.ds(0, 32), pl.ds(LANES * c, LANES)] = jnp.where(top, row, 0.0).astype(jnp.bfloat16)


def unpack(owner, image_size, parts, micros):
    return pl.pallas_call(
        unpack_kernel,
        grid=(4,),
        in_specs=[pl.BlockSpec(memory_space=pltpu.SMEM)] * 2
        + [pl.BlockSpec((4, 512, LANES), lambda g: (0, g, 0)), pl.BlockSpec((4, 512, LANES), lambda g: (0, 0, 0))],
        out_specs=pl.BlockSpec((2, 8, GRID, CHANNELS), lambda g: (0, g, 0, 0)),
        out_shape=jax.ShapeDtypeStruct((2, 32, GRID, CHANNELS), jnp.bfloat16),
        cost_estimate=cost(micros),
        compiler_params=params(7),
    )(owner, image_size, parts, parts)


def to_bins_kernel(order_ref, weight_ref, out_ref, arrived, rows, sems, section):
    del order_ref
    taken = arrived.shape[1]
    blocks = weight_ref.shape[1] // taken

    def fetch(c):
        slot = c % 2
        return pltpu.make_async_copy(weight_ref.at[section, pl.ds(c * taken, taken), :], arrived.at[slot], sems.at[slot])

    fetch(0).start()
    fetch(1).start()

    def step(c, carry):
        fetch(c).wait()
        for t in range(rows.shape[0]):
            rows[t] = arrived[c % 2, :, pl.ds(t * LANES, LANES)].astype(jnp.float32)

        @pl.when(c + 2 < blocks)
        def _():
            fetch(c + 2).start()

        here = pl.ds(pl.multiple_of(c * 16, 16), 16)
        for place, source in enumerate(bin_order()):
            for t in range(rows.shape[0]):
                out_ref[place, here, pl.ds(t * LANES, LANES)] = rows[t, pl.ds(source, 16, stride=49), :].astype(jnp.bfloat16)
        return carry

    lax.fori_loop(0, blocks, step, 0)
    out_ref[49] = jnp.zeros(out_ref.shape[1:], jnp.bfloat16)


def to_bins(order, weight, section, micros):
    rows, width = weight.shape[1:]
    channels = rows // 49
    return pl.pallas_call(
        lambda *refs: to_bins_kernel(*refs, section),
        in_specs=[pl.BlockSpec(memory_space=pltpu.SMEM), pl.BlockSpec(memory_space=pltpu.HBM)],
        out_specs=pl.BlockSpec(memory_space=pltpu.VMEM),
        out_shape=jax.ShapeDtypeStruct((50, channels, width), jnp.bfloat16),
        scratch_shapes=[
            pltpu.VMEM((2, 784, width), jnp.bfloat16),
            pltpu.VMEM((width // LANES, 784, LANES), jnp.float32),
            pltpu.SemaphoreType.DMA((2,)),
        ],
        cost_estimate=cost(micros),
        compiler_params=params(8),
    )(order, in_hbm(weight)).reshape(WIDE, width)


def first_kernel(pooled_ref, weight_ref, out_ref):
    for n in range(0, out_ref.shape[1], 256):
        here = pl.ds(n, 256)
        out_ref[:, here] = jnp.dot(pooled_ref[...], weight_ref[:, here], preferred_element_type=jnp.float32).astype(jnp.bfloat16)


def first_product(pooled, weight, micros):
    vmem = pl.BlockSpec(memory_space=pltpu.VMEM)
    return pl.pallas_call(
        first_kernel,
        in_specs=[vmem, vmem],
        out_specs=vmem,
        out_shape=jax.ShapeDtypeStruct((pooled.shape[0], weight.shape[1]), jnp.bfloat16),
        cost_estimate=cost(micros),
        compiler_params=params(6),
    )(pooled, weight)


def back_kernel(order_ref, grads_ref, weight_ref, out_ref):
    del order_ref
    for n in range(0, WIDE, 640):
        here = pl.ds(n, 640)
        value = lax.dot_general(grads_ref[...], weight_ref[here, :], NT, preferred_element_type=jnp.float32)
        out_ref[:, here] = value.astype(jnp.bfloat16)


def back_product(order, grads, weight, micros):
    vmem = pl.BlockSpec(memory_space=pltpu.VMEM)
    return pl.pallas_call(
        back_kernel,
        in_specs=[pl.BlockSpec(memory_space=pltpu.SMEM), vmem, vmem],
        out_specs=vmem,
        out_shape=jax.ShapeDtypeStruct((grads.shape[0], WIDE), jnp.bfloat16),
        cost_estimate=cost(micros),
        compiler_params=params(6),
    )(order, grads, weight)


SPLIT = 1920
TAIL = WIDE - SPLIT


def outer_kernel(bits_ref, own, cross, own_pooled, cross_pooled, sent_one, kept_one, sent_two, kept_two):
    rows = own.shape[2]

    def product(pick, at, width, out):
        mine, theirs = [pick(ref).reshape(2 * rows, -1) for ref in (own, cross)]
        for n in range(0, width, 256):
            wide = min(256, width - n)
            here = pl.ds(at + n, wide)
            value = jnp.dot(mine, own_pooled[:, here], preferred_element_type=jnp.float32)
            value = value + jnp.dot(theirs, cross_pooled[:, here], preferred_element_type=jnp.float32)
            out[:, :, pl.ds(n, wide)] = value.astype(out.dtype).reshape(2, rows, wide)

    product(lambda ref: ref[:, bits_ref[1]], 0, SPLIT, sent_one)
    product(lambda ref: ref[bits_ref[3]], SPLIT, TAIL, sent_two)
    product(lambda ref: ref[:, bits_ref[0]], 0, SPLIT, kept_one)
    product(lambda ref: ref[bits_ref[2]], SPLIT, TAIL, kept_two)


def outer_sums(bits, own, cross, own_pooled, cross_pooled, micros):
    rows = own.shape[2]
    vmem = pl.BlockSpec(memory_space=pltpu.VMEM)
    kinds = [(width, jnp.bfloat16) for width in (SPLIT, TAIL) for _ in range(2)]
    return pl.pallas_call(
        outer_kernel,
        in_specs=[pl.BlockSpec(memory_space=pltpu.SMEM)] + [vmem] * 4,
        out_specs=[vmem] * 4,
        out_shape=[jax.ShapeDtypeStruct((2, rows, width), dtype) for width, dtype in kinds],
        cost_estimate=cost(micros),
        compiler_params=params(6),
    )(bits, own, cross, own_pooled, cross_pooled)


def fold_kernel(bits_ref, kept_one, arrived_one, kept_two, arrived_two, one_ref, two_ref):
    up, low = bits_ref[3], bits_ref[1]
    one_ref[...] = (kept_one[up].astype(jnp.float32) + arrived_one[up].astype(jnp.float32)).astype(jnp.bfloat16)
    two_ref[...] = (kept_two[low].astype(jnp.float32) + arrived_two[low].astype(jnp.float32)).astype(jnp.bfloat16)


def fold(bits, kept_one, arrived_one, kept_two, arrived_two):
    rows = kept_one.shape[1]
    vmem = pl.BlockSpec(memory_space=pltpu.VMEM)
    return pl.pallas_call(
        fold_kernel,
        in_specs=[pl.BlockSpec(memory_space=pltpu.SMEM)] + [vmem] * 4,
        out_specs=[vmem] * 2,
        out_shape=[jax.ShapeDtypeStruct((rows, SPLIT), jnp.bfloat16), jax.ShapeDtypeStruct((rows, TAIL), jnp.bfloat16)],
        cost_estimate=cost(8),
        compiler_params=params(5),
    )(bits, kept_one, arrived_one, kept_two, arrived_two)


def from_bins_kernel(bits_ref, *refs):
    del bits_ref
    kept_one, arrived_one, last_one, kept_two, arrived_two, last_two = refs[:6]
    out_ref, turned = refs[-2:]
    for kept, arrived, last, at in ((kept_one, arrived_one, last_one, 0), (kept_two, arrived_two, last_two, SPLIT)):
        for t in range(kept.shape[2] // LANES):
            here = pl.ds(t * LANES, LANES)
            value = kept[0, :, here].astype(jnp.float32) + arrived[0, :, here].astype(jnp.float32)
            value = value + last[:, here].astype(jnp.float32)
            turned[pl.ds(at + t * LANES, LANES), :] = jnp.transpose(value, (1, 0))
    for place, source in enumerate(bin_order()):
        out_ref[0, pl.ds(source, 64, stride=49), :] = turned[pl.ds(place * 64, 64), :]


def from_bins(bits, section, kept, arrived, last, before, rows, micros):
    columns = kept[0].shape[1]
    specs = []
    for at, width in ((2, SPLIT), (0, TAIL)):
        both = pl.BlockSpec((1, columns, width), lambda i, b, at=at: (b[at], 0, 0))
        specs += [both, both, pl.BlockSpec((columns, width), lambda i, b: (0, 0))]
    operands = [kept[0], arrived[0], last[0], kept[1], arrived[1], last[1]]
    aliases = {}
    if before is not None:
        specs.append(pl.BlockSpec(memory_space=pl.ANY))
        operands.append(before)
        aliases = {7: 0}
    return pl.pallas_call(
        from_bins_kernel,
        grid_spec=pltpu.PrefetchScalarGridSpec(
            num_scalar_prefetch=1,
            grid=(1,),
            in_specs=specs,
            out_specs=pl.BlockSpec((1, rows, columns), lambda i, b: (section, 0, 0)),
            scratch_shapes=[pltpu.VMEM((WIDE, LANES), jnp.float32)],
        ),
        out_shape=jax.ShapeDtypeStruct((2, rows, columns), jnp.float32),
        input_output_aliases=aliases,
        cost_estimate=cost(micros),
        compiler_params=params(6),
    )(bits, *operands)


def silu_slope(values):
    sigma = jax.nn.sigmoid(values)
    return sigma * (1.0 + values * (1.0 - sigma))


NT = (((1,), (1,)), ((), ()))
TN = (((0,), (0,)), ((), ()))
OUTER = 128


def write_sums(sums, width):
    high = sums.astype(jnp.bfloat16).astype(jnp.float32)
    rows = []
    for part in (high, sums - high):
        rest = part[:, width:]
        if rest.shape[1] < width:
            rest = jnp.concatenate([rest, jnp.zeros((1, width - rest.shape[1]), jnp.float32)], axis=1)
        rows += [part[:, :width], rest]
    return jnp.concatenate(rows + [jnp.zeros((EXTRA - 4, width), jnp.float32)], axis=0).astype(jnp.bfloat16)


def read_sums(note, count):
    note = note.astype(jnp.float32)
    rows = note[0:2] + note[2:4]
    return jnp.concatenate([rows[0:1], rows[1:2]], axis=1)[:, :count]


def head_kernel(
    me_ref, mine_ref, theirs_ref, info_ref, feature_bias_ref, hidden_ref, hidden_bias_ref, class_ref, class_bias_ref,
    delta_ref, delta_bias_ref,
    *refs, images,
):
    logits_ref, deltas_ref, small_ref, small_away_ref, grad_feature_ref, stay_ref, away_ref = refs[-12:-5]
    outer_scr, turned_scr, weight_scr, row_scr, small_scr = refs[-5:]
    me, half = me_ref[0], me_ref[1]
    weight_scr[...] = jnp.zeros_like(weight_scr)
    weight_scr[pl.ds(0, CLASSES), :] = class_ref[0]
    weight_scr[pl.ds(OUTER, DELTAS), :] = delta_ref[0]
    row_scr[...] = jnp.zeros_like(row_scr)
    row_scr[:, pl.ds(0, CLASSES)] = class_bias_ref[0]
    row_scr[:, pl.ds(OUTER, DELTAS)] = delta_bias_ref[0]
    f32 = jnp.float32
    rows, hidden = mine_ref.shape
    pre_feature = mine_ref[...].astype(f32) + theirs_ref[...].astype(f32) + feature_bias_ref[0]
    gate_one = jax.nn.sigmoid(pre_feature)
    hidden_one = (pre_feature * gate_one).astype(jnp.bfloat16)
    pre_hidden = jnp.dot(hidden_one, hidden_ref[0], preferred_element_type=f32) + hidden_bias_ref[0]
    gate_two = jax.nn.sigmoid(pre_hidden)
    hidden_two = (pre_hidden * gate_two).astype(jnp.bfloat16)
    outer = lax.dot_general(hidden_two, weight_scr[...], NT, preferred_element_type=f32) + row_scr[...]
    outer_scr[...] = outer
    own = pl.ds(pl.multiple_of(me * (rows // 4), rows // 4), rows // 4)
    logits_ref[0] = outer_scr[own, pl.ds(0, CLASSES)]
    deltas_ref[0] = outer_scr[own, pl.ds(OUTER, DELTAS)]

    columns = jnp.transpose(info_ref[0], (1, 0))
    label = columns[:, 5:6].astype(jnp.int32)
    lane = lax.broadcasted_iota(jnp.int32, (rows, OUTER), 1)
    logits = jnp.where(lane < CLASSES, outer[:, :OUTER], -jnp.inf)
    shifted = jnp.exp(logits - jnp.max(logits, axis=1, keepdims=True))
    grad_logits = shifted / jnp.sum(shifted, axis=1, keepdims=True) - (lane == label).astype(f32)
    wide = lax.broadcasted_iota(jnp.int32, (rows, outer.shape[1] - OUTER), 1)
    hot = (wide // 4 == label) & (label < CLASSES - 1)
    picked = jnp.where(hot, outer[:, OUTER:], 0.0)
    grad_deltas = jnp.zeros_like(picked)
    for j in range(4):
        mine = wide % 4 == j
        chosen = jnp.sum(jnp.where(mine, picked, 0.0), axis=1, keepdims=True)
        error = jnp.clip(chosen - columns[:, 6 + j : 7 + j], -1.0, 1.0)
        grad_deltas = jnp.where(mine & hot, error, grad_deltas)
    grad_outer = jnp.concatenate([grad_logits, grad_deltas], axis=1).astype(jnp.bfloat16)

    grad_two = jnp.dot(grad_outer, weight_scr[...], preferred_element_type=f32)
    slope_two = gate_two * (1.0 + pre_hidden * (1.0 - gate_two))
    grad_pre_hidden = (grad_two * slope_two).astype(jnp.bfloat16)
    grad_one = lax.dot_general(grad_pre_hidden, hidden_ref[0], NT, preferred_element_type=f32)
    slope_one = gate_one * (1.0 + pre_feature * (1.0 - gate_one))
    grad_feature = grad_one * slope_one
    grad_pre_feature = grad_feature.astype(jnp.bfloat16)
    grad_feature_ref[...] = grad_pre_feature
    turned_scr[...] = jnp.transpose(grad_feature, (1, 0)).astype(jnp.bfloat16)
    stay_ref[...] = turned_scr[pl.ds(pl.multiple_of(half * (hidden // 2), hidden // 2), hidden // 2), :]
    away_ref[...] = turned_scr[pl.ds(pl.multiple_of((1 - half) * (hidden // 2), hidden // 2), hidden // 2), :]

    run = hidden // (4 * images)
    row = lax.broadcasted_iota(jnp.int32, (hidden, hidden // 4), 0)
    col = lax.broadcasted_iota(jnp.int32, (hidden, hidden // 4), 1)
    pick = (row == (col // run) * (4 * run) + me * run + col % run).astype(jnp.bfloat16)
    one_rows = jnp.dot(hidden_one, pick, preferred_element_type=f32).astype(jnp.bfloat16)
    two_rows = jnp.dot(hidden_two, pick, preferred_element_type=f32).astype(jnp.bfloat16)
    small_scr[:, pl.ds(0, hidden)] = lax.dot_general(one_rows, grad_pre_hidden, TN, preferred_element_type=f32).astype(jnp.bfloat16)
    small_scr[:, pl.ds(hidden, outer.shape[1])] = lax.dot_general(two_rows, grad_outer, TN, preferred_element_type=f32).astype(jnp.bfloat16)
    middle = me_ref[2]
    part = small_scr.shape[0] // 2
    if images == 8:
        for j in range(images // 2):
            here = pl.ds(j * run, run)
            for bit, ref in ((middle, small_ref), (1 - middle, small_away_ref)):
                source = (j // 2) * 4 * run + bit * 2 * run + (j % 2) * run
                ref[0, here, :] = small_scr[pl.ds(pl.multiple_of(source, run), run), :]
    else:
        small_ref[0, pl.ds(0, part), :] = small_scr[pl.ds(0, part), :]
        small_away_ref[0, pl.ds(0, part), :] = small_scr[pl.ds(part, part), :]
    sums = [jnp.sum(v.astype(f32), axis=0, keepdims=True) for v in (grad_pre_feature, grad_pre_hidden, grad_outer)]
    sums = jnp.concatenate(sums, axis=1)
    note = write_sums(sums, small_scr.shape[1])
    for ref in (small_ref, small_away_ref):
        ref[0, pl.ds(ref.shape[1] - EXTRA, EXTRA), :] = note


def head(me, mine, theirs, section, stacked, images, before, micros):
    rows, hidden = mine.shape
    width = 512
    sections = stacked[0].shape[0]

    def whole(shape):
        return pl.BlockSpec(shape, lambda g, m: (0,) * len(shape))

    def of_section(array):
        return pl.BlockSpec((1,) + array.shape[1:], lambda g, m: (section, 0, 0))

    def kernel(*refs):
        head_kernel(*refs, images=images)

    shared = [
        jax.ShapeDtypeStruct((sections, rows // 4, CLASSES), jnp.float32),
        jax.ShapeDtypeStruct((sections, rows // 4, DELTAS), jnp.float32),
    ]
    single = [
        pltpu.HBM((1, hidden // 8 + EXTRA, hidden + width), jnp.bfloat16),
        pltpu.HBM((1, hidden // 8 + EXTRA, hidden + width), jnp.bfloat16),
        pltpu.HBM((rows, hidden), jnp.bfloat16),
        jax.ShapeDtypeStruct((hidden // 2, rows), jnp.bfloat16),
        jax.ShapeDtypeStruct((hidden // 2, rows), jnp.bfloat16),
    ]
    return pl.pallas_call(
        kernel,
        grid_spec=pltpu.PrefetchScalarGridSpec(
            num_scalar_prefetch=1,
            grid=(1,),
            in_specs=[whole(mine.shape), whole(theirs.shape)]
            + [of_section(a) for a in stacked]
            + [pl.BlockSpec(memory_space=pl.ANY)] * len(before),
            out_specs=[of_section(o) for o in shared] + [whole(o.shape) for o in single],
            scratch_shapes=[
                pltpu.VMEM((rows, width), jnp.float32),
                pltpu.VMEM((hidden, rows), jnp.bfloat16),
                pltpu.VMEM((width, hidden), jnp.bfloat16),
                pltpu.VMEM((1, width), jnp.float32),
                pltpu.VMEM((hidden // 4, hidden + width), jnp.bfloat16),
            ],
        ),
        out_shape=shared + single,
        input_output_aliases={3 + len(stacked) + j: j for j in range(len(before))},
        cost_estimate=cost(micros),
        compiler_params=params(13),
    )(me, mine, theirs, *stacked, *before)


def pass_sums(s, kept_ref, arrived_ref, refs):
    rows, width = kept_ref.shape[1:]
    notes = [ref[s, pl.ds(rows - EXTRA, EXTRA), :] for ref in (kept_ref, arrived_ref)]
    total = write_sums(read_sums(notes[0], 2 * width) + read_sums(notes[1], 2 * width), width)
    for ref in refs:
        ref[s, pl.ds(ref.shape[1] - EXTRA, EXTRA), :] = total


def small_step_kernel(bits_ref, kept_ref, arrived_ref, stay_ref, away_ref, at):
    sections, rows, width = kept_ref.shape
    run = 32
    for s in range(sections):
        for j in range((rows - EXTRA) // (2 * run)):
            for place, ref in ((bits_ref[at], stay_ref), (bits_ref[at + 1], away_ref)):
                here = pl.ds(pl.multiple_of(j * 2 * run + place * run, run), run)
                value = kept_ref[s, here, :].astype(jnp.float32) + arrived_ref[s, here, :].astype(jnp.float32)
                ref[s, pl.ds(j * run, run), :] = value.astype(jnp.bfloat16)
        pass_sums(s, kept_ref, arrived_ref, (stay_ref, away_ref))


def small_last_kernel(order_ref, kept_ref, arrived_ref, hidden_ref, class_ref, delta_ref, one_ref, two_ref, class_sum_ref, delta_sum_ref):
    del order_ref
    run, hidden = hidden_ref.shape[1:]
    width = kept_ref.shape[2]
    for s in range(kept_ref.shape[0]):
        value = kept_ref[s, pl.ds(0, run), :].astype(jnp.float32) + arrived_ref[s, pl.ds(0, run), :].astype(jnp.float32)
        hidden_ref[s] = value[:, :hidden]
        class_ref[s] = value[:, hidden : hidden + CLASSES]
        delta_ref[s] = value[:, hidden + OUTER : hidden + OUTER + DELTAS]
        sums = read_sums(kept_ref[s, pl.ds(run, EXTRA), :], 2 * width) + read_sums(arrived_ref[s, pl.ds(run, EXTRA), :], 2 * width)
        at = 0
        for ref, step in ((one_ref, hidden), (two_ref, hidden), (class_sum_ref, OUTER), (delta_sum_ref, DELTAS)):
            ref[s : s + 1, :] = sums[:, at : at + ref.shape[1]]
            at += step


def small_join_kernel(bits_ref, *refs):
    outs = refs[4:]
    rows = refs[0].shape[1]
    run = 32
    for s in range(2):
        kept_ref, arrived_ref = refs[s], refs[2 + s]
        count = (rows - EXTRA) // (2 * run)
        for j in range(count):
            for place, ref in ((bits_ref[4], outs[0]), (bits_ref[5], outs[1])):
                here = pl.ds(pl.multiple_of(place * count * run + j * run, run), run)
                value = kept_ref[0, here, :].astype(jnp.float32) + arrived_ref[0, here, :].astype(jnp.float32)
                ref[s, pl.ds(j * run, run), :] = value.astype(jnp.bfloat16)
        notes = [ref[0, pl.ds(rows - EXTRA, EXTRA), :] for ref in (kept_ref, arrived_ref)]
        width = kept_ref.shape[2]
        total = write_sums(read_sums(notes[0], 2 * width) + read_sums(notes[1], 2 * width), width)
        for ref in outs:
            ref[s, pl.ds(ref.shape[1] - EXTRA, EXTRA), :] = total


def small_join(bits, kept, arrived):
    vmem = pl.BlockSpec(memory_space=pltpu.VMEM)
    _, rows, width = kept[0].shape
    return pl.pallas_call(
        small_join_kernel,
        in_specs=[pl.BlockSpec(memory_space=pltpu.SMEM)] + [vmem] * 4,
        out_specs=[vmem] * 2,
        out_shape=[jax.ShapeDtypeStruct((2, (rows - EXTRA) // 2 + EXTRA, width), jnp.bfloat16)] * 2,
        cost_estimate=cost(1),
        compiler_params=params(8),
    )(bits, *kept, *arrived)


def small_step(bits, at, kept, arrived):
    vmem = pl.BlockSpec(memory_space=pltpu.VMEM)
    sections, rows, width = kept.shape
    return pl.pallas_call(
        lambda *refs: small_step_kernel(*refs, at),
        in_specs=[pl.BlockSpec(memory_space=pltpu.SMEM), vmem, vmem],
        out_specs=[vmem] * 2,
        out_shape=[jax.ShapeDtypeStruct((sections, (rows - EXTRA) // 2 + EXTRA, width), jnp.bfloat16)] * 2,
        cost_estimate=cost(1),
        compiler_params=params(8),
    )(bits, kept, arrived)


def small_last(order, kept, arrived, hidden):
    sections, rows, width = kept.shape
    shapes = [(sections, rows - EXTRA, n) for n in (hidden, CLASSES, DELTAS)]
    shapes += [(sections, n) for n in (hidden, hidden, CLASSES, DELTAS)]
    vmem = pl.BlockSpec(memory_space=pltpu.VMEM)
    return pl.pallas_call(
        small_last_kernel,
        in_specs=[pl.BlockSpec(memory_space=pltpu.SMEM), vmem, vmem],
        out_shape=[jax.ShapeDtypeStruct(shape, jnp.float32) for shape in shapes],
        cost_estimate=cost(1),
        compiler_params=params(8),
    )(order, kept, arrived)


def swap(value, axis, bit):
    size = lax.axis_size(axis)
    return lax.ppermute(value, axis, [(i, i ^ bit) for i in range(size)])


def after(value, *others):
    return lax.optimization_barrier((value,) + others)[0]


def choose(array, axis, bit):
    return lax.dynamic_index_in_dim(array, bit, axis, keepdims=False)


def split_bits(array, bits):
    return array.reshape((2,) * bits + (array.shape[0] >> bits,) + array.shape[1:])


def body(
    pyramid,
    image_size,
    region_boxes,
    routes,
    labels,
    targets,
    feature_weight,
    feature_bias,
    hidden_weight,
    hidden_bias,
    class_weight,
    class_bias,
    delta_weight,
    delta_bias,
):
    images = lax.axis_size("img")
    me = lax.axis_index("lvl").astype(jnp.int32)
    image = lax.axis_index("img").astype(jnp.int32)
    sections = routes.shape[0]
    features = feature_weight.shape[1]
    hidden = hidden_weight.shape[2]
    top = images // 2
    steps = images.bit_length() - 2
    half = jnp.minimum(image & top, 1)
    own_bits = [jnp.minimum(image & (1 << b), 1) for b in range(steps)]
    me_list = jnp.stack([me, half, jnp.minimum(image & 2, 1)])

    own, *packed = pack(me_list, image_size, pyramid, region_boxes, routes, labels, targets)
    quarters, small = packed[:3], packed[3:]
    arrived = [lax.ppermute(quarters[d], "lvl", [(0, d + 1)]) for d in (1, 2, 0)]
    coarse = [small[0]] + [swap(small[k], "lvl", k) for k in (1, 2, 3)]
    weight_a = to_bins(me_list, feature_weight, 0, 10)
    slot = jnp.stack([jnp.zeros((), jnp.int32), me])
    levels, info, table = arrange(after(slot, weight_a), 1, own, arrived, coarse)
    cross_levels = swap(levels, "img", top)

    stacked = (
        info, feature_bias[:, None], hidden_weight, hidden_bias[:, None], jnp.swapaxes(class_weight, 1, 2),
        class_bias[:, None], jnp.swapaxes(delta_weight, 1, 2), delta_bias[:, None],
    )

    def run_head(s, parts, before, ready, micros):
        results = head(after(me_list, *ready), *parts, s, stacked, images, before, micros)
        shared, small, (grads, stay, away) = results[:2], results[2:4], results[4:]
        return shared, small, grads, stay, swap(away, "img", top)

    def add(first, second):
        return (first.astype(jnp.float32) + second.astype(jnp.float32)).astype(jnp.bfloat16)

    pooled_a = crop(table, 0, levels, 12)
    part_a = first_product(pooled_a, weight_a, 1)
    weight_b = to_bins(after(me_list, part_a), feature_weight, 1, 8)
    chip_a = add(part_a, swap(part_a, "lvl", 1))
    pooled_b = crop(after(table, weight_b, chip_a), 1, levels, 8)
    part_b = first_product(pooled_b, weight_b, 0)
    shared, small_a, grads_a, stay_a, cross_a = run_head(0, (chip_a, swap(chip_a, "lvl", 2)), (), [part_b], 0)
    part_b = after(part_b, grads_a)
    theirs_b = swap(part_b, "lvl", 1)
    cross_table = prepare(after(slot, grads_a), cross_levels)
    chip_b = add(after(part_b, cross_table), theirs_b)
    far_a = crop(after(cross_table, chip_b), 0, cross_levels, 8)
    parts_b = (chip_b, swap(chip_b, "lvl", 2))
    if images == 8:
        bits = jnp.stack([own_bits[0], 1 - own_bits[0], own_bits[1], 1 - own_bits[1], half, 1 - half])

        def weight_sums(stay, cross, pooled, far, ready):
            pieces = [v.reshape(2, 2, hidden // images, -1) for v in (stay, cross)]
            sent_one, kept_one, sent_two, kept_two = outer_sums(after(bits, *ready), *pieces, pooled, far, 0)
            return (kept_one, kept_two), (swap(sent_one, "img", 1), swap(sent_two, "img", 2))

        def second_step(kept, arrived, ready):
            one, two = fold(after(bits, *ready), kept[0], arrived[0], kept[1], arrived[1])
            return one, (swap(one, "img", 2), swap(two, "img", 1))

        small_near_a = swap(small_a[1], "img", 2)
        kept_a, arrived_a = weight_sums(stay_a, cross_a, pooled_a, far_a, [])
        shared, small_b, grads_b, stay_b, cross_b = run_head(1, parts_b, shared, [kept_a[0]], 0)
        small_near_b = swap(small_b[1], "img", 2)
        far_b = crop(after(cross_table, grads_b, small_near_a), 1, cross_levels, 10)
        kept_b, arrived_b = weight_sums(stay_b, cross_b, pooled_b, far_b, [])
        folded, last_a = second_step(kept_a, arrived_a, [kept_b[0]])
        slots_a = back_product(after(me_list, folded), grads_a, weight_a, 10)
        small, away = small_join(after(bits, slots_a), (small_a[0], small_b[0]), (small_near_a, small_near_b))
        arrived_small = swap(away, "img", 4)
        slots_b = back_product(after(me_list, away), grads_b, weight_b, 0)
        spread_out = spread(table, slots_a, slots_b, 0)
        folded, last_b = second_step(kept_b, arrived_b, [spread_out, *last_a])
        small, away = small_step(after(bits, folded), 0, small, arrived_small)
        arrived_small = swap(away, "img", 1)
    else:
        shared, small_b, grads_b, stay_b, cross_b = run_head(1, parts_b, shared, [far_a], 0)
        slots_a = back_product(me_list, grads_a, weight_a, 8)
        slots_b = back_product(me_list, grads_b, weight_b, 5)
        spread_out = spread(table, slots_a, slots_b, 20)
        far_b = crop(cross_table, 1, cross_levels, 10)
        totals = []
        for stay, cross, pooled, far in ((stay_a, cross_a, pooled_a, far_a), (stay_b, cross_b, pooled_b, far_b)):
            total = jnp.dot(stay, pooled, preferred_element_type=jnp.float32)
            total = total + jnp.dot(cross, far, preferred_element_type=jnp.float32)
            for b in range(steps)[::-1]:
                halves = split_bits(total, 1)
                away = choose(halves, 0, 1 - own_bits[b]).astype(jnp.bfloat16)
                total = choose(halves, 0, own_bits[b]) + swap(away, "img", 1 << b).astype(jnp.float32)
            totals.append(total[:, :features])
        order = bin_order()
        back = jnp.array([order.index(j) for j in range(49)])
        total = jnp.stack(totals)
        total = total.reshape(sections, total.shape[1], 49, features // 49)[:, :, back]
        feature_weight_grad = total.transpose(0, 3, 2, 1).reshape(sections, features, -1)

    parts = lax.all_to_all(spread_out, "lvl", split_axis=0, concat_axis=0, tiled=True)
    logits, deltas = shared
    if images == 8:
        feature_weight_grad = from_bins(after(bits, folded), 0, kept_a, arrived_a, last_a, None, features, 8)
        small = small_last(after(me_list, feature_weight_grad), small, arrived_small, hidden)
        sums = small[3:]
        feature_weight_grad = from_bins(after(bits, small[0]), 1, kept_b, arrived_b, last_b, feature_weight_grad, features, 8)
        me_list = after(me_list, feature_weight_grad)
    pyramid_grad = unpack(me_list, image_size, parts, 0)
    pyramid_grad = pyramid_grad.reshape(1, 1, GRID, GRID, CHANNELS)

    if images != 8:
        small, small_away = [jnp.concatenate([a, b], axis=0) for a, b in zip(small_a, small_b)]
        notes = small[:, hidden // 8 :].astype(jnp.float32)
        sums = (notes[:, 0:2] + notes[:, 2:4]).reshape(sections, -1)
        sums = lax.psum(sums, "img")
        small = jnp.concatenate([small[:, : hidden // 8], small_away[:, : hidden // 8]], axis=1)
        small = lax.psum_scatter(small, "img", scatter_dimension=1, tiled=True).astype(jnp.float32)
        small = (small[:, :, :hidden], small[:, :, hidden : hidden + CLASSES], small[:, :, hidden + OUTER : hidden + OUTER + DELTAS])
        at = 2 * hidden
        sums = (sums[:, :hidden], sums[:, hidden:at], sums[:, at : at + CLASSES], sums[:, at + OUTER : at + OUTER + DELTAS])
    return (
        logits,
        deltas,
        pyramid_grad,
        feature_weight_grad,
        sums[0],
        small[0],
        sums[1],
        small[1],
        sums[2],
        small[2],
        sums[3],
    )


def solution(mesh):
    return jax.shard_map(
        body,
        mesh=mesh,
        in_specs=(
            P("img", "lvl", None, None, None),
            P("img", None),
            P(None, None, ("img", "lvl")),
            P(None, ("img", "lvl")),
            P(None, ("img", "lvl")),
            P(None, None, ("img", "lvl")),
            P(None, "lvl", None),
            P(),
            P(),
            P(),
            P(),
            P(),
            P(),
            P(),
        ),
        out_specs=(
            P(None, ("img", "lvl"), None),
            P(None, ("img", "lvl"), None),
            P("img", "lvl", None, None, None),
            P(None, "lvl", "img"),
            P(),
            P(None, ("img", "lvl"), None),
            P(),
            P(None, ("img", "lvl"), None),
            P(),
            P(None, ("img", "lvl"), None),
            P(),
        ),
        check_vma=False,
    )
```

```python
import jax
import jax.numpy as jnp
from jax import lax
from jax.experimental import pallas as pl
from jax.experimental.pallas import tpu as pltpu
from jax.sharding import PartitionSpec as P

CHANNELS = 256
CLASSES = 81
POOL = 7
GRID = 64
DELTAS = 320

WIDTH = 80
ROWS = 140
BASES = (1, 66, 99, 116)
CELLS = ROWS * WIDTH
LANES = 128
WIDE = 3200
EXTRA = 16
FINE = 2048
NOTES = FINE + 3 * 512
BUFFER = NOTES + 4 * 32
UNROLL = 64


def cost(microseconds):
    return pl.CostEstimate(flops=int(microseconds * SCALE * 1_150_000_000), bytes_accessed=0, transcendentals=0)


def in_hbm(array):
    return pltpu.with_memory_space_constraint(array, pltpu.HBM)


def params(mebibytes):
    return pltpu.CompilerParams(vmem_limit_bytes=mebibytes << 20)


SCALE = 1.0


def low_half(rows):
    return lax.broadcasted_iota(jnp.int32, (rows, LANES), 1) < 64


def tent(position, step, cell):
    first = jnp.maximum(1.0 - jnp.abs(position - cell), 0.0)
    second = jnp.maximum(1.0 - jnp.abs(position + step - cell), 0.0)
    return ((first + second) * 0.5).astype(jnp.bfloat16).astype(jnp.float32)


def place_rows(maps, upper, lower, upper_row, lower_row, cells):
    low = low_half(8)
    tiles = cells // 8
    zero = jnp.zeros((8, LANES), jnp.float32)
    values = [upper[8 * t : 8 * t + 8] for t in range(tiles)]
    turned = [pltpu.roll(v, 64, 1) for v in values]
    for t in range(-1, tiles):
        here, here_turned = (values[t], turned[t]) if t >= 0 else (zero, zero)
        after, after_turned = (values[t + 1], turned[t + 1]) if t + 1 < tiles else (zero, zero)
        maps[pl.ds(upper_row * WIDTH + 8 + 8 * t, 8), :] = jnp.where(low, here, after_turned)
        maps[pl.ds(lower_row * WIDTH + 8 + 8 * t, 8), :] = jnp.where(low, here_turned, after)


def fill_maps(maps, levels_ref):
    zero = jnp.zeros((8, LANES), jnp.float32)
    for row in (0, BASES[1] - 1):
        for t in range(WIDTH // 8):
            maps[pl.ds(row * WIDTH + 8 * t, 8), :] = zero

    def clear_edge(y, carry):
        maps[pl.ds(pl.multiple_of((BASES[0] + y) * WIDTH + WIDTH - 8, 8), 8), :] = zero
        return carry

    lax.fori_loop(0, GRID, clear_edge, 0, unroll=8)

    def clear(t, carry):
        maps[pl.ds(pl.multiple_of(BASES[1] * WIDTH + t * 160, 160), 160), :] = jnp.zeros((160, LANES), jnp.float32)
        return carry

    lax.fori_loop(0, (ROWS - BASES[1]) * WIDTH // 160, clear, 0, unroll=2)

    def fine_row(y, carry):
        row = levels_ref[0, pl.ds(pl.multiple_of(y * 64, 64), 64), :].astype(jnp.float32)
        place_rows(maps, row, row, BASES[0] + y, BASES[0] + 32 + y, 64)
        return carry

    lax.fori_loop(0, 32, fine_row, 0, unroll=4)
    for level, cells in ((1, 32), (2, 16), (3, 8)):
        for y in range(cells // 2 if level == 1 else cells):
            row = levels_ref[0, pl.ds(FINE + (level - 1) * 512 + y * 32, 32), :].astype(jnp.float32)[:cells]
            if level == 1:
                place_rows(maps, row, row, BASES[1] + y, BASES[1] + 16 + y, 32)
            else:
                place_upper(maps, row, BASES[level] + y, cells)


def place_upper(maps, row, at, cells):
    low = low_half(8)
    tiles = cells // 8
    zero = jnp.zeros((8, LANES), jnp.float32)
    values = [row[8 * t : 8 * t + 8] for t in range(tiles)]
    for t in range(-1, tiles):
        here = values[t] if t >= 0 else zero
        after = pltpu.roll(values[t + 1], 64, 1) if t + 1 < tiles else zero
        maps[pl.ds(at * WIDTH + 8 + 8 * t, 8), :] = jnp.where(low, here, after)


def crop_kernel(table_ref, levels_ref, out_ref, slab, maps, section):
    rb = out_ref.shape[0]
    base = pl.program_id(0) * rb

    @pl.when(pl.program_id(0) == 0)
    def _():
        fill_maps(maps, levels_ref)

    low = low_half(8)
    lane = lax.broadcasted_iota(jnp.int32, (8, LANES), 1)
    bins = (2 * lax.broadcasted_iota(jnp.int32, (8, LANES), 0)).astype(jnp.float32)
    lane_y = (lane // 8).astype(jnp.float32)
    lane_x = (lane % 8).astype(jnp.float32)

    def one(r):
        start = table_ref[section, 0, base + r].astype(jnp.int32)
        y_at, y_step, x_at, x_step = [table_ref[section, 1 + j, base + r] for j in range(4)]
        window = jnp.concatenate([maps[pl.ds(start + WIDTH * j, 8), :] for j in range(16)], axis=0)
        wy = tent(y_at + y_step * bins, y_step, lane_y)
        x_position = x_at + x_step * bins
        wx = [tent(x_position, x_step, lane_x + 8.0 * h) for h in range(2)]
        rows = [jnp.broadcast_to(wy[b : b + 1], (8, LANES)) for b in range(POOL)]
        weight = jnp.concatenate([rows[b] * wx[h] for h in range(2) for b in range(POOL)], axis=0)
        both = jnp.dot(weight.astype(jnp.bfloat16), window.astype(jnp.bfloat16), preferred_element_type=jnp.float32)
        near = [both[8 * b : 8 * b + 8] for b in range(POOL)]
        far = [both[56 + 8 * b : 64 + 8 * b] for b in range(POOL)]
        zero = jnp.zeros((8, LANES), jnp.float32)
        for i in range(4):
            near_odd, far_odd = (near[2 * i + 1], far[2 * i + 1]) if i < 3 else (zero, zero)
            pair = jnp.where(low, near[2 * i], far_odd) + pltpu.roll(jnp.where(low, near_odd, far[2 * i]), 64, 1)
            slab[pl.ds(i * 8 * rb + r, 8, stride=rb), :] = pair

    def step(t, carry):
        for u in range(UNROLL):
            one(t * UNROLL + u)
        return carry

    lax.fori_loop(0, rb // UNROLL, step, 0)
    for i in range(3):
        for e in range(POOL):
            out_ref[:, pl.ds((7 * i + e) * LANES, LANES)] = slab[pl.ds((8 * i + e) * rb, rb), :].astype(jnp.bfloat16)
    for j in range(4):
        first = slab[pl.ds((24 + 2 * j) * rb, rb), :]
        if j < 3:
            second = slab[pl.ds((25 + 2 * j) * rb, rb), :]
            joined = jnp.where(low_half(rb), first, pltpu.roll(second, 64, 1))
            out_ref[:, pl.ds((21 + j) * LANES, LANES)] = joined.astype(jnp.bfloat16)
        else:
            out_ref[:, pl.ds(24 * LANES, LANES)] = jnp.where(low_half(rb), first, 0.0).astype(jnp.bfloat16)


def crop(table, section, levels, micros, block=128):
    count = table.shape[2]
    return pl.pallas_call(
        lambda *refs: crop_kernel(*refs, section),
        grid=(count // block,),
        in_specs=[pl.BlockSpec(memory_space=pltpu.SMEM), pl.BlockSpec(memory_space=pltpu.VMEM)],
        out_specs=pl.BlockSpec((block, WIDE), lambda g: (g, 0)),
        scratch_shapes=[pltpu.VMEM((32 * block, LANES), jnp.float32), pltpu.VMEM((CELLS, LANES), jnp.float32)],
        out_shape=jax.ShapeDtypeStruct((count, WIDE), jnp.bfloat16),
        cost_estimate=cost(micros),
        compiler_params=params(13),
    )(table, levels)


def spread_kernel(table_ref, first_ref, second_ref, out_ref, slab, sums, fine, coarse, sems):
    rb = slab.shape[0] // 32
    steps = pl.num_programs(0) // 2
    section = pl.program_id(0) // steps
    base = (pl.program_id(0) % steps) * rb

    @pl.when(pl.program_id(0) == 0)
    def _():
        def clear(t, carry):
            sums[pl.ds(pl.multiple_of(t * 160, 160), 160), :] = jnp.zeros((160, LANES), jnp.float32)
            return carry

        lax.fori_loop(0, CELLS // 160, clear, 0, unroll=2)
        for i in range(4):
            slab[pl.ds((8 * i + 7) * rb, rb), :] = jnp.zeros((rb, LANES), jnp.float32)

    def lay_out(grads):
        grads_ref = grads.at[pl.ds(pl.multiple_of(base, rb), rb), :]
        for i in range(3):
            for e in range(POOL):
                slab[pl.ds((8 * i + e) * rb, rb), :] = grads_ref[:, pl.ds((7 * i + e) * LANES, LANES)].astype(jnp.float32)
        for j in range(4):
            pair = grads_ref[:, pl.ds((21 + j) * LANES, LANES)].astype(jnp.float32)
            slab[pl.ds((24 + 2 * j) * rb, rb), :] = pair
            if j < 3:
                slab[pl.ds((25 + 2 * j) * rb, rb), :] = pltpu.roll(pair, 64, 1)

    @pl.when(section == 0)
    def _():
        lay_out(first_ref)

    @pl.when(section == 1)
    def _():
        lay_out(second_ref)

    low = low_half(8)
    lane = lax.broadcasted_iota(jnp.int32, (8, LANES), 1)
    row = lax.broadcasted_iota(jnp.int32, (8, LANES), 0).astype(jnp.float32)
    bins_y = (2 * ((lane // 8) % 8)).astype(jnp.float32)
    bins_x = (2 * (lane % 8)).astype(jnp.float32)
    cell_x = row + 8.0 * (lane // 64).astype(jnp.float32)

    def one(r):
        start = table_ref[section, 0, base + r].astype(jnp.int32)
        y_at, y_step, x_at, x_step = [table_ref[section, 1 + j, base + r] for j in range(4)]
        y_position = y_at + y_step * bins_y
        wy = [tent(y_position, y_step, row + 8.0 * h) for h in range(2)]
        wx = tent(x_at + x_step * bins_x, x_step, cell_x)
        rows = [jnp.broadcast_to(wy[y // 8][y % 8 : y % 8 + 1], (8, LANES)) for y in range(16)]
        weight = jnp.concatenate([rows[y] * wx for y in range(16)], axis=0)
        near, far = [], []
        for i in range(4):
            pair = slab[pl.ds(i * 8 * rb + r, 8, stride=rb), :]
            turned = pltpu.roll(pair, 64, 1)
            zero = jnp.zeros_like(pair)
            near.append(jnp.where(low, pair, zero))
            far.append(jnp.where(low, zero, turned))
            near.append(jnp.where(low, turned, zero) if i < 3 else zero)
            far.append(jnp.where(low, zero, pair) if i < 3 else zero)
        grads = jnp.concatenate(near + far, axis=0)
        out = jnp.dot(weight.astype(jnp.bfloat16), grads.astype(jnp.bfloat16), preferred_element_type=jnp.float32)
        for j in range(16):
            sums[pl.ds(start + WIDTH * j, 8), :] += out[8 * j : 8 * j + 8]

    def step(t, carry):
        for u in range(UNROLL):
            one(t * UNROLL + u)
        return carry

    lax.fori_loop(0, rb // UNROLL, step, 0)

    @pl.when(pl.program_id(0) == pl.num_programs(0) - 1)
    def _():
        def gather(upper_row, lower_row, cells):
            tiles = []
            for t in range(cells // 8):
                up, up_far = [sums[pl.ds(upper_row * WIDTH + 8 * t + s, 8), :] for s in (8, 0)]
                down, down_far = [sums[pl.ds(lower_row * WIDTH + 8 * t + s, 8), :] for s in (8, 0)]
                tiles.append(jnp.where(low, up, down_far) + pltpu.roll(jnp.where(low, down, up_far), 64, 1))
            return jnp.concatenate(tiles, axis=0)

        def fine_row(y, carry):
            here = pl.ds(pl.multiple_of(y * 64, 64), 64)
            fine[here, :] = gather(BASES[0] + y, BASES[0] + 32 + y, 64).astype(jnp.bfloat16)
            return carry

        lax.fori_loop(0, 32, fine_row, 0, unroll=4)
        fine_copy = pltpu.make_async_copy(fine, out_ref.at[0], sems.at[0])
        fine_copy.start()
        coarse[...] = jnp.zeros_like(coarse)
        for y in range(16):
            coarse[0, pl.ds(32 * y, 32), :] = gather(BASES[1] + y, BASES[1] + 16 + y, 32).astype(jnp.bfloat16)
        for level, cells in ((2, 16), (3, 8)):
            for y in range(cells):
                tile = gather(BASES[level] + y, BASES[level] + y, cells)
                tile = jnp.where(low_half(cells), tile, 0.0)
                if cells < 16:
                    tile = jnp.concatenate([tile, jnp.zeros_like(tile)], axis=0)
                coarse[level - 1, pl.ds(32 * y, 16), :] = tile.astype(jnp.bfloat16)
        coarse_copy = pltpu.make_async_copy(coarse, out_ref.at[pl.ds(1, 3), pl.ds(0, 512), :], sems.at[1])
        coarse_copy.start()
        fine_copy.wait()
        coarse_copy.wait()


def spread(table, first, second, micros, block=128):
    steps = first.shape[0] // block
    return pl.pallas_call(
        spread_kernel,
        grid=(2 * steps,),
        in_specs=[pl.BlockSpec(memory_space=pltpu.SMEM)] + [pl.BlockSpec(memory_space=pltpu.VMEM)] * 2,
        out_specs=pl.BlockSpec(memory_space=pltpu.HBM),
        scratch_shapes=[
            pltpu.VMEM((32 * block, LANES), jnp.float32),
            pltpu.VMEM((CELLS, LANES), jnp.float32),
            pltpu.VMEM((FINE, LANES), jnp.bfloat16),
            pltpu.VMEM((3, 512, LANES), jnp.bfloat16),
            pltpu.SemaphoreType.DMA((2,)),
        ],
        out_shape=pltpu.HBM((4, FINE, LANES), jnp.bfloat16),
        cost_estimate=cost(micros),
        compiler_params=params(16),
    )(table, first, second)


def bin_order():
    pairs = [(2 * i + p) * POOL + e for i in range(3) for e in range(POOL) for p in range(2)]
    return pairs + [6 * POOL + e for e in range(POOL)]


def write_note(boxes_ref, routes_ref, labels_ref, targets_ref, image_ref):
    halves = []
    for s in range(2):
        boxes = boxes_ref[s]
        high = jnp.right_shift(boxes, 6)
        rest = targets_ref[s]
        parts = [high.astype(jnp.float32), (boxes - 64 * high).astype(jnp.float32)]
        parts += [routes_ref[s : s + 1].astype(jnp.float32), labels_ref[s : s + 1].astype(jnp.float32)]
        for _ in range(3):
            part = rest.astype(jnp.bfloat16).astype(jnp.float32)
            parts.append(part)
            rest = rest - part
        parts += [jnp.full((1, 64), image_ref[0, j], jnp.int32).astype(jnp.float32) for j in range(2)]
        halves.append(jnp.concatenate(parts + [jnp.zeros((8, 64), jnp.float32)], axis=0))
    return jnp.concatenate(halves, axis=1).astype(jnp.bfloat16)


def decode(notes, info_ref, table_ref):
    notes = [n.astype(jnp.float32) for n in notes]
    for s in range(2):
        rows = jnp.concatenate([n[:, 64 * s : 64 * s + 64] for n in notes], axis=1)
        boxes_float = rows[:4] * 64.0 + rows[4:8]
        targets = (rows[10:14] + rows[14:18]) + rows[18:22]
        pad = jnp.zeros((6, rows.shape[1]), jnp.float32)
        info_ref[s] = jnp.concatenate([boxes_float, rows[8:10], targets, pad], axis=0)
        boxes = boxes_float.astype(jnp.int32)
        route = rows[8:9].astype(jnp.int32)
        sizes = rows[22:24].astype(jnp.int32) * 16
        lines = []
        for axis in range(2):
            limit = sizes[axis : axis + 1]
            low_edge = jnp.minimum(jnp.maximum(boxes[axis : axis + 1], 0), limit)
            high_edge = jnp.minimum(jnp.maximum(boxes[axis + 2 : axis + 3], 0), limit)
            stride = jnp.left_shift(4, route)
            first = 28 * low_edge + (high_edge - low_edge) - 224 * stride
            cell = jnp.right_shift((jnp.right_shift(first, 8 + route) + 7) * 9363, 16) - 1
            units = 448 * stride
            scale = 1.0 / units.astype(jnp.float32)
            lines.append((cell, (first - cell * units).astype(jnp.float32) * scale, (2 * (high_edge - low_edge)).astype(jnp.float32) * scale))
        row = jnp.where(route == 0, BASES[0], jnp.where(route == 1, BASES[1], jnp.where(route == 2, BASES[2], BASES[3])))
        start = (row + lines[0][0]) * WIDTH + 8 + lines[1][0]
        parts = [start.astype(jnp.float32), lines[0][1], lines[0][2], lines[1][1], lines[1][2]]
        table_ref[s] = jnp.concatenate(parts + [jnp.zeros((3, rows.shape[1]), jnp.float32)], axis=0)


TABLES = [jax.ShapeDtypeStruct((2, 16, 256), jnp.float32), jax.ShapeDtypeStruct((2, 8, 256), jnp.float32)]


def arrange_kernel(
    slot_ref, own_ref, one_ref, two_ref, three_ref, near_ref, core_ref, chip_ref, far_ref,
    levels_ref, info_ref, table_ref, coarse_ref,
):
    slot, me = 0, slot_ref[6]
    for k, ref in enumerate((near_ref, core_ref, chip_ref, far_ref)):
        coarse_ref[jnp.bitwise_xor(me, k)] = ref[...]
    fine = own_ref[...] + one_ref[...] + two_ref[...] + three_ref[...]
    levels_ref[slot, pl.ds(0, FINE), :] = fine.reshape(FINE, LANES)
    for level in range(1, 4):
        levels_ref[slot, pl.ds(FINE + (level - 1) * 512, 512), :] = coarse_ref[level, pl.ds(0, 512), :]
    for d in range(4):
        levels_ref[slot, pl.ds(NOTES + 32 * d, 32), :] = coarse_ref[d, pl.ds(512, 32), :]
    decode([coarse_ref[d, pl.ds(512, 32), :] for d in range(4)], info_ref, table_ref)


def arrange(slot, slots, own, arrived, coarse):
    vmem = pl.BlockSpec(memory_space=pltpu.VMEM)
    return pl.pallas_call(
        arrange_kernel,
        in_specs=[pl.BlockSpec(memory_space=pltpu.SMEM)] + [vmem] * 8,
        out_shape=[jax.ShapeDtypeStruct((slots, BUFFER, LANES), jnp.bfloat16)] + TABLES,
        scratch_shapes=[pltpu.VMEM((4, 544, LANES), jnp.bfloat16)],
        cost_estimate=cost(2),
        compiler_params=params(7),
    )(slot, own, *arrived, *coarse)


def prepare_kernel(slot_ref, levels_ref, info_ref, table_ref):
    del slot_ref
    slot = 0
    decode([levels_ref[slot, pl.ds(NOTES + 32 * d, 32), :] for d in range(4)], info_ref, table_ref)


def prepare(slot, levels):
    vmem = pl.BlockSpec(memory_space=pltpu.VMEM)
    return pl.pallas_call(
        prepare_kernel,
        in_specs=[pl.BlockSpec(memory_space=pltpu.SMEM), vmem],
        out_shape=TABLES,
        cost_estimate=cost(1),
    )(slot, levels)[1]


def valid_edges(owner, image_ref):
    shift = 2 + owner
    round_up = jnp.left_shift(1, shift) - 1
    return [jnp.right_shift(image_ref[0, j] + round_up, shift) for j in range(2)]


def pack_kernel(
    owner_ref, image_ref, upper_ref, lower_ref, small_ref, boxes_hbm, routes_hbm, labels_hbm, targets_hbm,
    own_ref, one_ref, two_ref, three_ref, near_ref, core_ref, chip_ref, far_ref,
    boxes_ref, routes_ref, labels_ref, targets_ref, sems, coarse_ref,
):
    g = pl.program_id(0)
    owner = owner_ref[6]
    rows_valid, cols_valid = valid_edges(owner, image_ref)
    pairs = ((boxes_hbm, boxes_ref), (routes_hbm, routes_ref), (labels_hbm, labels_ref), (targets_hbm, targets_ref))
    copies = [pltpu.make_async_copy(a, b, sems.at[j]) for j, (a, b) in enumerate(pairs)]

    @pl.when(g == 0)
    def _():
        for copy in copies:
            copy.start()

    cell = lax.broadcasted_iota(jnp.int32, (GRID, LANES), 0)
    low = low_half(GRID)
    outs = (own_ref, one_ref, two_ref, three_ref)
    for y in range(upper_ref.shape[2]):
        top = (cell < cols_valid) & (g * upper_ref.shape[2] + y < rows_valid)
        bottom = (cell < cols_valid) & (32 + g * upper_ref.shape[2] + y < rows_valid)
        for c in range(2):
            a = jnp.where(top, upper_ref[0, 0, y, :, pl.ds(LANES * c, LANES)].astype(jnp.float32), 0.0)
            b = jnp.where(bottom, lower_ref[0, 0, y, :, pl.ds(LANES * c, LANES)].astype(jnp.float32), 0.0)
            even = jnp.where(low, a, pltpu.roll(b, 64, 1))
            if c == 0:
                even = jnp.where(owner == 0, even, 0.0)
            outs[2 * c][y] = even.astype(jnp.bfloat16)
            outs[2 * c + 1][y] = jnp.where(low, pltpu.roll(a, 64, 1), b).astype(jnp.bfloat16)

    @pl.when(g == 0)
    def _():
        low = low_half(32)
        cell = lax.broadcasted_iota(jnp.int32, (32, LANES), 0)
        for y in range(16):
            top = (cell < cols_valid) & (y < rows_valid)
            bottom = (cell < cols_valid) & (16 + y < rows_valid) & (owner < 2)
            for c in range(2):
                a = jnp.where(top, small_ref[0, 0, y, pl.ds(0, 32), pl.ds(LANES * c, LANES)].astype(jnp.float32), 0.0)
                b = jnp.where(bottom, small_ref[0, 0, 16 + y, pl.ds(0, 32), pl.ds(LANES * c, LANES)].astype(jnp.float32), 0.0)
                here = pl.ds(32 * y, 32)
                coarse_ref[2 * c, here, :] = jnp.where(low, a, pltpu.roll(b, 64, 1)).astype(jnp.bfloat16)
                coarse_ref[2 * c + 1, here, :] = jnp.where(low, pltpu.roll(a, 64, 1), b).astype(jnp.bfloat16)
        for copy in copies:
            copy.wait()
        note = write_note(boxes_ref, routes_ref, labels_ref, targets_ref, image_ref)
        for d in range(4):
            coarse_ref[d, pl.ds(512, 32), :] = note
        for k, ref in enumerate((near_ref, core_ref, chip_ref, far_ref)):
            ref[...] = coarse_ref[jnp.bitwise_xor(owner, k)]


def pack(owner, image_size, pyramid, boxes, routes, labels, targets):
    regions = (boxes, routes, labels, targets)
    return pl.pallas_call(
        pack_kernel,
        grid=(4,),
        in_specs=[
            pl.BlockSpec(memory_space=pltpu.SMEM),
            pl.BlockSpec(memory_space=pltpu.SMEM),
            pl.BlockSpec((1, 1, 8, GRID, CHANNELS), lambda g: (0, 0, g, 0, 0)),
            pl.BlockSpec((1, 1, 8, GRID, CHANNELS), lambda g: (0, 0, g + 4, 0, 0)),
            pl.BlockSpec((1, 1, 32, GRID, CHANNELS), lambda g: (0, 0, 0, 0, 0)),
        ]
        + [pl.BlockSpec(memory_space=pltpu.HBM)] * 4,
        out_specs=[pl.BlockSpec((8, GRID, LANES), lambda g: (g, 0, 0))] * 4
        + [pl.BlockSpec((544, LANES), lambda g: (0, 0))] * 4,
        scratch_shapes=[pltpu.VMEM(v.shape, v.dtype) for v in regions]
        + [pltpu.SemaphoreType.DMA((4,)), pltpu.VMEM((4, 544, LANES), jnp.bfloat16)],
        out_shape=[jax.ShapeDtypeStruct((32, GRID, LANES), jnp.bfloat16)] * 4
        + [jax.ShapeDtypeStruct((544, LANES), jnp.bfloat16)] * 4,
        cost_estimate=cost(2.7),
        compiler_params=params(8),
    )(owner, in_hbm(image_size), *[in_hbm(pyramid)] * 3, *[in_hbm(v) for v in regions])


def unpack_kernel(owner_ref, image_ref, fine_ref, coarse_ref, out_ref):
    g = pl.program_id(0)
    owner = owner_ref[6]
    rows_valid, cols_valid = valid_edges(owner, image_ref)
    count = out_ref.shape[1]

    @pl.when(owner == 0)
    def _():
        cell = lax.broadcasted_iota(jnp.int32, (GRID, LANES), 0)
        low = low_half(GRID)
        for y in range(count):
            top = (cell < cols_valid) & (g * count + y < rows_valid)
            bottom = (cell < cols_valid) & (32 + g * count + y < rows_valid)
            for c in range(2):
                a = fine_ref[2 * c, pl.ds(y * GRID, GRID), :].astype(jnp.float32)
                b = fine_ref[2 * c + 1, pl.ds(y * GRID, GRID), :].astype(jnp.float32)
                upper = jnp.where(low, a, pltpu.roll(b, 64, 1))
                lower = jnp.where(low, pltpu.roll(a, 64, 1), b)
                out_ref[0, y, :, pl.ds(LANES * c, LANES)] = jnp.where(top, upper, 0.0).astype(jnp.bfloat16)
                out_ref[1, y, :, pl.ds(LANES * c, LANES)] = jnp.where(bottom, lower, 0.0).astype(jnp.bfloat16)

    @pl.when(owner != 0)
    def _():
        out_ref[...] = jnp.zeros_like(out_ref)
        cell = lax.broadcasted_iota(jnp.int32, (32, LANES), 0)
        low = low_half(32)
        for y in range(count):
            top = (cell < cols_valid) & (g * count + y < rows_valid)
            line = pl.ds(pl.multiple_of(((g % 2) * count + y) * 32, 32), 32)
            for c in range(2):
                a = coarse_ref[2 * c, line, :].astype(jnp.float32)
                b = coarse_ref[2 * c + 1, line, :].astype(jnp.float32)
                upper = jnp.where(low, a, pltpu.roll(b, 64, 1))
                lower = jnp.where(low, pltpu.roll(a, 64, 1), b)
                row = jnp.where(g < 2, upper, lower)
                out_ref[0, y, pl.ds(0, 32), pl.ds(LANES * c, LANES)] = jnp.where(top, row, 0.0).astype(jnp.bfloat16)


def unpack(owner, image_size, parts, micros):
    return pl.pallas_call(
        unpack_kernel,
        grid=(4,),
        in_specs=[pl.BlockSpec(memory_space=pltpu.SMEM)] * 2
        + [pl.BlockSpec((4, 512, LANES), lambda g: (0, g, 0)), pl.BlockSpec((4, 512, LANES), lambda g: (0, 0, 0))],
        out_specs=pl.BlockSpec((2, 8, GRID, CHANNELS), lambda g: (0, g, 0, 0)),
        out_shape=jax.ShapeDtypeStruct((2, 32, GRID, CHANNELS), jnp.bfloat16),
        cost_estimate=cost(micros),
        compiler_params=params(7),
    )(owner, image_size, parts, parts)


def to_bins_kernel(order_ref, weight_ref, out_ref, arrived, rows, sems, section):
    del order_ref
    taken = arrived.shape[1]
    blocks = weight_ref.shape[1] // taken

    def fetch(c):
        slot = c % 2
        return pltpu.make_async_copy(weight_ref.at[section, pl.ds(c * taken, taken), :], arrived.at[slot], sems.at[slot])

    fetch(0).start()
    fetch(1).start()

    def step(c, carry):
        fetch(c).wait()
        for t in range(rows.shape[0]):
            rows[t] = arrived[c % 2, :, pl.ds(t * LANES, LANES)].astype(jnp.float32)

        @pl.when(c + 2 < blocks)
        def _():
            fetch(c + 2).start()

        here = pl.ds(pl.multiple_of(c * 16, 16), 16)
        for place, source in enumerate(bin_order()):
            for t in range(rows.shape[0]):
                out_ref[place, here, pl.ds(t * LANES, LANES)] = rows[t, pl.ds(source, 16, stride=49), :].astype(jnp.bfloat16)
        return carry

    lax.fori_loop(0, blocks, step, 0)
    out_ref[49] = jnp.zeros(out_ref.shape[1:], jnp.bfloat16)


def to_bins(order, weight, section, micros):
    rows, width = weight.shape[1:]
    channels = rows // 49
    return pl.pallas_call(
        lambda *refs: to_bins_kernel(*refs, section),
        in_specs=[pl.BlockSpec(memory_space=pltpu.SMEM), pl.BlockSpec(memory_space=pltpu.HBM)],
        out_specs=pl.BlockSpec(memory_space=pltpu.VMEM),
        out_shape=jax.ShapeDtypeStruct((50, channels, width), jnp.bfloat16),
        scratch_shapes=[
            pltpu.VMEM((2, 784, width), jnp.bfloat16),
            pltpu.VMEM((width // LANES, 784, LANES), jnp.float32),
            pltpu.SemaphoreType.DMA((2,)),
        ],
        cost_estimate=cost(micros),
        compiler_params=params(8),
    )(order, in_hbm(weight)).reshape(WIDE, width)


def first_kernel(pooled_ref, weight_ref, out_ref):
    for n in range(0, out_ref.shape[1], 256):
        here = pl.ds(n, 256)
        out_ref[:, here] = jnp.dot(pooled_ref[...], weight_ref[:, here], preferred_element_type=jnp.float32).astype(jnp.bfloat16)


def first_product(pooled, weight, micros):
    vmem = pl.BlockSpec(memory_space=pltpu.VMEM)
    return pl.pallas_call(
        first_kernel,
        in_specs=[vmem, vmem],
        out_specs=vmem,
        out_shape=jax.ShapeDtypeStruct((pooled.shape[0], weight.shape[1]), jnp.bfloat16),
        cost_estimate=cost(micros),
        compiler_params=params(6),
    )(pooled, weight)


def back_kernel(order_ref, grads_ref, weight_ref, out_ref):
    del order_ref
    for n in range(0, WIDE, 640):
        here = pl.ds(n, 640)
        value = lax.dot_general(grads_ref[...], weight_ref[here, :], NT, preferred_element_type=jnp.float32)
        out_ref[:, here] = value.astype(jnp.bfloat16)


def back_product(order, grads, weight, micros):
    vmem = pl.BlockSpec(memory_space=pltpu.VMEM)
    return pl.pallas_call(
        back_kernel,
        in_specs=[pl.BlockSpec(memory_space=pltpu.SMEM), vmem, vmem],
        out_specs=vmem,
        out_shape=jax.ShapeDtypeStruct((grads.shape[0], WIDE), jnp.bfloat16),
        cost_estimate=cost(micros),
        compiler_params=params(6),
    )(order, grads, weight)


SPLIT = 2176
TAIL = WIDE - SPLIT


def outer_kernel(bits_ref, own, cross, own_pooled, cross_pooled, sent_one, kept_one, sent_two, kept_two):
    rows = own.shape[2]

    def product(pick, at, width, out):
        mine, theirs = [pick(ref).reshape(2 * rows, -1) for ref in (own, cross)]
        for n in range(0, width, 256):
            wide = min(256, width - n)
            here = pl.ds(at + n, wide)
            value = jnp.dot(mine, own_pooled[:, here], preferred_element_type=jnp.float32)
            value = value + jnp.dot(theirs, cross_pooled[:, here], preferred_element_type=jnp.float32)
            out[:, :, pl.ds(n, wide)] = value.astype(out.dtype).reshape(2, rows, wide)

    product(lambda ref: ref[:, bits_ref[1]], 0, SPLIT, sent_one)
    product(lambda ref: ref[bits_ref[3]], SPLIT, TAIL, sent_two)
    product(lambda ref: ref[:, bits_ref[0]], 0, SPLIT, kept_one)
    product(lambda ref: ref[bits_ref[2]], SPLIT, TAIL, kept_two)


def outer_sums(bits, own, cross, own_pooled, cross_pooled, micros):
    rows = own.shape[2]
    vmem = pl.BlockSpec(memory_space=pltpu.VMEM)
    kinds = [(width, jnp.bfloat16) for width in (SPLIT, TAIL) for _ in range(2)]
    return pl.pallas_call(
        outer_kernel,
        in_specs=[pl.BlockSpec(memory_space=pltpu.SMEM)] + [vmem] * 4,
        out_specs=[vmem] * 4,
        out_shape=[jax.ShapeDtypeStruct((2, rows, width), dtype) for width, dtype in kinds],
        cost_estimate=cost(micros),
        compiler_params=params(6),
    )(bits, own, cross, own_pooled, cross_pooled)


def fold_kernel(bits_ref, kept_one, arrived_one, kept_two, arrived_two, one_ref, two_ref):
    up, low = bits_ref[3], bits_ref[1]
    one_ref[...] = (kept_one[up].astype(jnp.float32) + arrived_one[up].astype(jnp.float32)).astype(jnp.bfloat16)
    two_ref[...] = (kept_two[low].astype(jnp.float32) + arrived_two[low].astype(jnp.float32)).astype(jnp.bfloat16)


def fold(bits, kept_one, arrived_one, kept_two, arrived_two):
    rows = kept_one.shape[1]
    vmem = pl.BlockSpec(memory_space=pltpu.VMEM)
    return pl.pallas_call(
        fold_kernel,
        in_specs=[pl.BlockSpec(memory_space=pltpu.SMEM)] + [vmem] * 4,
        out_specs=[vmem] * 2,
        out_shape=[jax.ShapeDtypeStruct((rows, SPLIT), jnp.bfloat16), jax.ShapeDtypeStruct((rows, TAIL), jnp.bfloat16)],
        cost_estimate=cost(8),
        compiler_params=params(5),
    )(bits, kept_one, arrived_one, kept_two, arrived_two)


def from_bins_kernel(bits_ref, *refs):
    del bits_ref
    kept_one, arrived_one, last_one, kept_two, arrived_two, last_two = refs[:6]
    out_ref, turned = refs[-2:]
    for kept, arrived, last, at in ((kept_one, arrived_one, last_one, 0), (kept_two, arrived_two, last_two, SPLIT)):
        for t in range(kept.shape[2] // LANES):
            here = pl.ds(t * LANES, LANES)
            value = kept[0, :, here].astype(jnp.float32) + arrived[0, :, here].astype(jnp.float32)
            value = value + last[:, here].astype(jnp.float32)
            turned[pl.ds(at + t * LANES, LANES), :] = jnp.transpose(value, (1, 0))
    for place, source in enumerate(bin_order()):
        out_ref[0, pl.ds(source, 64, stride=49), :] = turned[pl.ds(place * 64, 64), :]


def from_bins(bits, section, kept, arrived, last, before, rows, micros):
    columns = kept[0].shape[1]
    specs = []
    for at, width in ((2, SPLIT), (0, TAIL)):
        both = pl.BlockSpec((1, columns, width), lambda i, b, at=at: (b[at], 0, 0))
        specs += [both, both, pl.BlockSpec((columns, width), lambda i, b: (0, 0))]
    operands = [kept[0], arrived[0], last[0], kept[1], arrived[1], last[1]]
    aliases = {}
    if before is not None:
        specs.append(pl.BlockSpec(memory_space=pl.ANY))
        operands.append(before)
        aliases = {7: 0}
    return pl.pallas_call(
        from_bins_kernel,
        grid_spec=pltpu.PrefetchScalarGridSpec(
            num_scalar_prefetch=1,
            grid=(1,),
            in_specs=specs,
            out_specs=pl.BlockSpec((1, rows, columns), lambda i, b: (section, 0, 0)),
            scratch_shapes=[pltpu.VMEM((WIDE, LANES), jnp.float32)],
        ),
        out_shape=jax.ShapeDtypeStruct((2, rows, columns), jnp.float32),
        input_output_aliases=aliases,
        cost_estimate=cost(micros),
        compiler_params=params(6),
    )(bits, *operands)


def silu_slope(values):
    sigma = jax.nn.sigmoid(values)
    return sigma * (1.0 + values * (1.0 - sigma))


NT = (((1,), (1,)), ((), ()))
TN = (((0,), (0,)), ((), ()))
OUTER = 128


def write_sums(sums, width):
    high = sums.astype(jnp.bfloat16).astype(jnp.float32)
    rows = []
    for part in (high, sums - high):
        rest = part[:, width:]
        if rest.shape[1] < width:
            rest = jnp.concatenate([rest, jnp.zeros((1, width - rest.shape[1]), jnp.float32)], axis=1)
        rows += [part[:, :width], rest]
    return jnp.concatenate(rows + [jnp.zeros((EXTRA - 4, width), jnp.float32)], axis=0).astype(jnp.bfloat16)


def read_sums(note, count):
    note = note.astype(jnp.float32)
    rows = note[0:2] + note[2:4]
    return jnp.concatenate([rows[0:1], rows[1:2]], axis=1)[:, :count]


def head_kernel(
    me_ref, mine_ref, theirs_ref, info_ref, feature_bias_ref, hidden_ref, hidden_bias_ref, class_ref, class_bias_ref,
    delta_ref, delta_bias_ref,
    *refs, images,
):
    logits_ref, deltas_ref, small_ref, small_away_ref, grad_feature_ref, stay_ref, away_ref = refs[-12:-5]
    outer_scr, turned_scr, weight_scr, row_scr, small_scr = refs[-5:]
    me, half = me_ref[6], me_ref[4]
    weight_scr[...] = jnp.zeros_like(weight_scr)
    weight_scr[pl.ds(0, CLASSES), :] = class_ref[0]
    weight_scr[pl.ds(OUTER, DELTAS), :] = delta_ref[0]
    row_scr[...] = jnp.zeros_like(row_scr)
    row_scr[:, pl.ds(0, CLASSES)] = class_bias_ref[0]
    row_scr[:, pl.ds(OUTER, DELTAS)] = delta_bias_ref[0]
    f32 = jnp.float32
    rows, hidden = mine_ref.shape
    pre_feature = mine_ref[...].astype(f32) + theirs_ref[...].astype(f32) + feature_bias_ref[0]
    gate_one = jax.nn.sigmoid(pre_feature)
    hidden_one = (pre_feature * gate_one).astype(jnp.bfloat16)
    pre_hidden = jnp.dot(hidden_one, hidden_ref[0], preferred_element_type=f32) + hidden_bias_ref[0]
    gate_two = jax.nn.sigmoid(pre_hidden)
    hidden_two = (pre_hidden * gate_two).astype(jnp.bfloat16)
    outer = lax.dot_general(hidden_two, weight_scr[...], NT, preferred_element_type=f32) + row_scr[...]
    outer_scr[...] = outer
    own = pl.ds(pl.multiple_of(me * (rows // 4), rows // 4), rows // 4)
    logits_ref[0] = outer_scr[own, pl.ds(0, CLASSES)]
    deltas_ref[0] = outer_scr[own, pl.ds(OUTER, DELTAS)]

    columns = jnp.transpose(info_ref[0], (1, 0))
    label = columns[:, 5:6].astype(jnp.int32)
    lane = lax.broadcasted_iota(jnp.int32, (rows, OUTER), 1)
    logits = jnp.where(lane < CLASSES, outer[:, :OUTER], -jnp.inf)
    shifted = jnp.exp(logits - jnp.max(logits, axis=1, keepdims=True))
    grad_logits = shifted / jnp.sum(shifted, axis=1, keepdims=True) - (lane == label).astype(f32)
    wide = lax.broadcasted_iota(jnp.int32, (rows, outer.shape[1] - OUTER), 1)
    hot = (wide // 4 == label) & (label < CLASSES - 1)
    picked = jnp.where(hot, outer[:, OUTER:], 0.0)
    grad_deltas = jnp.zeros_like(picked)
    for j in range(4):
        mine = wide % 4 == j
        chosen = jnp.sum(jnp.where(mine, picked, 0.0), axis=1, keepdims=True)
        error = jnp.clip(chosen - columns[:, 6 + j : 7 + j], -1.0, 1.0)
        grad_deltas = jnp.where(mine & hot, error, grad_deltas)
    grad_outer = jnp.concatenate([grad_logits, grad_deltas], axis=1).astype(jnp.bfloat16)

    grad_two = jnp.dot(grad_outer, weight_scr[...], preferred_element_type=f32)
    slope_two = gate_two * (1.0 + pre_hidden * (1.0 - gate_two))
    grad_pre_hidden = (grad_two * slope_two).astype(jnp.bfloat16)
    grad_one = lax.dot_general(grad_pre_hidden, hidden_ref[0], NT, preferred_element_type=f32)
    slope_one = gate_one * (1.0 + pre_feature * (1.0 - gate_one))
    grad_feature = grad_one * slope_one
    grad_pre_feature = grad_feature.astype(jnp.bfloat16)
    grad_feature_ref[...] = grad_pre_feature
    turned_scr[...] = jnp.transpose(grad_feature, (1, 0)).astype(jnp.bfloat16)
    stay_ref[...] = turned_scr[pl.ds(pl.multiple_of(half * (hidden // 2), hidden // 2), hidden // 2), :]
    away_ref[...] = turned_scr[pl.ds(pl.multiple_of((1 - half) * (hidden // 2), hidden // 2), hidden // 2), :]

    run = hidden // (4 * images)
    row = lax.broadcasted_iota(jnp.int32, (hidden, hidden // 4), 0)
    col = lax.broadcasted_iota(jnp.int32, (hidden, hidden // 4), 1)
    pick = (row == (col // run) * (4 * run) + me * run + col % run).astype(jnp.bfloat16)
    one_rows = jnp.dot(hidden_one, pick, preferred_element_type=f32).astype(jnp.bfloat16)
    two_rows = jnp.dot(hidden_two, pick, preferred_element_type=f32).astype(jnp.bfloat16)
    small_scr[:, pl.ds(0, hidden)] = lax.dot_general(one_rows, grad_pre_hidden, TN, preferred_element_type=f32).astype(jnp.bfloat16)
    small_scr[:, pl.ds(hidden, outer.shape[1])] = lax.dot_general(two_rows, grad_outer, TN, preferred_element_type=f32).astype(jnp.bfloat16)
    middle = me_ref[2]
    part = small_scr.shape[0] // 2
    if images == 8:
        for j in range(images // 2):
            here = pl.ds(j * run, run)
            for bit, ref in ((middle, small_ref), (1 - middle, small_away_ref)):
                source = (j // 2) * 4 * run + bit * 2 * run + (j % 2) * run
                ref[0, here, :] = small_scr[pl.ds(pl.multiple_of(source, run), run), :]
    else:
        small_ref[0, pl.ds(0, part), :] = small_scr[pl.ds(0, part), :]
        small_away_ref[0, pl.ds(0, part), :] = small_scr[pl.ds(part, part), :]
    sums = [jnp.sum(v.astype(f32), axis=0, keepdims=True) for v in (grad_pre_feature, grad_pre_hidden, grad_outer)]
    sums = jnp.concatenate(sums, axis=1)
    note = write_sums(sums, small_scr.shape[1])
    for ref in (small_ref, small_away_ref):
        ref[0, pl.ds(ref.shape[1] - EXTRA, EXTRA), :] = note


def head(me, mine, theirs, section, stacked, images, before, micros):
    rows, hidden = mine.shape
    width = 512
    sections = stacked[0].shape[0]

    def whole(shape):
        return pl.BlockSpec(shape, lambda g, m: (0,) * len(shape))

    def of_section(array):
        return pl.BlockSpec((1,) + array.shape[1:], lambda g, m: (section, 0, 0))

    def kernel(*refs):
        head_kernel(*refs, images=images)

    shared = [
        jax.ShapeDtypeStruct((sections, rows // 4, CLASSES), jnp.float32),
        jax.ShapeDtypeStruct((sections, rows // 4, DELTAS), jnp.float32),
    ]
    single = [
        pltpu.HBM((1, hidden // 8 + EXTRA, hidden + width), jnp.bfloat16),
        pltpu.HBM((1, hidden // 8 + EXTRA, hidden + width), jnp.bfloat16),
        pltpu.HBM((rows, hidden), jnp.bfloat16),
        jax.ShapeDtypeStruct((hidden // 2, rows), jnp.bfloat16),
        jax.ShapeDtypeStruct((hidden // 2, rows), jnp.bfloat16),
    ]
    return pl.pallas_call(
        kernel,
        grid_spec=pltpu.PrefetchScalarGridSpec(
            num_scalar_prefetch=1,
            grid=(1,),
            in_specs=[whole(mine.shape), whole(theirs.shape)]
            + [of_section(a) for a in stacked]
            + [pl.BlockSpec(memory_space=pl.ANY)] * len(before),
            out_specs=[of_section(o) for o in shared] + [whole(o.shape) for o in single],
            scratch_shapes=[
                pltpu.VMEM((rows, width), jnp.float32),
                pltpu.VMEM((hidden, rows), jnp.bfloat16),
                pltpu.VMEM((width, hidden), jnp.bfloat16),
                pltpu.VMEM((1, width), jnp.float32),
                pltpu.VMEM((hidden // 4, hidden + width), jnp.bfloat16),
            ],
        ),
        out_shape=shared + single,
        input_output_aliases={3 + len(stacked) + j: j for j in range(len(before))},
        cost_estimate=cost(micros),
        compiler_params=params(13),
    )(me, mine, theirs, *stacked, *before)


def pass_sums(s, kept_ref, arrived_ref, refs):
    rows, width = kept_ref.shape[1:]
    notes = [ref[s, pl.ds(rows - EXTRA, EXTRA), :] for ref in (kept_ref, arrived_ref)]
    total = write_sums(read_sums(notes[0], 2 * width) + read_sums(notes[1], 2 * width), width)
    for ref in refs:
        ref[s, pl.ds(ref.shape[1] - EXTRA, EXTRA), :] = total


def small_step_kernel(bits_ref, kept_ref, arrived_ref, stay_ref, away_ref, at):
    sections, rows, width = kept_ref.shape
    run = 32
    for s in range(sections):
        for j in range((rows - EXTRA) // (2 * run)):
            for place, ref in ((bits_ref[at], stay_ref), (bits_ref[at + 1], away_ref)):
                here = pl.ds(pl.multiple_of(j * 2 * run + place * run, run), run)
                value = kept_ref[s, here, :].astype(jnp.float32) + arrived_ref[s, here, :].astype(jnp.float32)
                ref[s, pl.ds(j * run, run), :] = value.astype(jnp.bfloat16)
        pass_sums(s, kept_ref, arrived_ref, (stay_ref, away_ref))


def small_last_kernel(order_ref, kept_ref, arrived_ref, hidden_ref, class_ref, delta_ref, one_ref, two_ref, class_sum_ref, delta_sum_ref):
    del order_ref
    run, hidden = hidden_ref.shape[1:]
    width = kept_ref.shape[2]
    for s in range(kept_ref.shape[0]):
        value = kept_ref[s, pl.ds(0, run), :].astype(jnp.float32) + arrived_ref[s, pl.ds(0, run), :].astype(jnp.float32)
        hidden_ref[s] = value[:, :hidden]
        class_ref[s] = value[:, hidden : hidden + CLASSES]
        delta_ref[s] = value[:, hidden + OUTER : hidden + OUTER + DELTAS]
        sums = read_sums(kept_ref[s, pl.ds(run, EXTRA), :], 2 * width) + read_sums(arrived_ref[s, pl.ds(run, EXTRA), :], 2 * width)
        at = 0
        for ref, step in ((one_ref, hidden), (two_ref, hidden), (class_sum_ref, OUTER), (delta_sum_ref, DELTAS)):
            ref[s : s + 1, :] = sums[:, at : at + ref.shape[1]]
            at += step


def small_join_kernel(bits_ref, *refs):
    outs = refs[4:]
    rows = refs[0].shape[1]
    run = 32
    for s in range(2):
        kept_ref, arrived_ref = refs[s], refs[2 + s]
        count = (rows - EXTRA) // (2 * run)
        for j in range(count):
            for place, ref in ((bits_ref[4], outs[0]), (bits_ref[5], outs[1])):
                here = pl.ds(pl.multiple_of(place * count * run + j * run, run), run)
                value = kept_ref[0, here, :].astype(jnp.float32) + arrived_ref[0, here, :].astype(jnp.float32)
                ref[s, pl.ds(j * run, run), :] = value.astype(jnp.bfloat16)
        notes = [ref[0, pl.ds(rows - EXTRA, EXTRA), :] for ref in (kept_ref, arrived_ref)]
        width = kept_ref.shape[2]
        total = write_sums(read_sums(notes[0], 2 * width) + read_sums(notes[1], 2 * width), width)
        for ref in outs:
            ref[s, pl.ds(ref.shape[1] - EXTRA, EXTRA), :] = total


def small_join(bits, kept, arrived):
    vmem = pl.BlockSpec(memory_space=pltpu.VMEM)
    _, rows, width = kept[0].shape
    return pl.pallas_call(
        small_join_kernel,
        in_specs=[pl.BlockSpec(memory_space=pltpu.SMEM)] + [vmem] * 4,
        out_specs=[vmem] * 2,
        out_shape=[jax.ShapeDtypeStruct((2, (rows - EXTRA) // 2 + EXTRA, width), jnp.bfloat16)] * 2,
        cost_estimate=cost(1),
        compiler_params=params(8),
    )(bits, *kept, *arrived)


def small_step(bits, at, kept, arrived):
    vmem = pl.BlockSpec(memory_space=pltpu.VMEM)
    sections, rows, width = kept.shape
    return pl.pallas_call(
        lambda *refs: small_step_kernel(*refs, at),
        in_specs=[pl.BlockSpec(memory_space=pltpu.SMEM), vmem, vmem],
        out_specs=[vmem] * 2,
        out_shape=[jax.ShapeDtypeStruct((sections, (rows - EXTRA) // 2 + EXTRA, width), jnp.bfloat16)] * 2,
        cost_estimate=cost(1),
        compiler_params=params(8),
    )(bits, kept, arrived)


def small_last(order, kept, arrived, hidden):
    sections, rows, width = kept.shape
    shapes = [(sections, rows - EXTRA, n) for n in (hidden, CLASSES, DELTAS)]
    shapes += [(sections, n) for n in (hidden, hidden, CLASSES, DELTAS)]
    vmem = pl.BlockSpec(memory_space=pltpu.VMEM)
    return pl.pallas_call(
        small_last_kernel,
        in_specs=[pl.BlockSpec(memory_space=pltpu.SMEM), vmem, vmem],
        out_shape=[jax.ShapeDtypeStruct(shape, jnp.float32) for shape in shapes],
        cost_estimate=cost(1),
        compiler_params=params(8),
    )(order, kept, arrived)


def swap(value, axis, bit):
    size = lax.axis_size(axis)
    return lax.ppermute(value, axis, [(i, i ^ bit) for i in range(size)])


def after(value, *others):
    return lax.optimization_barrier((value,) + others)[0]


def choose(array, axis, bit):
    return lax.dynamic_index_in_dim(array, bit, axis, keepdims=False)


def split_bits(array, bits):
    return array.reshape((2,) * bits + (array.shape[0] >> bits,) + array.shape[1:])


def body(
    pyramid,
    image_size,
    region_boxes,
    routes,
    labels,
    targets,
    feature_weight,
    feature_bias,
    hidden_weight,
    hidden_bias,
    class_weight,
    class_bias,
    delta_weight,
    delta_bias,
):
    images = lax.axis_size("img")
    me = lax.axis_index("lvl").astype(jnp.int32)
    image = lax.axis_index("img").astype(jnp.int32)
    sections = routes.shape[0]
    features = feature_weight.shape[1]
    hidden = hidden_weight.shape[2]
    top = images // 2
    steps = images.bit_length() - 2
    half = jnp.minimum(image & top, 1)
    own_bits = [jnp.minimum(image & (1 << b), 1) for b in range(steps)]
    bits = jnp.stack([own_bits[0], 1 - own_bits[0], own_bits[1], 1 - own_bits[1], half, 1 - half, me])
    me_list = bits

    own, *packed = pack(me_list, image_size, pyramid, region_boxes, routes, labels, targets)
    quarters, small = packed[:3], packed[3:]
    arrived = [lax.ppermute(quarters[d], "lvl", [(0, d + 1)]) for d in (1, 2, 0)]
    coarse = [small[0]] + [swap(small[k], "lvl", k) for k in (1, 2, 3)]
    weight_a = to_bins(me_list, feature_weight, 0, 10)
    slot = me_list
    levels, info, table = arrange(after(slot, weight_a), 1, own, arrived, coarse)
    cross_levels = swap(levels, "img", top)

    stacked = (
        info, feature_bias[:, None], hidden_weight, hidden_bias[:, None], jnp.swapaxes(class_weight, 1, 2),
        class_bias[:, None], jnp.swapaxes(delta_weight, 1, 2), delta_bias[:, None],
    )

    def run_head(s, parts, before, ready, micros):
        results = head(after(me_list, *ready), *parts, s, stacked, images, before, micros)
        shared, small, (grads, stay, away) = results[:2], results[2:4], results[4:]
        return shared, small, grads, stay, swap(away, "img", top)

    def add(first, second):
        return (first.astype(jnp.float32) + second.astype(jnp.float32)).astype(jnp.bfloat16)

    pooled_a = crop(table, 0, levels, 12)
    part_a = first_product(pooled_a, weight_a, 1)
    weight_b = to_bins(after(me_list, part_a), feature_weight, 1, 8)
    chip_a = add(part_a, swap(part_a, "lvl", 1))
    pooled_b = crop(after(table, weight_b, chip_a), 1, levels, 8)
    part_b = first_product(pooled_b, weight_b, 0)
    shared, small_a, grads_a, stay_a, cross_a = run_head(0, (chip_a, swap(chip_a, "lvl", 2)), (), [part_b], 0)
    part_b = after(part_b, grads_a)
    theirs_b = swap(part_b, "lvl", 1)
    cross_table = prepare(after(slot, grads_a), cross_levels)
    chip_b = add(after(part_b, cross_table), theirs_b)
    far_a = crop(after(cross_table, chip_b), 0, cross_levels, 8)
    parts_b = (chip_b, swap(chip_b, "lvl", 2))
    if images == 8:
        def weight_sums(stay, cross, pooled, far, ready):
            pieces = [v.reshape(2, 2, hidden // images, -1) for v in (stay, cross)]
            sent_one, kept_one, sent_two, kept_two = outer_sums(after(bits, *ready), *pieces, pooled, far, 0)
            return (kept_one, kept_two), (swap(sent_one, "img", 1), swap(sent_two, "img", 2))

        def second_step(kept, arrived, ready):
            one, two = fold(after(bits, *ready), kept[0], arrived[0], kept[1], arrived[1])
            return one, (swap(one, "img", 2), swap(two, "img", 1))

        small_near_a = swap(small_a[1], "img", 2)
        kept_a, arrived_a = weight_sums(stay_a, cross_a, pooled_a, far_a, [])
        shared, small_b, grads_b, stay_b, cross_b = run_head(1, parts_b, shared, [kept_a[0]], 0)
        small_near_b = swap(small_b[1], "img", 2)
        far_b = crop(after(cross_table, grads_b, small_near_a), 1, cross_levels, 10)
        kept_b, arrived_b = weight_sums(stay_b, cross_b, pooled_b, far_b, [])
        folded, last_a = second_step(kept_a, arrived_a, [kept_b[0]])
        slots_a = back_product(after(me_list, folded), grads_a, weight_a, 10)
        small, away = small_join(after(bits, slots_a), (small_a[0], small_b[0]), (small_near_a, small_near_b))
        arrived_small = swap(away, "img", 4)
        slots_b = back_product(after(me_list, away), grads_b, weight_b, 0)
        spread_out = spread(table, slots_a, slots_b, 0)
        folded, last_b = second_step(kept_b, arrived_b, [spread_out, *last_a])
        small, away = small_step(after(bits, folded), 0, small, arrived_small)
        arrived_small = swap(away, "img", 1)
    else:
        shared, small_b, grads_b, stay_b, cross_b = run_head(1, parts_b, shared, [far_a], 0)
        slots_a = back_product(me_list, grads_a, weight_a, 8)
        slots_b = back_product(me_list, grads_b, weight_b, 5)
        spread_out = spread(table, slots_a, slots_b, 20)
        far_b = crop(cross_table, 1, cross_levels, 10)
        totals = []
        for stay, cross, pooled, far in ((stay_a, cross_a, pooled_a, far_a), (stay_b, cross_b, pooled_b, far_b)):
            total = jnp.dot(stay, pooled, preferred_element_type=jnp.float32)
            total = total + jnp.dot(cross, far, preferred_element_type=jnp.float32)
            for b in range(steps)[::-1]:
                halves = split_bits(total, 1)
                away = choose(halves, 0, 1 - own_bits[b]).astype(jnp.bfloat16)
                total = choose(halves, 0, own_bits[b]) + swap(away, "img", 1 << b).astype(jnp.float32)
            totals.append(total[:, :features])
        order = bin_order()
        back = jnp.array([order.index(j) for j in range(49)])
        total = jnp.stack(totals)
        total = total.reshape(sections, total.shape[1], 49, features // 49)[:, :, back]
        feature_weight_grad = total.transpose(0, 3, 2, 1).reshape(sections, features, -1)

    parts = lax.all_to_all(spread_out, "lvl", split_axis=0, concat_axis=0, tiled=True)
    logits, deltas = shared
    if images == 8:
        feature_weight_grad = from_bins(after(bits, folded), 0, kept_a, arrived_a, last_a, None, features, 8)
        small = small_last(after(me_list, feature_weight_grad), small, arrived_small, hidden)
        sums = small[3:]
        feature_weight_grad = from_bins(after(bits, small[0]), 1, kept_b, arrived_b, last_b, feature_weight_grad, features, 8)
        me_list = after(me_list, feature_weight_grad)
    pyramid_grad = unpack(me_list, image_size, parts, 0)
    pyramid_grad = pyramid_grad.reshape(1, 1, GRID, GRID, CHANNELS)

    if images != 8:
        small, small_away = [jnp.concatenate([a, b], axis=0) for a, b in zip(small_a, small_b)]
        notes = small[:, hidden // 8 :].astype(jnp.float32)
        sums = (notes[:, 0:2] + notes[:, 2:4]).reshape(sections, -1)
        sums = lax.psum(sums, "img")
        small = jnp.concatenate([small[:, : hidden // 8], small_away[:, : hidden // 8]], axis=1)
        small = lax.psum_scatter(small, "img", scatter_dimension=1, tiled=True).astype(jnp.float32)
        small = (small[:, :, :hidden], small[:, :, hidden : hidden + CLASSES], small[:, :, hidden + OUTER : hidden + OUTER + DELTAS])
        at = 2 * hidden
        sums = (sums[:, :hidden], sums[:, hidden:at], sums[:, at : at + CLASSES], sums[:, at + OUTER : at + OUTER + DELTAS])
    return (
        logits,
        deltas,
        pyramid_grad,
        feature_weight_grad,
        sums[0],
        small[0],
        sums[1],
        small[1],
        sums[2],
        small[2],
        sums[3],
    )


def solution(mesh):
    return jax.shard_map(
        body,
        mesh=mesh,
        in_specs=(
            P("img", "lvl", None, None, None),
            P("img", None),
            P(None, None, ("img", "lvl")),
            P(None, ("img", "lvl")),
            P(None, ("img", "lvl")),
            P(None, None, ("img", "lvl")),
            P(None, "lvl", None),
            P(),
            P(),
            P(),
            P(),
            P(),
            P(),
            P(),
        ),
        out_specs=(
            P(None, ("img", "lvl"), None),
            P(None, ("img", "lvl"), None),
            P("img", "lvl", None, None, None),
            P(None, "lvl", "img"),
            P(),
            P(None, ("img", "lvl"), None),
            P(),
            P(None, ("img", "lvl"), None),
            P(),
            P(None, ("img", "lvl"), None),
            P(),
        ),
        check_vma=False,
    )
```

```python
import jax
import jax.numpy as jnp
from jax import lax
from jax.experimental import pallas as pl
from jax.experimental.pallas import tpu as pltpu
from jax.sharding import PartitionSpec as P

CHANNELS = 256
CLASSES = 81
POOL = 7
GRID = 64
DELTAS = 320

WIDTH = 80
ROWS = 140
BASES = (1, 66, 99, 116)
CELLS = ROWS * WIDTH
LANES = 128
WIDE = 3200
EXTRA = 16
FINE = 2048
NOTES = FINE + 3 * 512
BUFFER = NOTES + 4 * 32
UNROLL = 64


def cost(microseconds):
    return pl.CostEstimate(flops=int(microseconds * SCALE * 1_150_000_000), bytes_accessed=0, transcendentals=0)


def in_hbm(array):
    return pltpu.with_memory_space_constraint(array, pltpu.HBM)


def params(mebibytes):
    return pltpu.CompilerParams(vmem_limit_bytes=mebibytes << 20)


SCALE = 1.0


def low_half(rows):
    return lax.broadcasted_iota(jnp.int32, (rows, LANES), 1) < 64


def tent(position, step, cell):
    first = jnp.maximum(1.0 - jnp.abs(position - cell), 0.0)
    second = jnp.maximum(1.0 - jnp.abs(position + step - cell), 0.0)
    return ((first + second) * 0.5).astype(jnp.bfloat16).astype(jnp.float32)


def place_rows(maps, upper, lower, upper_row, lower_row, cells):
    low = low_half(8)
    tiles = cells // 8
    zero = jnp.zeros((8, LANES), jnp.float32)
    values = [upper[8 * t : 8 * t + 8] for t in range(tiles)]
    turned = [pltpu.roll(v, 64, 1) for v in values]
    for t in range(-1, tiles):
        here, here_turned = (values[t], turned[t]) if t >= 0 else (zero, zero)
        after, after_turned = (values[t + 1], turned[t + 1]) if t + 1 < tiles else (zero, zero)
        maps[pl.ds(upper_row * WIDTH + 8 + 8 * t, 8), :] = jnp.where(low, here, after_turned)
        maps[pl.ds(lower_row * WIDTH + 8 + 8 * t, 8), :] = jnp.where(low, here_turned, after)


def fill_maps(maps, levels_ref):
    zero = jnp.zeros((8, LANES), jnp.float32)
    for row in (0, BASES[1] - 1):
        for t in range(WIDTH // 8):
            maps[pl.ds(row * WIDTH + 8 * t, 8), :] = zero

    def clear_edge(y, carry):
        maps[pl.ds(pl.multiple_of((BASES[0] + y) * WIDTH + WIDTH - 8, 8), 8), :] = zero
        return carry

    lax.fori_loop(0, GRID, clear_edge, 0, unroll=8)

    def clear(t, carry):
        maps[pl.ds(pl.multiple_of(BASES[1] * WIDTH + t * 160, 160), 160), :] = jnp.zeros((160, LANES), jnp.float32)
        return carry

    lax.fori_loop(0, (ROWS - BASES[1]) * WIDTH // 160, clear, 0, unroll=2)

    def fine_row(y, carry):
        row = levels_ref[0, pl.ds(pl.multiple_of(y * 64, 64), 64), :].astype(jnp.float32)
        place_rows(maps, row, row, BASES[0] + y, BASES[0] + 32 + y, 64)
        return carry

    lax.fori_loop(0, 32, fine_row, 0, unroll=8)
    for level, cells in ((1, 32), (2, 16), (3, 8)):
        for y in range(cells // 2 if level == 1 else cells):
            row = levels_ref[0, pl.ds(FINE + (level - 1) * 512 + y * 32, 32), :].astype(jnp.float32)[:cells]
            if level == 1:
                place_rows(maps, row, row, BASES[1] + y, BASES[1] + 16 + y, 32)
            else:
                place_upper(maps, row, BASES[level] + y, cells)


def place_upper(maps, row, at, cells):
    low = low_half(8)
    tiles = cells // 8
    zero = jnp.zeros((8, LANES), jnp.float32)
    values = [row[8 * t : 8 * t + 8] for t in range(tiles)]
    for t in range(-1, tiles):
        here = values[t] if t >= 0 else zero
        after = pltpu.roll(values[t + 1], 64, 1) if t + 1 < tiles else zero
        maps[pl.ds(at * WIDTH + 8 + 8 * t, 8), :] = jnp.where(low, here, after)


def crop_kernel(table_ref, levels_ref, out_ref, slab, maps, section):
    rb = out_ref.shape[0]
    base = pl.program_id(0) * rb

    @pl.when(pl.program_id(0) == 0)
    def _():
        fill_maps(maps, levels_ref)

    low = low_half(8)
    lane = lax.broadcasted_iota(jnp.int32, (8, LANES), 1)
    bins = (2 * lax.broadcasted_iota(jnp.int32, (8, LANES), 0)).astype(jnp.float32)
    lane_y = (lane // 8).astype(jnp.float32)
    lane_x = (lane % 8).astype(jnp.float32)

    def one(r):
        start = table_ref[section, 0, base + r].astype(jnp.int32)
        y_at, y_step, x_at, x_step = [table_ref[section, 1 + j, base + r] for j in range(4)]
        window = jnp.concatenate([maps[pl.ds(start + WIDTH * j, 8), :] for j in range(16)], axis=0)
        wy = tent(y_at + y_step * bins, y_step, lane_y)
        x_position = x_at + x_step * bins
        wx = [tent(x_position, x_step, lane_x + 8.0 * h) for h in range(2)]
        rows = [jnp.broadcast_to(wy[b : b + 1], (8, LANES)) for b in range(POOL)]
        weight = jnp.concatenate([rows[b] * wx[h] for h in range(2) for b in range(POOL)], axis=0)
        both = jnp.dot(weight.astype(jnp.bfloat16), window.astype(jnp.bfloat16), preferred_element_type=jnp.float32)
        near = [both[8 * b : 8 * b + 8] for b in range(POOL)]
        far = [both[56 + 8 * b : 64 + 8 * b] for b in range(POOL)]
        zero = jnp.zeros((8, LANES), jnp.float32)
        for i in range(4):
            near_odd, far_odd = (near[2 * i + 1], far[2 * i + 1]) if i < 3 else (zero, zero)
            pair = jnp.where(low, near[2 * i], far_odd) + pltpu.roll(jnp.where(low, near_odd, far[2 * i]), 64, 1)
            slab[pl.ds(i * 8 * rb + r, 8, stride=rb), :] = pair

    def step(t, carry):
        for u in range(UNROLL):
            one(t * UNROLL + u)
        return carry

    lax.fori_loop(0, rb // UNROLL, step, 0)
    for i in range(3):
        for e in range(POOL):
            out_ref[:, pl.ds((7 * i + e) * LANES, LANES)] = slab[pl.ds((8 * i + e) * rb, rb), :].astype(jnp.bfloat16)
    for j in range(4):
        first = slab[pl.ds((24 + 2 * j) * rb, rb), :]
        if j < 3:
            second = slab[pl.ds((25 + 2 * j) * rb, rb), :]
            joined = jnp.where(low_half(rb), first, pltpu.roll(second, 64, 1))
            out_ref[:, pl.ds((21 + j) * LANES, LANES)] = joined.astype(jnp.bfloat16)
        else:
            out_ref[:, pl.ds(24 * LANES, LANES)] = jnp.where(low_half(rb), first, 0.0).astype(jnp.bfloat16)


def crop(table, section, levels, micros, block=128):
    count = table.shape[2]
    return pl.pallas_call(
        lambda *refs: crop_kernel(*refs, section),
        grid=(count // block,),
        in_specs=[pl.BlockSpec(memory_space=pltpu.SMEM), pl.BlockSpec(memory_space=pltpu.VMEM)],
        out_specs=pl.BlockSpec((block, WIDE), lambda g: (g, 0)),
        scratch_shapes=[pltpu.VMEM((32 * block, LANES), jnp.float32), pltpu.VMEM((CELLS, LANES), jnp.float32)],
        out_shape=jax.ShapeDtypeStruct((count, WIDE), jnp.bfloat16),
        cost_estimate=cost(micros),
        compiler_params=params(13),
    )(table, levels)


def spread_kernel(table_ref, first_ref, second_ref, out_ref, slab, sums, fine, coarse, sems):
    rb = slab.shape[0] // 32
    steps = pl.num_programs(0) // 2
    section = pl.program_id(0) // steps
    base = (pl.program_id(0) % steps) * rb

    @pl.when(pl.program_id(0) == 0)
    def _():
        def clear(t, carry):
            sums[pl.ds(pl.multiple_of(t * 160, 160), 160), :] = jnp.zeros((160, LANES), jnp.float32)
            return carry

        lax.fori_loop(0, CELLS // 160, clear, 0, unroll=2)
        for i in range(4):
            slab[pl.ds((8 * i + 7) * rb, rb), :] = jnp.zeros((rb, LANES), jnp.float32)

    def lay_out(grads):
        grads_ref = grads.at[pl.ds(pl.multiple_of(base, rb), rb), :]
        for i in range(3):
            for e in range(POOL):
                slab[pl.ds((8 * i + e) * rb, rb), :] = grads_ref[:, pl.ds((7 * i + e) * LANES, LANES)].astype(jnp.float32)
        for j in range(4):
            pair = grads_ref[:, pl.ds((21 + j) * LANES, LANES)].astype(jnp.float32)
            slab[pl.ds((24 + 2 * j) * rb, rb), :] = pair
            if j < 3:
                slab[pl.ds((25 + 2 * j) * rb, rb), :] = pltpu.roll(pair, 64, 1)

    @pl.when(section == 0)
    def _():
        lay_out(first_ref)

    @pl.when(section == 1)
    def _():
        lay_out(second_ref)

    low = low_half(8)
    lane = lax.broadcasted_iota(jnp.int32, (8, LANES), 1)
    row = lax.broadcasted_iota(jnp.int32, (8, LANES), 0).astype(jnp.float32)
    bins_y = (2 * ((lane // 8) % 8)).astype(jnp.float32)
    bins_x = (2 * (lane % 8)).astype(jnp.float32)
    cell_x = row + 8.0 * (lane // 64).astype(jnp.float32)

    def one(r):
        start = table_ref[section, 0, base + r].astype(jnp.int32)
        y_at, y_step, x_at, x_step = [table_ref[section, 1 + j, base + r] for j in range(4)]
        y_position = y_at + y_step * bins_y
        wy = [tent(y_position, y_step, row + 8.0 * h) for h in range(2)]
        wx = tent(x_at + x_step * bins_x, x_step, cell_x)
        rows = [jnp.broadcast_to(wy[y // 8][y % 8 : y % 8 + 1], (8, LANES)) for y in range(16)]
        weight = jnp.concatenate([rows[y] * wx for y in range(16)], axis=0)
        near, far = [], []
        for i in range(4):
            pair = slab[pl.ds(i * 8 * rb + r, 8, stride=rb), :]
            turned = pltpu.roll(pair, 64, 1)
            zero = jnp.zeros_like(pair)
            near.append(jnp.where(low, pair, zero))
            far.append(jnp.where(low, zero, turned))
            near.append(jnp.where(low, turned, zero) if i < 3 else zero)
            far.append(jnp.where(low, zero, pair) if i < 3 else zero)
        grads = jnp.concatenate(near + far, axis=0)
        out = jnp.dot(weight.astype(jnp.bfloat16), grads.astype(jnp.bfloat16), preferred_element_type=jnp.float32)
        for j in range(16):
            sums[pl.ds(start + WIDTH * j, 8), :] += out[8 * j : 8 * j + 8]

    def step(t, carry):
        for u in range(UNROLL):
            one(t * UNROLL + u)
        return carry

    lax.fori_loop(0, rb // UNROLL, step, 0)

    @pl.when(pl.program_id(0) == pl.num_programs(0) - 1)
    def _():
        def gather(upper_row, lower_row, cells):
            tiles = []
            for t in range(cells // 8):
                up, up_far = [sums[pl.ds(upper_row * WIDTH + 8 * t + s, 8), :] for s in (8, 0)]
                down, down_far = [sums[pl.ds(lower_row * WIDTH + 8 * t + s, 8), :] for s in (8, 0)]
                tiles.append(jnp.where(low, up, down_far) + pltpu.roll(jnp.where(low, down, up_far), 64, 1))
            return jnp.concatenate(tiles, axis=0)

        def fine_row(y, carry):
            here = pl.ds(pl.multiple_of(y * 64, 64), 64)
            fine[here, :] = gather(BASES[0] + y, BASES[0] + 32 + y, 64).astype(jnp.bfloat16)
            return carry

        lax.fori_loop(0, 32, fine_row, 0, unroll=8)
        fine_copy = pltpu.make_async_copy(fine, out_ref.at[0], sems.at[0])
        fine_copy.start()
        coarse[...] = jnp.zeros_like(coarse)
        for y in range(16):
            coarse[0, pl.ds(32 * y, 32), :] = gather(BASES[1] + y, BASES[1] + 16 + y, 32).astype(jnp.bfloat16)
        for level, cells in ((2, 16), (3, 8)):
            for y in range(cells):
                tile = gather(BASES[level] + y, BASES[level] + y, cells)
                tile = jnp.where(low_half(cells), tile, 0.0)
                if cells < 16:
                    tile = jnp.concatenate([tile, jnp.zeros_like(tile)], axis=0)
                coarse[level - 1, pl.ds(32 * y, 16), :] = tile.astype(jnp.bfloat16)
        coarse_copy = pltpu.make_async_copy(coarse, out_ref.at[pl.ds(1, 3), pl.ds(0, 512), :], sems.at[1])
        coarse_copy.start()
        fine_copy.wait()
        coarse_copy.wait()


def spread(table, first, second, micros, block=128):
    steps = first.shape[0] // block
    return pl.pallas_call(
        spread_kernel,
        grid=(2 * steps,),
        in_specs=[pl.BlockSpec(memory_space=pltpu.SMEM)] + [pl.BlockSpec(memory_space=pltpu.VMEM)] * 2,
        out_specs=pl.BlockSpec(memory_space=pltpu.HBM),
        scratch_shapes=[
            pltpu.VMEM((32 * block, LANES), jnp.float32),
            pltpu.VMEM((CELLS, LANES), jnp.float32),
            pltpu.VMEM((FINE, LANES), jnp.bfloat16),
            pltpu.VMEM((3, 512, LANES), jnp.bfloat16),
            pltpu.SemaphoreType.DMA((2,)),
        ],
        out_shape=pltpu.HBM((4, FINE, LANES), jnp.bfloat16),
        cost_estimate=cost(micros),
        compiler_params=params(16),
    )(table, first, second)


def bin_order():
    pairs = [(2 * i + p) * POOL + e for i in range(3) for e in range(POOL) for p in range(2)]
    return pairs + [6 * POOL + e for e in range(POOL)]


def write_note(boxes_ref, routes_ref, labels_ref, targets_ref, image_ref):
    halves = []
    for s in range(2):
        boxes = boxes_ref[s]
        high = jnp.right_shift(boxes, 6)
        rest = targets_ref[s]
        parts = [high.astype(jnp.float32), (boxes - 64 * high).astype(jnp.float32)]
        parts += [routes_ref[s : s + 1].astype(jnp.float32), labels_ref[s : s + 1].astype(jnp.float32)]
        for _ in range(3):
            part = rest.astype(jnp.bfloat16).astype(jnp.float32)
            parts.append(part)
            rest = rest - part
        parts += [jnp.full((1, 64), image_ref[0, j], jnp.int32).astype(jnp.float32) for j in range(2)]
        halves.append(jnp.concatenate(parts + [jnp.zeros((8, 64), jnp.float32)], axis=0))
    return jnp.concatenate(halves, axis=1).astype(jnp.bfloat16)


def decode(notes, info_ref, table_ref):
    notes = [n.astype(jnp.float32) for n in notes]
    for s in range(2):
        rows = jnp.concatenate([n[:, 64 * s : 64 * s + 64] for n in notes], axis=1)
        boxes_float = rows[:4] * 64.0 + rows[4:8]
        targets = (rows[10:14] + rows[14:18]) + rows[18:22]
        pad = jnp.zeros((6, rows.shape[1]), jnp.float32)
        info_ref[s] = jnp.concatenate([boxes_float, rows[8:10], targets, pad], axis=0)
        boxes = boxes_float.astype(jnp.int32)
        route = rows[8:9].astype(jnp.int32)
        sizes = rows[22:24].astype(jnp.int32) * 16
        lines = []
        for axis in range(2):
            limit = sizes[axis : axis + 1]
            low_edge = jnp.minimum(jnp.maximum(boxes[axis : axis + 1], 0), limit)
            high_edge = jnp.minimum(jnp.maximum(boxes[axis + 2 : axis + 3], 0), limit)
            stride = jnp.left_shift(4, route)
            first = 28 * low_edge + (high_edge - low_edge) - 224 * stride
            cell = jnp.right_shift((jnp.right_shift(first, 8 + route) + 7) * 9363, 16) - 1
            units = 448 * stride
            scale = 1.0 / units.astype(jnp.float32)
            lines.append((cell, (first - cell * units).astype(jnp.float32) * scale, (2 * (high_edge - low_edge)).astype(jnp.float32) * scale))
        row = jnp.where(route == 0, BASES[0], jnp.where(route == 1, BASES[1], jnp.where(route == 2, BASES[2], BASES[3])))
        start = (row + lines[0][0]) * WIDTH + 8 + lines[1][0]
        parts = [start.astype(jnp.float32), lines[0][1], lines[0][2], lines[1][1], lines[1][2]]
        table_ref[s] = jnp.concatenate(parts + [jnp.zeros((3, rows.shape[1]), jnp.float32)], axis=0)


TABLES = [jax.ShapeDtypeStruct((2, 16, 256), jnp.float32), jax.ShapeDtypeStruct((2, 8, 256), jnp.float32)]


def arrange_kernel(
    slot_ref, own_ref, one_ref, two_ref, three_ref, near_ref, core_ref, chip_ref, far_ref,
    levels_ref, info_ref, table_ref, coarse_ref,
):
    slot, me = 0, slot_ref[6]
    for k, ref in enumerate((near_ref, core_ref, chip_ref, far_ref)):
        coarse_ref[jnp.bitwise_xor(me, k)] = ref[...]
    fine = own_ref[...] + one_ref[...] + two_ref[...] + three_ref[...]
    levels_ref[slot, pl.ds(0, FINE), :] = fine.reshape(FINE, LANES)
    for level in range(1, 4):
        levels_ref[slot, pl.ds(FINE + (level - 1) * 512, 512), :] = coarse_ref[level, pl.ds(0, 512), :]
    for d in range(4):
        levels_ref[slot, pl.ds(NOTES + 32 * d, 32), :] = coarse_ref[d, pl.ds(512, 32), :]
    decode([coarse_ref[d, pl.ds(512, 32), :] for d in range(4)], info_ref, table_ref)


def arrange(slot, slots, own, arrived, coarse):
    vmem = pl.BlockSpec(memory_space=pltpu.VMEM)
    return pl.pallas_call(
        arrange_kernel,
        in_specs=[pl.BlockSpec(memory_space=pltpu.SMEM)] + [vmem] * 8,
        out_shape=[jax.ShapeDtypeStruct((slots, BUFFER, LANES), jnp.bfloat16)] + TABLES,
        scratch_shapes=[pltpu.VMEM((4, 544, LANES), jnp.bfloat16)],
        cost_estimate=cost(2),
        compiler_params=params(7),
    )(slot, own, *arrived, *coarse)


def prepare_kernel(slot_ref, levels_ref, info_ref, table_ref):
    del slot_ref
    slot = 0
    decode([levels_ref[slot, pl.ds(NOTES + 32 * d, 32), :] for d in range(4)], info_ref, table_ref)


def prepare(slot, levels):
    vmem = pl.BlockSpec(memory_space=pltpu.VMEM)
    return pl.pallas_call(
        prepare_kernel,
        in_specs=[pl.BlockSpec(memory_space=pltpu.SMEM), vmem],
        out_shape=TABLES,
        cost_estimate=cost(1),
    )(slot, levels)[1]


def valid_edges(owner, image_ref):
    shift = 2 + owner
    round_up = jnp.left_shift(1, shift) - 1
    return [jnp.right_shift(image_ref[0, j] + round_up, shift) for j in range(2)]


def pack_kernel(
    owner_ref, image_ref, upper_ref, lower_ref, small_ref, boxes_hbm, routes_hbm, labels_hbm, targets_hbm,
    own_ref, one_ref, two_ref, three_ref, near_ref, core_ref, chip_ref, far_ref,
    boxes_ref, routes_ref, labels_ref, targets_ref, sems, coarse_ref,
):
    g = pl.program_id(0)
    owner = owner_ref[6]
    rows_valid, cols_valid = valid_edges(owner, image_ref)
    pairs = ((boxes_hbm, boxes_ref), (routes_hbm, routes_ref), (labels_hbm, labels_ref), (targets_hbm, targets_ref))
    copies = [pltpu.make_async_copy(a, b, sems.at[j]) for j, (a, b) in enumerate(pairs)]

    @pl.when(g == 0)
    def _():
        for copy in copies:
            copy.start()

    cell = lax.broadcasted_iota(jnp.int32, (GRID, LANES), 0)
    low = low_half(GRID)
    outs = (own_ref, one_ref, two_ref, three_ref)
    for y in range(upper_ref.shape[2]):
        top = (cell < cols_valid) & (g * upper_ref.shape[2] + y < rows_valid)
        bottom = (cell < cols_valid) & (32 + g * upper_ref.shape[2] + y < rows_valid)
        for c in range(2):
            a = jnp.where(top, upper_ref[0, 0, y, :, pl.ds(LANES * c, LANES)].astype(jnp.float32), 0.0)
            b = jnp.where(bottom, lower_ref[0, 0, y, :, pl.ds(LANES * c, LANES)].astype(jnp.float32), 0.0)
            even = jnp.where(low, a, pltpu.roll(b, 64, 1))
            if c == 0:
                even = jnp.where(owner == 0, even, 0.0)
            outs[2 * c][y] = even.astype(jnp.bfloat16)
            outs[2 * c + 1][y] = jnp.where(low, pltpu.roll(a, 64, 1), b).astype(jnp.bfloat16)

    @pl.when(g == 0)
    def _():
        low = low_half(32)
        cell = lax.broadcasted_iota(jnp.int32, (32, LANES), 0)
        for y in range(16):
            top = (cell < cols_valid) & (y < rows_valid)
            bottom = (cell < cols_valid) & (16 + y < rows_valid) & (owner < 2)
            for c in range(2):
                a = jnp.where(top, small_ref[0, 0, y, pl.ds(0, 32), pl.ds(LANES * c, LANES)].astype(jnp.float32), 0.0)
                b = jnp.where(bottom, small_ref[0, 0, 16 + y, pl.ds(0, 32), pl.ds(LANES * c, LANES)].astype(jnp.float32), 0.0)
                here = pl.ds(32 * y, 32)
                coarse_ref[2 * c, here, :] = jnp.where(low, a, pltpu.roll(b, 64, 1)).astype(jnp.bfloat16)
                coarse_ref[2 * c + 1, here, :] = jnp.where(low, pltpu.roll(a, 64, 1), b).astype(jnp.bfloat16)
        for copy in copies:
            copy.wait()
        note = write_note(boxes_ref, routes_ref, labels_ref, targets_ref, image_ref)
        for d in range(4):
            coarse_ref[d, pl.ds(512, 32), :] = note
        for k, ref in enumerate((near_ref, core_ref, chip_ref, far_ref)):
            ref[...] = coarse_ref[jnp.bitwise_xor(owner, k)]


def pack(owner, image_size, pyramid, boxes, routes, labels, targets):
    regions = (boxes, routes, labels, targets)
    return pl.pallas_call(
        pack_kernel,
        grid=(4,),
        in_specs=[
            pl.BlockSpec(memory_space=pltpu.SMEM),
            pl.BlockSpec(memory_space=pltpu.SMEM),
            pl.BlockSpec((1, 1, 8, GRID, CHANNELS), lambda g: (0, 0, g, 0, 0)),
            pl.BlockSpec((1, 1, 8, GRID, CHANNELS), lambda g: (0, 0, g + 4, 0, 0)),
            pl.BlockSpec((1, 1, 32, GRID, CHANNELS), lambda g: (0, 0, 0, 0, 0)),
        ]
        + [pl.BlockSpec(memory_space=pltpu.HBM)] * 4,
        out_specs=[pl.BlockSpec((8, GRID, LANES), lambda g: (g, 0, 0))] * 4
        + [pl.BlockSpec((544, LANES), lambda g: (0, 0))] * 4,
        scratch_shapes=[pltpu.VMEM(v.shape, v.dtype) for v in regions]
        + [pltpu.SemaphoreType.DMA((4,)), pltpu.VMEM((4, 544, LANES), jnp.bfloat16)],
        out_shape=[jax.ShapeDtypeStruct((32, GRID, LANES), jnp.bfloat16)] * 4
        + [jax.ShapeDtypeStruct((544, LANES), jnp.bfloat16)] * 4,
        cost_estimate=cost(2.7),
        compiler_params=params(8),
    )(owner, in_hbm(image_size), *[in_hbm(pyramid)] * 3, *[in_hbm(v) for v in regions])


def unpack_kernel(owner_ref, image_ref, fine_ref, coarse_ref, out_ref):
    g = pl.program_id(0)
    owner = owner_ref[6]
    rows_valid, cols_valid = valid_edges(owner, image_ref)
    count = out_ref.shape[1]

    @pl.when(owner == 0)
    def _():
        cell = lax.broadcasted_iota(jnp.int32, (GRID, LANES), 0)
        low = low_half(GRID)
        for y in range(count):
            top = (cell < cols_valid) & (g * count + y < rows_valid)
            bottom = (cell < cols_valid) & (32 + g * count + y < rows_valid)
            for c in range(2):
                a = fine_ref[2 * c, pl.ds(y * GRID, GRID), :].astype(jnp.float32)
                b = fine_ref[2 * c + 1, pl.ds(y * GRID, GRID), :].astype(jnp.float32)
                upper = jnp.where(low, a, pltpu.roll(b, 64, 1))
                lower = jnp.where(low, pltpu.roll(a, 64, 1), b)
                out_ref[0, y, :, pl.ds(LANES * c, LANES)] = jnp.where(top, upper, 0.0).astype(jnp.bfloat16)
                out_ref[1, y, :, pl.ds(LANES * c, LANES)] = jnp.where(bottom, lower, 0.0).astype(jnp.bfloat16)

    @pl.when(owner != 0)
    def _():
        out_ref[...] = jnp.zeros_like(out_ref)
        cell = lax.broadcasted_iota(jnp.int32, (32, LANES), 0)
        low = low_half(32)
        for y in range(count):
            top = (cell < cols_valid) & (g * count + y < rows_valid)
            line = pl.ds(pl.multiple_of(((g % 2) * count + y) * 32, 32), 32)
            for c in range(2):
                a = coarse_ref[2 * c, line, :].astype(jnp.float32)
                b = coarse_ref[2 * c + 1, line, :].astype(jnp.float32)
                upper = jnp.where(low, a, pltpu.roll(b, 64, 1))
                lower = jnp.where(low, pltpu.roll(a, 64, 1), b)
                row = jnp.where(g < 2, upper, lower)
                out_ref[0, y, pl.ds(0, 32), pl.ds(LANES * c, LANES)] = jnp.where(top, row, 0.0).astype(jnp.bfloat16)


def unpack(owner, image_size, parts, micros):
    return pl.pallas_call(
        unpack_kernel,
        grid=(4,),
        in_specs=[pl.BlockSpec(memory_space=pltpu.SMEM)] * 2
        + [pl.BlockSpec((4, 512, LANES), lambda g: (0, g, 0)), pl.BlockSpec((4, 512, LANES), lambda g: (0, 0, 0))],
        out_specs=pl.BlockSpec((2, 8, GRID, CHANNELS), lambda g: (0, g, 0, 0)),
        out_shape=jax.ShapeDtypeStruct((2, 32, GRID, CHANNELS), jnp.bfloat16),
        cost_estimate=cost(micros),
        compiler_params=params(7),
    )(owner, image_size, parts, parts)


def to_bins_kernel(order_ref, weight_ref, out_ref, arrived, rows, sems, section):
    del order_ref
    taken = arrived.shape[1]
    blocks = weight_ref.shape[1] // taken

    def fetch(c):
        slot = c % 2
        return pltpu.make_async_copy(weight_ref.at[section, pl.ds(c * taken, taken), :], arrived.at[slot], sems.at[slot])

    fetch(0).start()
    fetch(1).start()

    def step(c, carry):
        fetch(c).wait()
        for t in range(rows.shape[0]):
            rows[t] = arrived[c % 2, :, pl.ds(t * LANES, LANES)].astype(jnp.float32)

        @pl.when(c + 2 < blocks)
        def _():
            fetch(c + 2).start()

        here = pl.ds(pl.multiple_of(c * 16, 16), 16)
        for place, source in enumerate(bin_order()):
            for t in range(rows.shape[0]):
                out_ref[place, here, pl.ds(t * LANES, LANES)] = rows[t, pl.ds(source, 16, stride=49), :].astype(jnp.bfloat16)
        return carry

    lax.fori_loop(0, blocks, step, 0)
    out_ref[49] = jnp.zeros(out_ref.shape[1:], jnp.bfloat16)


def to_bins(order, weight, section, micros):
    rows, width = weight.shape[1:]
    channels = rows // 49
    return pl.pallas_call(
        lambda *refs: to_bins_kernel(*refs, section),
        in_specs=[pl.BlockSpec(memory_space=pltpu.SMEM), pl.BlockSpec(memory_space=pltpu.HBM)],
        out_specs=pl.BlockSpec(memory_space=pltpu.VMEM),
        out_shape=jax.ShapeDtypeStruct((50, channels, width), jnp.bfloat16),
        scratch_shapes=[
            pltpu.VMEM((2, 784, width), jnp.bfloat16),
            pltpu.VMEM((width // LANES, 784, LANES), jnp.float32),
            pltpu.SemaphoreType.DMA((2,)),
        ],
        cost_estimate=cost(micros),
        compiler_params=params(8),
    )(order, in_hbm(weight)).reshape(WIDE, width)


def first_kernel(pooled_ref, weight_ref, out_ref):
    for n in range(0, out_ref.shape[1], 256):
        here = pl.ds(n, 256)
        out_ref[:, here] = jnp.dot(pooled_ref[...], weight_ref[:, here], preferred_element_type=jnp.float32).astype(jnp.bfloat16)


def first_product(pooled, weight, micros):
    vmem = pl.BlockSpec(memory_space=pltpu.VMEM)
    return pl.pallas_call(
        first_kernel,
        in_specs=[vmem, vmem],
        out_specs=vmem,
        out_shape=jax.ShapeDtypeStruct((pooled.shape[0], weight.shape[1]), jnp.bfloat16),
        cost_estimate=cost(micros),
        compiler_params=params(6),
    )(pooled, weight)


def back_kernel(order_ref, grads_ref, weight_ref, out_ref):
    del order_ref
    for n in range(0, WIDE, 640):
        here = pl.ds(n, 640)
        value = lax.dot_general(grads_ref[...], weight_ref[here, :], NT, preferred_element_type=jnp.float32)
        out_ref[:, here] = value.astype(jnp.bfloat16)


def back_product(order, grads, weight, micros):
    vmem = pl.BlockSpec(memory_space=pltpu.VMEM)
    return pl.pallas_call(
        back_kernel,
        in_specs=[pl.BlockSpec(memory_space=pltpu.SMEM), vmem, vmem],
        out_specs=vmem,
        out_shape=jax.ShapeDtypeStruct((grads.shape[0], WIDE), jnp.bfloat16),
        cost_estimate=cost(micros),
        compiler_params=params(6),
    )(order, grads, weight)


SPLIT = 2176
TAIL = WIDE - SPLIT


def outer_kernel(bits_ref, own, cross, own_pooled, cross_pooled, sent_one, kept_one, sent_two, kept_two):
    rows = own.shape[2]

    def product(pick, at, width, out):
        mine, theirs = [pick(ref).reshape(2 * rows, -1) for ref in (own, cross)]
        for n in range(0, width, 256):
            wide = min(256, width - n)
            here = pl.ds(at + n, wide)
            value = jnp.dot(mine, own_pooled[:, here], preferred_element_type=jnp.float32)
            value = value + jnp.dot(theirs, cross_pooled[:, here], preferred_element_type=jnp.float32)
            out[:, :, pl.ds(n, wide)] = value.astype(out.dtype).reshape(2, rows, wide)

    product(lambda ref: ref[:, bits_ref[1]], 0, SPLIT, sent_one)
    product(lambda ref: ref[bits_ref[3]], SPLIT, TAIL, sent_two)
    product(lambda ref: ref[:, bits_ref[0]], 0, SPLIT, kept_one)
    product(lambda ref: ref[bits_ref[2]], SPLIT, TAIL, kept_two)


def outer_sums(bits, own, cross, own_pooled, cross_pooled, micros):
    rows = own.shape[2]
    vmem = pl.BlockSpec(memory_space=pltpu.VMEM)
    kinds = [(width, jnp.bfloat16) for width in (SPLIT, TAIL) for _ in range(2)]
    return pl.pallas_call(
        outer_kernel,
        in_specs=[pl.BlockSpec(memory_space=pltpu.SMEM)] + [vmem] * 4,
        out_specs=[vmem] * 4,
        out_shape=[jax.ShapeDtypeStruct((2, rows, width), dtype) for width, dtype in kinds],
        cost_estimate=cost(micros),
        compiler_params=params(6),
    )(bits, own, cross, own_pooled, cross_pooled)


def fold_kernel(bits_ref, kept_one, arrived_one, kept_two, arrived_two, one_ref, two_ref):
    up, low = bits_ref[3], bits_ref[1]
    one_ref[...] = (kept_one[up].astype(jnp.float32) + arrived_one[up].astype(jnp.float32)).astype(jnp.bfloat16)
    two_ref[...] = (kept_two[low].astype(jnp.float32) + arrived_two[low].astype(jnp.float32)).astype(jnp.bfloat16)


def fold(bits, kept_one, arrived_one, kept_two, arrived_two):
    rows = kept_one.shape[1]
    vmem = pl.BlockSpec(memory_space=pltpu.VMEM)
    return pl.pallas_call(
        fold_kernel,
        in_specs=[pl.BlockSpec(memory_space=pltpu.SMEM)] + [vmem] * 4,
        out_specs=[vmem] * 2,
        out_shape=[jax.ShapeDtypeStruct((rows, SPLIT), jnp.bfloat16), jax.ShapeDtypeStruct((rows, TAIL), jnp.bfloat16)],
        cost_estimate=cost(8),
        compiler_params=params(5),
    )(bits, kept_one, arrived_one, kept_two, arrived_two)


def from_bins_kernel(bits_ref, *refs):
    del bits_ref
    kept_one, arrived_one, last_one, kept_two, arrived_two, last_two = refs[:6]
    out_ref, turned = refs[-2:]
    for kept, arrived, last, at in ((kept_one, arrived_one, last_one, 0), (kept_two, arrived_two, last_two, SPLIT)):
        for t in range(kept.shape[2] // LANES):
            here = pl.ds(t * LANES, LANES)
            value = kept[0, :, here].astype(jnp.float32) + arrived[0, :, here].astype(jnp.float32)
            value = value + last[:, here].astype(jnp.float32)
            turned[pl.ds(at + t * LANES, LANES), :] = jnp.transpose(value, (1, 0))
    for place, source in enumerate(bin_order()):
        out_ref[0, pl.ds(source, 64, stride=49), :] = turned[pl.ds(place * 64, 64), :]


def from_bins(bits, section, kept, arrived, last, before, rows, micros):
    columns = kept[0].shape[1]
    specs = []
    for at, width in ((2, SPLIT), (0, TAIL)):
        both = pl.BlockSpec((1, columns, width), lambda i, b, at=at: (b[at], 0, 0))
        specs += [both, both, pl.BlockSpec((columns, width), lambda i, b: (0, 0))]
    operands = [kept[0], arrived[0], last[0], kept[1], arrived[1], last[1]]
    aliases = {}
    if before is not None:
        specs.append(pl.BlockSpec(memory_space=pl.ANY))
        operands.append(before)
        aliases = {7: 0}
    return pl.pallas_call(
        from_bins_kernel,
        grid_spec=pltpu.PrefetchScalarGridSpec(
            num_scalar_prefetch=1,
            grid=(1,),
            in_specs=specs,
            out_specs=pl.BlockSpec((1, rows, columns), lambda i, b: (section, 0, 0)),
            scratch_shapes=[pltpu.VMEM((WIDE, LANES), jnp.float32)],
        ),
        out_shape=jax.ShapeDtypeStruct((2, rows, columns), jnp.float32),
        input_output_aliases=aliases,
        cost_estimate=cost(micros),
        compiler_params=params(6),
    )(bits, *operands)


def silu_slope(values):
    sigma = jax.nn.sigmoid(values)
    return sigma * (1.0 + values * (1.0 - sigma))


NT = (((1,), (1,)), ((), ()))
TN = (((0,), (0,)), ((), ()))
OUTER = 128


def write_sums(sums, width):
    high = sums.astype(jnp.bfloat16).astype(jnp.float32)
    rows = []
    for part in (high, sums - high):
        rest = part[:, width:]
        if rest.shape[1] < width:
            rest = jnp.concatenate([rest, jnp.zeros((1, width - rest.shape[1]), jnp.float32)], axis=1)
        rows += [part[:, :width], rest]
    return jnp.concatenate(rows + [jnp.zeros((EXTRA - 4, width), jnp.float32)], axis=0).astype(jnp.bfloat16)


def read_sums(note, count):
    note = note.astype(jnp.float32)
    rows = note[0:2] + note[2:4]
    return jnp.concatenate([rows[0:1], rows[1:2]], axis=1)[:, :count]


def head_kernel(
    me_ref, mine_ref, theirs_ref, info_ref, feature_bias_ref, hidden_ref, hidden_bias_ref, class_ref, class_bias_ref,
    delta_ref, delta_bias_ref,
    *refs, images,
):
    logits_ref, deltas_ref, small_ref, small_away_ref, grad_feature_ref, stay_ref, away_ref = refs[-12:-5]
    outer_scr, turned_scr, weight_scr, row_scr, small_scr = refs[-5:]
    me, half = me_ref[6], me_ref[4]
    weight_scr[...] = jnp.zeros_like(weight_scr)
    weight_scr[pl.ds(0, CLASSES), :] = class_ref[0]
    weight_scr[pl.ds(OUTER, DELTAS), :] = delta_ref[0]
    row_scr[...] = jnp.zeros_like(row_scr)
    row_scr[:, pl.ds(0, CLASSES)] = class_bias_ref[0]
    row_scr[:, pl.ds(OUTER, DELTAS)] = delta_bias_ref[0]
    f32 = jnp.float32
    rows, hidden = mine_ref.shape
    pre_feature = mine_ref[...].astype(f32) + theirs_ref[...].astype(f32) + feature_bias_ref[0]
    gate_one = jax.nn.sigmoid(pre_feature)
    hidden_one = (pre_feature * gate_one).astype(jnp.bfloat16)
    pre_hidden = jnp.dot(hidden_one, hidden_ref[0], preferred_element_type=f32) + hidden_bias_ref[0]
    gate_two = jax.nn.sigmoid(pre_hidden)
    hidden_two = (pre_hidden * gate_two).astype(jnp.bfloat16)
    outer = lax.dot_general(hidden_two, weight_scr[...], NT, preferred_element_type=f32) + row_scr[...]
    outer_scr[...] = outer
    own = pl.ds(pl.multiple_of(me * (rows // 4), rows // 4), rows // 4)
    logits_ref[0] = outer_scr[own, pl.ds(0, CLASSES)]
    deltas_ref[0] = outer_scr[own, pl.ds(OUTER, DELTAS)]

    columns = jnp.transpose(info_ref[0], (1, 0))
    label = columns[:, 5:6].astype(jnp.int32)
    lane = lax.broadcasted_iota(jnp.int32, (rows, OUTER), 1)
    logits = jnp.where(lane < CLASSES, outer[:, :OUTER], -jnp.inf)
    shifted = jnp.exp(logits - jnp.max(logits, axis=1, keepdims=True))
    grad_logits = shifted / jnp.sum(shifted, axis=1, keepdims=True) - (lane == label).astype(f32)
    wide = lax.broadcasted_iota(jnp.int32, (rows, outer.shape[1] - OUTER), 1)
    hot = (wide // 4 == label) & (label < CLASSES - 1)
    picked = jnp.where(hot, outer[:, OUTER:], 0.0)
    grad_deltas = jnp.zeros_like(picked)
    for j in range(4):
        mine = wide % 4 == j
        chosen = jnp.sum(jnp.where(mine, picked, 0.0), axis=1, keepdims=True)
        error = jnp.clip(chosen - columns[:, 6 + j : 7 + j], -1.0, 1.0)
        grad_deltas = jnp.where(mine & hot, error, grad_deltas)
    grad_outer = jnp.concatenate([grad_logits, grad_deltas], axis=1).astype(jnp.bfloat16)

    grad_two = jnp.dot(grad_outer, weight_scr[...], preferred_element_type=f32)
    slope_two = gate_two * (1.0 + pre_hidden * (1.0 - gate_two))
    grad_pre_hidden = (grad_two * slope_two).astype(jnp.bfloat16)
    grad_one = lax.dot_general(grad_pre_hidden, hidden_ref[0], NT, preferred_element_type=f32)
    slope_one = gate_one * (1.0 + pre_feature * (1.0 - gate_one))
    grad_feature = grad_one * slope_one
    grad_pre_feature = grad_feature.astype(jnp.bfloat16)
    grad_feature_ref[...] = grad_pre_feature
    turned_scr[...] = jnp.transpose(grad_feature, (1, 0)).astype(jnp.bfloat16)
    stay_ref[...] = turned_scr[pl.ds(pl.multiple_of(half * (hidden // 2), hidden // 2), hidden // 2), :]
    away_ref[...] = turned_scr[pl.ds(pl.multiple_of((1 - half) * (hidden // 2), hidden // 2), hidden // 2), :]

    run = hidden // (4 * images)
    row = lax.broadcasted_iota(jnp.int32, (hidden, hidden // 4), 0)
    col = lax.broadcasted_iota(jnp.int32, (hidden, hidden // 4), 1)
    pick = (row == (col // run) * (4 * run) + me * run + col % run).astype(jnp.bfloat16)
    one_rows = jnp.dot(hidden_one, pick, preferred_element_type=f32).astype(jnp.bfloat16)
    two_rows = jnp.dot(hidden_two, pick, preferred_element_type=f32).astype(jnp.bfloat16)
    small_scr[:, pl.ds(0, hidden)] = lax.dot_general(one_rows, grad_pre_hidden, TN, preferred_element_type=f32).astype(jnp.bfloat16)
    small_scr[:, pl.ds(hidden, outer.shape[1])] = lax.dot_general(two_rows, grad_outer, TN, preferred_element_type=f32).astype(jnp.bfloat16)
    middle = me_ref[2]
    part = small_scr.shape[0] // 2
    if images == 8:
        for j in range(images // 2):
            here = pl.ds(j * run, run)
            for bit, ref in ((middle, small_ref), (1 - middle, small_away_ref)):
                source = (j // 2) * 4 * run + bit * 2 * run + (j % 2) * run
                ref[0, here, :] = small_scr[pl.ds(pl.multiple_of(source, run), run), :]
    else:
        small_ref[0, pl.ds(0, part), :] = small_scr[pl.ds(0, part), :]
        small_away_ref[0, pl.ds(0, part), :] = small_scr[pl.ds(part, part), :]
    sums = [jnp.sum(v.astype(f32), axis=0, keepdims=True) for v in (grad_pre_feature, grad_pre_hidden, grad_outer)]
    sums = jnp.concatenate(sums, axis=1)
    note = write_sums(sums, small_scr.shape[1])
    for ref in (small_ref, small_away_ref):
        ref[0, pl.ds(ref.shape[1] - EXTRA, EXTRA), :] = note


def head(me, mine, theirs, section, stacked, images, before, micros):
    rows, hidden = mine.shape
    width = 512
    sections = stacked[0].shape[0]

    def whole(shape):
        return pl.BlockSpec(shape, lambda g, m: (0,) * len(shape))

    def of_section(array):
        return pl.BlockSpec((1,) + array.shape[1:], lambda g, m: (section, 0, 0))

    def kernel(*refs):
        head_kernel(*refs, images=images)

    shared = [
        jax.ShapeDtypeStruct((sections, rows // 4, CLASSES), jnp.float32),
        jax.ShapeDtypeStruct((sections, rows // 4, DELTAS), jnp.float32),
    ]
    single = [
        pltpu.HBM((1, hidden // 8 + EXTRA, hidden + width), jnp.bfloat16),
        pltpu.HBM((1, hidden // 8 + EXTRA, hidden + width), jnp.bfloat16),
        pltpu.HBM((rows, hidden), jnp.bfloat16),
        jax.ShapeDtypeStruct((hidden // 2, rows), jnp.bfloat16),
        jax.ShapeDtypeStruct((hidden // 2, rows), jnp.bfloat16),
    ]
    return pl.pallas_call(
        kernel,
        grid_spec=pltpu.PrefetchScalarGridSpec(
            num_scalar_prefetch=1,
            grid=(1,),
            in_specs=[whole(mine.shape), whole(theirs.shape)]
            + [of_section(a) for a in stacked]
            + [pl.BlockSpec(memory_space=pl.ANY)] * len(before),
            out_specs=[of_section(o) for o in shared] + [whole(o.shape) for o in single],
            scratch_shapes=[
                pltpu.VMEM((rows, width), jnp.float32),
                pltpu.VMEM((hidden, rows), jnp.bfloat16),
                pltpu.VMEM((width, hidden), jnp.bfloat16),
                pltpu.VMEM((1, width), jnp.float32),
                pltpu.VMEM((hidden // 4, hidden + width), jnp.bfloat16),
            ],
        ),
        out_shape=shared + single,
        input_output_aliases={3 + len(stacked) + j: j for j in range(len(before))},
        cost_estimate=cost(micros),
        compiler_params=params(13),
    )(me, mine, theirs, *stacked, *before)


def pass_sums(s, kept_ref, arrived_ref, refs):
    rows, width = kept_ref.shape[1:]
    notes = [ref[s, pl.ds(rows - EXTRA, EXTRA), :] for ref in (kept_ref, arrived_ref)]
    total = write_sums(read_sums(notes[0], 2 * width) + read_sums(notes[1], 2 * width), width)
    for ref in refs:
        ref[s, pl.ds(ref.shape[1] - EXTRA, EXTRA), :] = total


def small_step_kernel(bits_ref, kept_ref, arrived_ref, stay_ref, away_ref, at):
    sections, rows, width = kept_ref.shape
    run = 32
    for s in range(sections):
        for j in range((rows - EXTRA) // (2 * run)):
            for place, ref in ((bits_ref[at], stay_ref), (bits_ref[at + 1], away_ref)):
                here = pl.ds(pl.multiple_of(j * 2 * run + place * run, run), run)
                value = kept_ref[s, here, :].astype(jnp.float32) + arrived_ref[s, here, :].astype(jnp.float32)
                ref[s, pl.ds(j * run, run), :] = value.astype(jnp.bfloat16)
        pass_sums(s, kept_ref, arrived_ref, (stay_ref, away_ref))


def small_last_kernel(order_ref, kept_ref, arrived_ref, hidden_ref, class_ref, delta_ref, one_ref, two_ref, class_sum_ref, delta_sum_ref):
    del order_ref
    run, hidden = hidden_ref.shape[1:]
    width = kept_ref.shape[2]
    for s in range(kept_ref.shape[0]):
        value = kept_ref[s, pl.ds(0, run), :].astype(jnp.float32) + arrived_ref[s, pl.ds(0, run), :].astype(jnp.float32)
        hidden_ref[s] = value[:, :hidden]
        class_ref[s] = value[:, hidden : hidden + CLASSES]
        delta_ref[s] = value[:, hidden + OUTER : hidden + OUTER + DELTAS]
        sums = read_sums(kept_ref[s, pl.ds(run, EXTRA), :], 2 * width) + read_sums(arrived_ref[s, pl.ds(run, EXTRA), :], 2 * width)
        at = 0
        for ref, step in ((one_ref, hidden), (two_ref, hidden), (class_sum_ref, OUTER), (delta_sum_ref, DELTAS)):
            ref[s : s + 1, :] = sums[:, at : at + ref.shape[1]]
            at += step


def small_join_kernel(bits_ref, *refs):
    outs = refs[4:]
    rows = refs[0].shape[1]
    run = 32
    for s in range(2):
        kept_ref, arrived_ref = refs[s], refs[2 + s]
        count = (rows - EXTRA) // (2 * run)
        for j in range(count):
            for place, ref in ((bits_ref[4], outs[0]), (bits_ref[5], outs[1])):
                here = pl.ds(pl.multiple_of(place * count * run + j * run, run), run)
                value = kept_ref[0, here, :].astype(jnp.float32) + arrived_ref[0, here, :].astype(jnp.float32)
                ref[s, pl.ds(j * run, run), :] = value.astype(jnp.bfloat16)
        notes = [ref[0, pl.ds(rows - EXTRA, EXTRA), :] for ref in (kept_ref, arrived_ref)]
        width = kept_ref.shape[2]
        total = write_sums(read_sums(notes[0], 2 * width) + read_sums(notes[1], 2 * width), width)
        for ref in outs:
            ref[s, pl.ds(ref.shape[1] - EXTRA, EXTRA), :] = total


def small_join(bits, kept, arrived):
    vmem = pl.BlockSpec(memory_space=pltpu.VMEM)
    _, rows, width = kept[0].shape
    return pl.pallas_call(
        small_join_kernel,
        in_specs=[pl.BlockSpec(memory_space=pltpu.SMEM)] + [vmem] * 4,
        out_specs=[vmem] * 2,
        out_shape=[jax.ShapeDtypeStruct((2, (rows - EXTRA) // 2 + EXTRA, width), jnp.bfloat16)] * 2,
        cost_estimate=cost(1),
        compiler_params=params(8),
    )(bits, *kept, *arrived)


def small_step(bits, at, kept, arrived):
    vmem = pl.BlockSpec(memory_space=pltpu.VMEM)
    sections, rows, width = kept.shape
    return pl.pallas_call(
        lambda *refs: small_step_kernel(*refs, at),
        in_specs=[pl.BlockSpec(memory_space=pltpu.SMEM), vmem, vmem],
        out_specs=[vmem] * 2,
        out_shape=[jax.ShapeDtypeStruct((sections, (rows - EXTRA) // 2 + EXTRA, width), jnp.bfloat16)] * 2,
        cost_estimate=cost(1),
        compiler_params=params(8),
    )(bits, kept, arrived)


def small_last(order, kept, arrived, hidden):
    sections, rows, width = kept.shape
    shapes = [(sections, rows - EXTRA, n) for n in (hidden, CLASSES, DELTAS)]
    shapes += [(sections, n) for n in (hidden, hidden, CLASSES, DELTAS)]
    vmem = pl.BlockSpec(memory_space=pltpu.VMEM)
    return pl.pallas_call(
        small_last_kernel,
        in_specs=[pl.BlockSpec(memory_space=pltpu.SMEM), vmem, vmem],
        out_shape=[jax.ShapeDtypeStruct(shape, jnp.float32) for shape in shapes],
        cost_estimate=cost(1),
        compiler_params=params(8),
    )(order, kept, arrived)


def swap(value, axis, bit):
    size = lax.axis_size(axis)
    return lax.ppermute(value, axis, [(i, i ^ bit) for i in range(size)])


def after(value, *others):
    return lax.optimization_barrier((value,) + others)[0]


def choose(array, axis, bit):
    return lax.dynamic_index_in_dim(array, bit, axis, keepdims=False)


def split_bits(array, bits):
    return array.reshape((2,) * bits + (array.shape[0] >> bits,) + array.shape[1:])


def body(
    pyramid,
    image_size,
    region_boxes,
    routes,
    labels,
    targets,
    feature_weight,
    feature_bias,
    hidden_weight,
    hidden_bias,
    class_weight,
    class_bias,
    delta_weight,
    delta_bias,
):
    images = lax.axis_size("img")
    me = lax.axis_index("lvl").astype(jnp.int32)
    image = lax.axis_index("img").astype(jnp.int32)
    sections = routes.shape[0]
    features = feature_weight.shape[1]
    hidden = hidden_weight.shape[2]
    top = images // 2
    steps = images.bit_length() - 2
    half = jnp.minimum(image & top, 1)
    own_bits = [jnp.minimum(image & (1 << b), 1) for b in range(steps)]
    bits = jnp.stack([own_bits[0], 1 - own_bits[0], own_bits[1], 1 - own_bits[1], half, 1 - half, me])
    me_list = bits

    own, *packed = pack(me_list, image_size, pyramid, region_boxes, routes, labels, targets)
    quarters, small = packed[:3], packed[3:]
    arrived = [lax.ppermute(quarters[d], "lvl", [(0, d + 1)]) for d in (1, 2, 0)]
    coarse = [small[0]] + [swap(small[k], "lvl", k) for k in (1, 2, 3)]
    weight_a = to_bins(me_list, feature_weight, 0, 10)
    slot = me_list
    levels, info, table = arrange(after(slot, weight_a), 1, own, arrived, coarse)
    cross_levels = swap(levels, "img", top)

    stacked = (
        info, feature_bias[:, None], hidden_weight, hidden_bias[:, None], jnp.swapaxes(class_weight, 1, 2),
        class_bias[:, None], jnp.swapaxes(delta_weight, 1, 2), delta_bias[:, None],
    )

    def run_head(s, parts, before, ready, micros):
        results = head(after(me_list, *ready), *parts, s, stacked, images, before, micros)
        shared, small, (grads, stay, away) = results[:2], results[2:4], results[4:]
        return shared, small, grads, stay, swap(away, "img", top)

    def add(first, second):
        return (first.astype(jnp.float32) + second.astype(jnp.float32)).astype(jnp.bfloat16)

    pooled_a = crop(table, 0, levels, 12)
    part_a = first_product(pooled_a, weight_a, 1)
    weight_b = to_bins(after(me_list, part_a), feature_weight, 1, 8)
    chip_a = add(part_a, swap(part_a, "lvl", 1))
    pooled_b = crop(after(table, weight_b, chip_a), 1, levels, 8)
    part_b = first_product(pooled_b, weight_b, 0)
    shared, small_a, grads_a, stay_a, cross_a = run_head(0, (chip_a, swap(chip_a, "lvl", 2)), (), [part_b], 0)
    part_b = after(part_b, grads_a)
    theirs_b = swap(part_b, "lvl", 1)
    cross_table = prepare(after(slot, grads_a), cross_levels)
    chip_b = add(after(part_b, cross_table), theirs_b)
    far_a = crop(after(cross_table, chip_b), 0, cross_levels, 8)
    parts_b = (chip_b, swap(chip_b, "lvl", 2))
    if images == 8:
        def weight_sums(stay, cross, pooled, far, ready):
            pieces = [v.reshape(2, 2, hidden // images, -1) for v in (stay, cross)]
            sent_one, kept_one, sent_two, kept_two = outer_sums(after(bits, *ready), *pieces, pooled, far, 0)
            return (kept_one, kept_two), (swap(sent_one, "img", 1), swap(sent_two, "img", 2))

        def second_step(kept, arrived, ready):
            one, two = fold(after(bits, *ready), kept[0], arrived[0], kept[1], arrived[1])
            return one, (swap(one, "img", 2), swap(two, "img", 1))

        small_near_a = swap(small_a[1], "img", 2)
        kept_a, arrived_a = weight_sums(stay_a, cross_a, pooled_a, far_a, [])
        shared, small_b, grads_b, stay_b, cross_b = run_head(1, parts_b, shared, [kept_a[0]], 0)
        small_near_b = swap(small_b[1], "img", 2)
        far_b = crop(after(cross_table, grads_b, small_near_a), 1, cross_levels, 10)
        kept_b, arrived_b = weight_sums(stay_b, cross_b, pooled_b, far_b, [])
        folded, last_a = second_step(kept_a, arrived_a, [kept_b[0]])
        slots_a = back_product(after(me_list, folded), grads_a, weight_a, 10)
        small, away = small_join(after(bits, slots_a), (small_a[0], small_b[0]), (small_near_a, small_near_b))
        arrived_small = swap(away, "img", 4)
        slots_b = back_product(after(me_list, away), grads_b, weight_b, 0)
        spread_out = spread(table, slots_a, slots_b, 0)
        folded, last_b = second_step(kept_b, arrived_b, [spread_out, *last_a])
        small, away = small_step(after(bits, folded), 0, small, arrived_small)
        arrived_small = swap(away, "img", 1)
    else:
        shared, small_b, grads_b, stay_b, cross_b = run_head(1, parts_b, shared, [far_a], 0)
        slots_a = back_product(me_list, grads_a, weight_a, 8)
        slots_b = back_product(me_list, grads_b, weight_b, 5)
        spread_out = spread(table, slots_a, slots_b, 20)
        far_b = crop(cross_table, 1, cross_levels, 10)
        totals = []
        for stay, cross, pooled, far in ((stay_a, cross_a, pooled_a, far_a), (stay_b, cross_b, pooled_b, far_b)):
            total = jnp.dot(stay, pooled, preferred_element_type=jnp.float32)
            total = total + jnp.dot(cross, far, preferred_element_type=jnp.float32)
            for b in range(steps)[::-1]:
                halves = split_bits(total, 1)
                away = choose(halves, 0, 1 - own_bits[b]).astype(jnp.bfloat16)
                total = choose(halves, 0, own_bits[b]) + swap(away, "img", 1 << b).astype(jnp.float32)
            totals.append(total[:, :features])
        order = bin_order()
        back = jnp.array([order.index(j) for j in range(49)])
        total = jnp.stack(totals)
        total = total.reshape(sections, total.shape[1], 49, features // 49)[:, :, back]
        feature_weight_grad = total.transpose(0, 3, 2, 1).reshape(sections, features, -1)

    parts = lax.all_to_all(spread_out, "lvl", split_axis=0, concat_axis=0, tiled=True)
    logits, deltas = shared
    if images == 8:
        feature_weight_grad = from_bins(after(bits, folded), 0, kept_a, arrived_a, last_a, None, features, 8)
        small = small_last(after(me_list, feature_weight_grad), small, arrived_small, hidden)
        sums = small[3:]
        feature_weight_grad = from_bins(after(bits, small[0]), 1, kept_b, arrived_b, last_b, feature_weight_grad, features, 8)
        me_list = after(me_list, feature_weight_grad)
    pyramid_grad = unpack(me_list, image_size, parts, 0)
    pyramid_grad = pyramid_grad.reshape(1, 1, GRID, GRID, CHANNELS)

    if images != 8:
        small, small_away = [jnp.concatenate([a, b], axis=0) for a, b in zip(small_a, small_b)]
        notes = small[:, hidden // 8 :].astype(jnp.float32)
        sums = (notes[:, 0:2] + notes[:, 2:4]).reshape(sections, -1)
        sums = lax.psum(sums, "img")
        small = jnp.concatenate([small[:, : hidden // 8], small_away[:, : hidden // 8]], axis=1)
        small = lax.psum_scatter(small, "img", scatter_dimension=1, tiled=True).astype(jnp.float32)
        small = (small[:, :, :hidden], small[:, :, hidden : hidden + CLASSES], small[:, :, hidden + OUTER : hidden + OUTER + DELTAS])
        at = 2 * hidden
        sums = (sums[:, :hidden], sums[:, hidden:at], sums[:, at : at + CLASSES], sums[:, at + OUTER : at + OUTER + DELTAS])
    return (
        logits,
        deltas,
        pyramid_grad,
        feature_weight_grad,
        sums[0],
        small[0],
        sums[1],
        small[1],
        sums[2],
        small[2],
        sums[3],
    )


def solution(mesh):
    return jax.shard_map(
        body,
        mesh=mesh,
        in_specs=(
            P("img", "lvl", None, None, None),
            P("img", None),
            P(None, None, ("img", "lvl")),
            P(None, ("img", "lvl")),
            P(None, ("img", "lvl")),
            P(None, None, ("img", "lvl")),
            P(None, "lvl", None),
            P(),
            P(),
            P(),
            P(),
            P(),
            P(),
            P(),
        ),
        out_specs=(
            P(None, ("img", "lvl"), None),
            P(None, ("img", "lvl"), None),
            P("img", "lvl", None, None, None),
            P(None, "lvl", "img"),
            P(),
            P(None, ("img", "lvl"), None),
            P(),
            P(None, ("img", "lvl"), None),
            P(),
            P(None, ("img", "lvl"), None),
            P(),
        ),
        check_vma=False,
    )
```
